32 devices in a mesh: dp: 8 (over y, x, core), tensor: 4 (over z).
Axes of the slice: x: 2, y: 2, z: 4, core: 2. Of those that a mesh axis runs over, the one named last changes fastest.
Arguments:
- hidden_in: bfloat16 [5632, 1024], P('dp', 'tensor'), may hold values from -9 to 9
- lengths: int32 [8], P('dp'), may hold values from 176 to 704, as said below
- w_query: bfloat16 [1024, 2048], P(None, 'tensor'), may hold values from -0.1875 to 0.1875
- w_key: bfloat16 [1024, 1024], P(None, 'tensor'), may hold values from -0.1875 to 0.1875
- w_value: bfloat16 [1024, 1024], P(None, 'tensor'), may hold values from -0.1875 to 0.1875
- w_out: bfloat16 [2048, 1024], P('tensor'), may hold values from -1 to 1
- attn_gain: float32 [1024], P('tensor'), may hold values from 0.5 to 1.5
- ffn_gain: float32 [1024], P('tensor'), may hold values from 0.5 to 1.5
- query_gain: float32 [128], replicated, may hold values from 0.5 to 1.5
- key_gain: float32 [128], replicated, may hold values from 0.5 to 1.5
- w_gate: bfloat16 [1024, 3072], P(None, 'tensor'), may hold values from -0.1875 to 0.1875
- w_up: bfloat16 [1024, 3072], P(None, 'tensor'), may hold values from -0.1875 to 0.1875
- w_down: bfloat16 [3072, 1024], P('tensor'), may hold values from -0.109375 to 0.109375
- cotangent: bfloat16 [5632, 1024], P('dp', 'tensor'), may hold values from -6 to 6
Outputs:
- out_rows: bfloat16 [5632, 1024], P('dp', 'tensor')
- input_grad: bfloat16 [5632, 1024], P('dp', 'tensor')
- grad_query: float32 [1024, 2048], P(None, 'tensor')
- grad_key: float32 [1024, 1024], P(None, 'tensor')
- grad_value: float32 [1024, 1024], P(None, 'tensor')
- grad_out: float32 [2048, 1024], P('tensor')
- grad_attn_gain: float32 [1024], P('tensor')
- grad_ffn_gain: float32 [1024], P('tensor')
- grad_query_gain: float32 [128], replicated
- grad_key_gain: float32 [128], replicated
- grad_gate: float32 [1024, 3072], P(None, 'tensor')
- grad_up: float32 [1024, 3072], P(None, 'tensor')
- grad_down: float32 [3072, 1024], P('tensor')
- stat_rms: float32 [3], replicated
The draws below stay inside these ranges and needn't reach their ends.
Inputs may be any that keep to these rules, and one draw needn't show every extreme that they name: `lengths`: some sequence is full, with 704 valid tokens, and some has 176.
All inputs are finite; a program needn't handle non-finite values.
Results may differ from the reference program's by a relative error of at most 0.015.
Values may be sent and summed in bfloat16 or wider, within the bound.
No kernel may reach another device: no remote copies, remote signals or barrier semaphores. Data moves between devices by JAX's collectives and lax.ppermute only.
A program may use at most 128 MiB of HBM per device.

```python
import jax
import jax.numpy as jnp
from jax import lax

D = 1024
H = 16
KV = 8
HD = 128
FF = 3072
SEQ_LEN = 704
BLOCK = 256
SEQS = 8
TOKENS = 5632


def draw_hidden_in(key, part):
    key = jax.random.fold_in(key, 11)
    row_count = SEQ_LEN * SEQS
    seq_ids = (jnp.arange(row_count) // SEQ_LEN).astype(jnp.float32)
    rising = 0.6 + 1.2 * seq_ids / (SEQS - 1)
    base = jax.random.truncated_normal(key, -5.0, 5.0, (row_count, D), jnp.float32)
    return (base * rising[:, None]).astype(jnp.bfloat16)


def draw_lengths(key, part):
    key = jax.random.fold_in(key, 23)
    first_key, second_key = jax.random.split(key)
    shortest = SEQ_LEN // 4
    drawn = jax.random.randint(first_key, (SEQS,), shortest, SEQ_LEN + 1)
    order = jax.random.permutation(second_key, SEQS)
    drawn = jnp.where(order == 0, SEQ_LEN, drawn)
    drawn = jnp.where(order == 1, shortest, drawn)
    return drawn.astype(jnp.int32)


def steps_of(key, extent, cuts, low, high):
    loudness, own = 1.0, jax.random.fold_in(key, 6)
    for dim, shards_of in cuts:
        draws = jnp.exp(jax.random.uniform(jax.random.fold_in(own, dim), (shards_of,), jnp.float32, low / len(cuts), high / len(cuts)))
        loudness = loudness * jnp.repeat(draws, extent[dim] // shards_of).reshape([-1 if axis == dim else 1 for axis in range(len(extent))])
    return loudness


def bell_draw(stream_key, dims, scale, limit, cuts=(), kind=jnp.bfloat16):
    gain = steps_of(stream_key, dims, cuts, -0.22, 0.18) if cuts else 1.0
    result = jax.random.normal(stream_key, dims, jnp.float32) * scale * gain
    return jnp.minimum(jnp.maximum(result, -limit), limit).astype(kind)


def setup_inputs(seed: int = 0) -> dict:
    keys = jax.random.split(jax.random.key(seed), 15)
    return {
        "hidden_in": draw_hidden_in(jax.random.fold_in(keys[14], 71), 0),
        "lengths": draw_lengths(jax.random.fold_in(keys[14], 71), 0),
        "w_query": bell_draw(keys[2], (D, H * HD), D ** -0.5, 0.1875, ((1, 4),)),
        "w_key": bell_draw(keys[3], (D, KV * HD), D ** -0.5, 0.1875, ((1, 4),)),
        "w_value": bell_draw(keys[4], (D, KV * HD), D ** -0.5, 0.1875, ((1, 4),)),
        "w_out": bell_draw(keys[5], (H * HD, D), (H * HD // 64) ** -0.5, 1.0, ((0, 4),)),
        "attn_gain": jnp.clip(1.0 + 0.1 * jax.random.normal(keys[6], (D,), jnp.float32), 0.5, 1.5),
        "ffn_gain": jnp.clip(1.0 + 0.1 * jax.random.normal(keys[7], (D,), jnp.float32), 0.5, 1.5),
        "query_gain": jnp.clip(1.0 + 0.1 * jax.random.normal(keys[8], (HD,), jnp.float32), 0.5, 1.5),
        "key_gain": jnp.clip(1.0 + 0.1 * jax.random.normal(keys[9], (HD,), jnp.float32), 0.5, 1.5),
        "w_gate": bell_draw(keys[10], (D, FF), D ** -0.5, 0.1875, ((1, 4),)),
        "w_up": bell_draw(keys[11], (D, FF), D ** -0.5, 0.1875, ((1, 4),)),
        "w_down": bell_draw(keys[12], (FF, D), FF ** -0.5, 0.109375, ((0, 4),)),
        "cotangent": bell_draw(keys[13], (TOKENS, D), 1.0, 6.0, ((0, 8), (1, 4))),
    }


NORM_EPSILON = 1e-06
ROPE_THETA = 1000000.0
HIGHEST = lax.Precision.HIGHEST

@jax.custom_vjp
def low(v):
    return lax.optimization_barrier(v.astype(jnp.bfloat16)).astype(jnp.float32)

@jax.custom_vjp
def low_back(v):
    return v

def low_keep(v):
    return (low(v), None)

def low_pass(kept, grad):
    return (grad,)

def back_keep(v):
    return (v, None)

def back_low(kept, grad):
    return (low(grad),)
low.defvjp(low_keep, low_pass)
low_back.defvjp(back_keep, back_low)

def rope_tables(length, width):
    half_width = width // 2
    frequency = ROPE_THETA ** (-(jnp.arange(half_width, dtype=jnp.float32) * (2.0 / width)))
    angles = jnp.arange(length, dtype=jnp.float32)[:, None] * frequency[None, :]
    angles = jnp.concatenate([angles, angles], axis=1)
    return (jnp.cos(angles), jnp.sin(angles))

def rotate(values, cos_table, sin_table):
    half_width = values.shape[-1] // 2
    turned = jnp.concatenate([-values[..., half_width:], values[..., :half_width]], axis=-1)
    return values * cos_table[:, None, :] + turned * sin_table[:, None, :]

def rms_scale(values):
    return lax.rsqrt(lax.optimization_barrier(jnp.mean(values * values, axis=-1, keepdims=True)) + NORM_EPSILON)

def layer_forward(params, rows_in, length):
    w_query, w_key, w_value, w_out, attn_gain, ffn_gain, query_gain, key_gain, w_gate, w_up, w_down = params
    seq_len = rows_in.shape[0]
    positions = jnp.arange(seq_len)
    block_ids = positions // BLOCK
    visible = (block_ids[None, :] <= block_ids[:, None]) & (positions[None, :] < length)
    normed_one = low(rows_in * rms_scale(rows_in) * attn_gain)
    query_pre = low_back(jnp.dot(normed_one, w_query, precision=HIGHEST)).reshape(seq_len, H, HD)
    key_pre = low_back(jnp.dot(normed_one, w_key, precision=HIGHEST)).reshape(seq_len, KV, HD)
    values = low(low_back(jnp.dot(normed_one, w_value, precision=HIGHEST))).reshape(seq_len, KV, HD)
    cos_table, sin_table = rope_tables(seq_len, HD)
    query_rows = low(rotate(query_pre * rms_scale(query_pre) * query_gain, cos_table, sin_table))
    query_rows = query_rows.reshape(seq_len, KV, H // KV, HD)
    key_rows = low(rotate(key_pre * rms_scale(key_pre) * key_gain, cos_table, sin_table))
    scores = jnp.einsum('sgrd,tgd->grst', query_rows, key_rows, precision=HIGHEST) * HD ** (-0.5)
    scores = jnp.where(visible, low_back(scores), -1e+30)
    row_top = lax.optimization_barrier(jnp.max(scores, axis=-1, keepdims=True))
    log_total = row_top + jnp.log(lax.optimization_barrier(jnp.sum(jnp.exp(scores - row_top), axis=-1, keepdims=True)))
    attn_probs = jnp.exp(scores - log_total)
    mixed_rows = jnp.einsum('grst,tgd->sgrd', low(attn_probs), values, precision=HIGHEST).reshape(seq_len, H * HD)
    mixed_rows = low(low_back(mixed_rows))
    attn_rows = low_back(jnp.dot(mixed_rows, w_out, precision=HIGHEST))
    middle = rows_in + attn_rows
    normed_two = low(middle * rms_scale(middle) * ffn_gain)
    gate_rows = low_back(jnp.dot(normed_two, w_gate, precision=HIGHEST))
    up_rows = low_back(jnp.dot(normed_two, w_up, precision=HIGHEST))
    hidden = low(gate_rows * jax.nn.sigmoid(gate_rows) * up_rows)
    ffn_rows = low_back(jnp.dot(hidden, w_down, precision=HIGHEST))
    return (middle + ffn_rows, (attn_rows, ffn_rows))

def reference(hidden_in, lengths, w_query, w_key, w_value, w_out, attn_gain, ffn_gain, query_gain, key_gain, w_gate, w_up, w_down, cotangent):
    params = tuple((weight_arr.astype(jnp.float32) for weight_arr in (w_query, w_key, w_value, w_out, attn_gain, ffn_gain, query_gain, key_gain, w_gate, w_up, w_down)))
    seq_count = lengths.shape[0]
    per_step = 4 if seq_count % 4 == 0 else 1
    seq_len = hidden_in.shape[0] // seq_count
    step_count = seq_count // per_step
    rows_all = hidden_in.astype(jnp.float32).reshape(step_count, per_step, seq_len, D)
    cot_all = cotangent.astype(jnp.float32).reshape(step_count, per_step, seq_len, D)
    len_all = lengths.reshape(step_count, per_step)
    positions = jnp.arange(seq_len)

    def step_fn(carry, item):
        grad_sum, stat_sum = carry
        rows_in, cot_rows, len_rows = item
        valid_rows = (positions[None, :] < len_rows[:, None]).astype(jnp.float32)[..., None]

        def run(pars, inputs):
            return jax.vmap(lambda one_rows, one_len: layer_forward(pars, one_rows, one_len))(inputs, len_rows)
        out_rows, pull, (attn_rows, ffn_rows) = jax.vjp(run, params, rows_in, has_aux=True)
        grad_pars, grad_rows = pull(cot_rows * valid_rows)
        stat_new = jnp.stack([jnp.sum(valid_rows * out_rows * out_rows), jnp.sum(valid_rows * attn_rows * attn_rows), jnp.sum(valid_rows * ffn_rows * ffn_rows), jnp.sum(valid_rows) * D])
        grad_sum = jax.tree.map(jnp.add, grad_sum, grad_pars)
        return ((grad_sum, stat_sum + stat_new), (out_rows, grad_rows))
    start = (jax.tree.map(jnp.zeros_like, params), jnp.zeros((4,), jnp.float32))
    (grads, stats), (out_all, grad_all) = lax.scan(step_fn, start, (rows_all, cot_all, len_all))
    out_rows = out_all.reshape(seq_count * seq_len, D).astype(jnp.bfloat16)
    input_grad = grad_all.reshape(seq_count * seq_len, D).astype(jnp.bfloat16)
    stat_rms = jnp.sqrt(stats[:3] / stats[3])
    return (out_rows, input_grad, grads[0], grads[1], grads[2], grads[3], grads[4], grads[5], grads[6], grads[7], grads[8], grads[9], grads[10], stat_rms)
```

```python
import functools

import jax
import jax.numpy as jnp
from jax import lax
from jax.experimental import pallas as pl
from jax.experimental.pallas import tpu as pltpu
from jax.sharding import PartitionSpec as P

BLOCK = 256
NORM_EPSILON = 1e-06
ROPE_THETA = 1000000.0
LOG2E = 1.4426950408889634
NEG = -1e30
ROWS = 64
VMEM_BYTES = 48 * 1024 * 1024

bf16 = jnp.bfloat16
f32 = jnp.float32


def dot(a, b):
    return jnp.dot(a, b, preferred_element_type=f32)


def dot_t(a, b):
    return lax.dot_general(a, b, (((1,), (1,)), ((), ())), preferred_element_type=f32)


def t_dot(a, b):
    return lax.dot_general(a, b, (((0,), (0,)), ((), ())), preferred_element_type=f32)


def row_loop(count, step, body):
    def run(i, carry):
        body(pl.ds(pl.multiple_of(i * step, step), step))
        return carry

    lax.fori_loop(0, count // step, run, 0)


def rope_tables(length, width):
    half_width = width // 2
    frequency = ROPE_THETA ** (-(jnp.arange(half_width, dtype=f32) * (2.0 / width)))
    angles = jnp.arange(length, dtype=f32)[:, None] * frequency[None, :]
    cos, sin = jnp.cos(angles), jnp.sin(angles)
    return jnp.concatenate([cos, cos], axis=1), jnp.concatenate([-sin, sin], axis=1)


def query_units(seq_len):
    units = []
    start = 0
    while start < seq_len:
        rows = min(128, seq_len - start)
        keys = (start // BLOCK + 1) * BLOCK
        units.append((start, rows, keys))
        start += rows
    return units


def roles(z):
    low = z < 2
    return jnp.where(low, 2, 1), jnp.where(low, 3, 0), z + 1 - 2 * lax.rem(z, 2), z


def shard_slices(z, width):
    return [pl.ds(pl.multiple_of(shard * width, width), width) for shard in roles(z)]


def assemble(z, pieces, body):
    own, pair, across_mid, across_end, far_mid, far_end = pieces
    end = (z == 0) | (z == 3)

    @pl.when(end)
    def _():
        body((across_end, far_end, pair, own))

    @pl.when(jnp.logical_not(end))
    def _():
        body((across_mid, far_mid, pair, own))


def key_bias(length, keys):
    slot = lax.broadcasted_iota(jnp.int32, (1, keys), 1)
    return jnp.where(slot < length, 0.0, NEG).astype(f32)


def attn_forward_kernel(
    info_ref, x0, x1, x2, x3, x4, x5, gain_ref, wq_ref, wk_ref, wv_ref, wo_ref, qg_ref, kg_ref, cos_ref, sin_ref,
    n1_ref, qpre_ref, kpre_ref, qrot_ref, krot_ref, val_ref, mixed_ref, stat_ref, p_across, p_far, p_pair, p_own,
):
    seq_len, width = n1_ref.shape
    hd = qg_ref.shape[1]
    heads = wq_ref.shape[1] // hd
    kvs = wk_ref.shape[1] // hd
    group = heads // kvs
    padded = krot_ref.shape[0]
    length, z = info_ref[0], info_ref[1]
    scale = hd ** (-0.5) * LOG2E
    slices = shard_slices(z, width // 4)

    def normalise(refs):
        def norm(rows):
            xs = [ref[rows, :].astype(f32) for ref in refs]
            r1 = lax.rsqrt(sum(jnp.sum(x * x, axis=1, keepdims=True) for x in xs) / width + NORM_EPSILON)
            stat_ref[rows, heads : heads + 1] = r1
            for x, cols in zip(xs, slices):
                n1_ref[rows, cols] = (x * r1 * gain_ref[:, cols]).astype(bf16)

        row_loop(seq_len, ROWS, norm)

    assemble(z, (x0, x1, x2, x3, x4, x5), normalise)

    def project(w_ref, pre_ref, rot_ref, g_ref):
        count = w_ref.shape[1]
        for c in range(0, count, 2 * hd):
            pre_ref[:, c : c + 2 * hd] = dot(n1_ref[...], w_ref[:, c : c + 2 * hd])

        def rotate(rows):
            cos, sin = cos_ref[rows, :], sin_ref[rows, :]
            for c in range(0, count, hd):
                v = pre_ref[rows, c : c + hd]
                r = lax.rsqrt(jnp.mean(v * v, axis=1, keepdims=True) + NORM_EPSILON)
                v = v * r * g_ref[...]
                rot_ref[rows, c : c + hd] = (v * cos + pltpu.roll(v, hd // 2, 1) * sin).astype(bf16)

        row_loop(seq_len, ROWS, rotate)

    project(wk_ref, kpre_ref, krot_ref, kg_ref)
    val_ref[0:seq_len, :] = dot(n1_ref[...], wv_ref[...]).astype(bf16)
    if padded > seq_len:
        krot_ref[seq_len:padded, :] = jnp.zeros((padded - seq_len, kvs * hd), bf16)
        val_ref[seq_len:padded, :] = jnp.zeros((padded - seq_len, kvs * hd), bf16)
    project(wq_ref, qpre_ref, qrot_ref, qg_ref)

    for start, rows, keys in query_units(seq_len):
        bias = key_bias(length, keys)
        for g in range(kvs):
            key = krot_ref[0:keys, g * hd : (g + 1) * hd]
            val = val_ref[0:keys, g * hd : (g + 1) * hd]
            first = g * group
            q = jnp.concatenate(
                [qrot_ref[start : start + rows, h * hd : (h + 1) * hd] for h in range(first, first + group)], axis=0
            )
            e = jnp.exp2(dot_t(q, key) * scale + bias)
            total = jnp.sum(e, axis=1, keepdims=True)
            mixed = dot(e.astype(bf16), val) * (1.0 / total)
            lse = jnp.log2(total)
            for r in range(group):
                h = first + r
                mixed_ref[start : start + rows, h * hd : (h + 1) * hd] = mixed[r * rows : (r + 1) * rows].astype(bf16)
                stat_ref[start : start + rows, h : h + 1] = lse[r * rows : (r + 1) * rows]

    for part_ref, cols in zip((p_across, p_far, p_pair, p_own), slices):
        part_ref[...] = dot(mixed_ref[...], wo_ref[:, cols]).astype(part_ref.dtype)


def norm_back(grad_s, normed_ref, row_scale, inner_s, gain_ref, part_ref, gain_grad_ref, cols, width):
    seq_len, step = grad_s.shape
    gain = gain_ref[:, cols]
    inverse = 1.0 / gain

    def finish(i, acc):
        rows = pl.ds(pl.multiple_of(i * ROWS, ROWS), ROWS)
        grad = grad_s[rows, :]
        unit = normed_ref[rows, cols].astype(f32) * inverse
        coef = inner_s[rows, 0:1] * (1.0 / width)
        part_ref[rows, :] = (row_scale(rows) * (grad * gain - unit * coef)).astype(part_ref.dtype)
        return acc + jnp.sum((grad * unit).reshape(ROWS // 8, 8, step), axis=0)

    gain_grad_ref[:, cols] = lax.fori_loop(0, seq_len // ROWS, finish, jnp.zeros((8, step), f32))


def ffn_kernel(
    info_ref, m0, m1, m2, m3, m4, m5, gain_ref, wg_ref, wu_ref, wd_ref, c0, c1, c2, c3, c4, c5,
    n2_ref, cotm_ref, hid_ref, dgu_ref, p_across, p_far, p_pair, p_own, gfg_ref,
    gate_s, up_s, gh_s, inner_s, r2_s,
):
    seq_len, width = n2_ref.shape
    hidden = wg_ref.shape[1]
    length, z = info_ref[0], info_ref[1]
    step = gate_s.shape[1]
    slices = shard_slices(z, width // 4)

    def normalise(refs):
        def norm(rows):
            ms = [ref[rows, :].astype(f32) for ref in refs]
            r2 = lax.rsqrt(sum(jnp.sum(m * m, axis=1, keepdims=True) for m in ms) / width + NORM_EPSILON)
            r2_s[rows, :] = jnp.broadcast_to(r2, (ROWS, 128))
            inner_s[rows, :] = jnp.zeros((ROWS, 128), f32)
            for m, cols in zip(ms, slices):
                n2_ref[rows, cols] = (m * r2 * gain_ref[:, cols]).astype(bf16)

        row_loop(seq_len, ROWS, norm)

    def mask(refs):
        def one(rows):
            slot = rows.start + lax.broadcasted_iota(jnp.int32, (ROWS, 1), 0)
            for ref, cols in zip(refs, slices):
                cotm_ref[rows, cols] = jnp.where(slot < length, ref[rows, :].astype(f32), 0.0).astype(bf16)

        row_loop(seq_len, ROWS, one)

    assemble(z, (m0, m1, m2, m3, m4, m5), normalise)
    assemble(z, (c0, c1, c2, c3, c4, c5), mask)

    for j in range(0, hidden, step):
        gate_s[...] = dot(n2_ref[...], wg_ref[:, j : j + step])
        up_s[...] = dot(n2_ref[...], wu_ref[:, j : j + step])
        gh_s[...] = dot_t(cotm_ref[...], wd_ref[j : j + step, :])

        def elementwise(rows):
            gate, up, gh = gate_s[rows, :], up_s[rows, :], gh_s[rows, :]
            sig = jax.nn.sigmoid(gate)
            silu = gate * sig
            hid_ref[rows, j : j + step] = (silu * up).astype(bf16)
            dg = (gh * up * (sig * (1.0 + gate * (1.0 - sig)))).astype(bf16)
            du = (gh * silu).astype(bf16)
            dgu_ref[rows, j : j + step] = dg
            dgu_ref[rows, hidden + j : hidden + j + step] = du
            inner = jnp.sum(dg.astype(f32) * gate + du.astype(f32) * up, axis=1, keepdims=True)
            inner_s[rows, :] += jnp.broadcast_to(inner, (ROWS, 128))

        row_loop(seq_len, ROWS, elementwise)

    for part_ref, cols in zip((p_across, p_far, p_pair, p_own), slices):
        gate_s[...] = dot_t(dgu_ref[:, 0:hidden], wg_ref[cols, :]) + dot_t(
            dgu_ref[:, hidden : 2 * hidden], wu_ref[cols, :]
        )
        norm_back(
            gate_s, n2_ref, lambda rows: r2_s[rows, 0:1], inner_s, gain_ref, part_ref, gfg_ref, cols, width
        )


def attn_backward_kernel(
    info_ref, g0, g1, g2, g3, g4, g5, n1_ref, gain_ref, wq_ref, wk_ref, wv_ref, wo_ref, qg_ref, kg_ref, cos_ref,
    sin_ref, qpre_ref, kpre_ref, qrot_ref, krot_ref, val_ref, mixed_ref, stat_ref,
    ga_ref, dqkv_ref, p_across, p_far, p_pair, p_own, gag_ref, qgg_ref, kgg_ref,
    gm_s, dq_s, dk_s, dv_s, acc_s, inner_s,
):
    seq_len, width = n1_ref.shape
    hd = qg_ref.shape[1]
    heads = wq_ref.shape[1] // hd
    kvs = wk_ref.shape[1] // hd
    group = heads // kvs
    length, z = info_ref[0], info_ref[1]
    scale = hd ** (-0.5)
    qw, kw = heads * hd, kvs * hd
    slices = shard_slices(z, width // 4)

    def collect(refs):
        for ref, cols in zip(refs, slices):
            ga_ref[:, cols] = ref[...]

    assemble(z, (g0, g1, g2, g3, g4, g5), collect)

    for c in range(0, qw, 256):
        gm_s[:, c : c + 256] = dot_t(ga_ref[...], wo_ref[c : c + 256, :]).astype(bf16)
    dk_s[...] = jnp.zeros_like(dk_s)
    dv_s[...] = jnp.zeros_like(dv_s)

    for start, rows, keys in query_units(seq_len):
        bias = key_bias(length, keys)
        for g in range(kvs):
            first = g * group
            cols = slice(g * hd, (g + 1) * hd)
            key, val = krot_ref[0:keys, cols], val_ref[0:keys, cols]

            def stacked(ref):
                return jnp.concatenate(
                    [ref[start : start + rows, h * hd : (h + 1) * hd] for h in range(first, first + group)], axis=0
                )

            q, gm, mixed = stacked(qrot_ref), stacked(gm_s), stacked(mixed_ref)
            lse = jnp.concatenate(
                [stat_ref[start : start + rows, h : h + 1] for h in range(first, first + group)], axis=0
            )
            p = jnp.exp2(dot_t(q, key) * (scale * LOG2E) + bias - lse)
            delta = jnp.sum(gm.astype(f32) * mixed.astype(f32), axis=1, keepdims=True)
            ds = (p * (dot_t(gm, val) - delta)).astype(bf16)
            dv_s[0:keys, cols] += t_dot(p.astype(bf16), gm)
            dk_s[0:keys, cols] += t_dot(ds, q)
            dq = dot(ds, key)
            for r in range(group):
                h = first + r
                dq_s[start : start + rows, h * hd : (h + 1) * hd] = dq[r * rows : (r + 1) * rows]

    def unrotate(rows, rot_s, pre_ref, g_ref, count, base):
        cos, sin = cos_ref[rows, :], sin_ref[rows, :]
        inner = jnp.zeros((ROWS, 1), f32)
        gain_sum = jnp.zeros((8, hd), f32)
        for c in range(0, count, hd):
            g = rot_s[rows, c : c + hd] * scale
            u = g * cos + pltpu.roll(g * sin, hd // 2, 1)
            v = pre_ref[rows, c : c + hd]
            r = lax.rsqrt(jnp.mean(v * v, axis=1, keepdims=True) + NORM_EPSILON)
            gain_sum = gain_sum + jnp.sum((u * v * r).reshape(ROWS // 8, 8, hd), axis=0)
            w = u * g_ref[...]
            mean = jnp.mean(w * v, axis=1, keepdims=True)
            d = (r * w - v * (r * r * r * mean)).astype(bf16)
            dqkv_ref[rows, base + c : base + c + hd] = d
            inner = inner + jnp.sum(d.astype(f32) * v, axis=1, keepdims=True)
        return inner, gain_sum

    def heads_back(i, carry):
        rows = pl.ds(pl.multiple_of(i * ROWS, ROWS), ROWS)
        qi, qgs = unrotate(rows, dq_s, qpre_ref, qg_ref, qw, 0)
        ki, kgs = unrotate(rows, dk_s, kpre_ref, kg_ref, kw, qw)
        dv = dv_s[rows, :].astype(bf16)
        dqkv_ref[rows, qw + kw : qw + 2 * kw] = dv
        vi = jnp.sum(dv.astype(f32) * val_ref[rows, :].astype(f32), axis=1, keepdims=True)
        inner_s[rows, :] = jnp.broadcast_to(qi + ki + vi, (ROWS, 128))
        return carry[0] + qgs, carry[1] + kgs

    zero = jnp.zeros((8, hd), f32)
    qgs, kgs = lax.fori_loop(0, seq_len // ROWS, heads_back, (zero, zero))
    qgg_ref[...] = qgs
    kgg_ref[...] = kgs

    for part_ref, cols in zip((p_across, p_far, p_pair, p_own), slices):
        acc_s[...] = (
            dot_t(dqkv_ref[:, 0:qw], wq_ref[cols, :])
            + dot_t(dqkv_ref[:, qw : qw + kw], wk_ref[cols, :])
            + dot_t(dqkv_ref[:, qw + kw : qw + 2 * kw], wv_ref[cols, :])
        )
        norm_back(
            acc_s, n1_ref, lambda rows: stat_ref[rows, heads : heads + 1], inner_s, gain_ref, part_ref, gag_ref,
            cols, width,
        )


def call(body, outs, args, scratch=(), flops=0, bytes_accessed=0):
    spec = pl.BlockSpec(memory_space=pltpu.VMEM)
    return pl.pallas_call(
        body,
        out_shape=[jax.ShapeDtypeStruct(s, d) for s, d in outs],
        in_specs=[pl.BlockSpec(memory_space=pltpu.SMEM)] + [spec] * (len(args) - 1),
        out_specs=[spec] * len(outs),
        scratch_shapes=[pltpu.VMEM(s, d) for s, d in scratch],
        compiler_params=pltpu.CompilerParams(vmem_limit_bytes=VMEM_BYTES),
        cost_estimate=pl.CostEstimate(flops=flops, bytes_accessed=bytes_accessed, transcendentals=0),
    )(*args)


PAIRS = ((0, 1), (1, 0), (2, 3), (3, 2))
MIDDLE = ((1, 2), (2, 1))
OUTWARD = ((1, 0), (2, 3))
INWARD = ((0, 1), (3, 2))
OUTWARD_TWO = ((2, 0), (1, 3))
INWARD_TWO = ((0, 2), (3, 1))


def send(rows, pairs):
    return lax.ppermute(rows, "tensor", pairs)


def gather_line(own):
    pair = send(own, PAIRS)
    across_mid = send(own, MIDDLE)
    across_end = send(across_mid, OUTWARD)
    far_end = send(pair, OUTWARD_TWO)
    far_mid = send(pair, MIDDLE)
    return own, pair, across_mid, across_end, far_mid, far_end


def scatter_line(across, far, pair, own):
    one = send(across, INWARD)
    two = send(far, INWARD_TWO)
    three = send(far, MIDDLE)
    to_pair = (pair.astype(f32) + (two.astype(f32) + three.astype(f32))).astype(bf16)
    to_across = (across.astype(f32) + one.astype(f32)).astype(bf16)
    from_pair = send(to_pair, PAIRS)
    from_across = send(to_across, MIDDLE)
    return own.astype(f32) + (from_pair.astype(f32) + from_across.astype(f32))


def per_device(
    hidden_in, lengths, w_query, w_key, w_value, w_out, attn_gain, ffn_gain,
    query_gain, key_gain, w_gate, w_up, w_down, cotangent,
):
    seq_len, shard = hidden_in.shape
    width = w_query.shape[0]
    hd = query_gain.shape[0]
    qw, kw = w_query.shape[1], w_key.shape[1]
    hidden = w_gate.shape[1]
    padded = -(-seq_len // BLOCK) * BLOCK
    z = lax.axis_index("tensor").astype(jnp.int32)
    info = jnp.stack([lengths[0], z])
    parts = [((seq_len, shard), bf16)] * 4

    x_parts = gather_line(hidden_in)
    gains = lax.all_gather(jnp.stack([attn_gain, ffn_gain]), "tensor", axis=1, tiled=True)
    gain_one, gain_two = gains[0:1], gains[1:2]
    cot_parts = gather_line(cotangent)
    cos, sin = rope_tables(seq_len, hd)
    qg, kg = query_gain[None], key_gain[None]
    resid = hidden_in.astype(f32)
    valid = (jnp.arange(seq_len, dtype=jnp.int32) < lengths[0]).astype(f32)[:, None]

    n1, qpre, kpre, qrot, krot, val, mixed, stat, *attn_parts = call(
        attn_forward_kernel,
        [
            ((seq_len, width), bf16), ((seq_len, qw), f32), ((seq_len, kw), f32), ((seq_len, qw), bf16),
            ((padded, kw), bf16), ((padded, kw), bf16), ((seq_len, qw), bf16), ((seq_len, 128), f32),
        ] + parts,
        (info, *x_parts, gain_one, w_query, w_key, w_value, w_out, qg, kg, cos, sin),
        flops=2 * seq_len * width * (2 * qw + 2 * kw) + 4 * seq_len * seq_len * qw,
        bytes_accessed=14_000_000,
    )
    attn_local = scatter_line(*attn_parts)
    middle = resid + attn_local
    m_parts = gather_line(middle.astype(bf16))

    n2, cotm, hid, dgu, *ffn_parts, gfg = call(
        ffn_kernel,
        [
            ((seq_len, width), bf16), ((seq_len, width), bf16), ((seq_len, hidden), bf16),
            ((seq_len, 2 * hidden), bf16),
        ] + parts + [((8, width), f32)],
        (info, *m_parts, gain_two, w_gate, w_up, w_down, *cot_parts),
        scratch=[((seq_len, 256), f32)] * 3 + [((seq_len, 128), f32)] * 2,
        flops=2 * seq_len * width * hidden * 5,
        bytes_accessed=16_000_000,
    )
    grad_top = cotangent.astype(f32) * valid
    grad_middle = grad_top + scatter_line(*ffn_parts)
    ga_parts = gather_line(grad_middle.astype(bf16))

    down = [
        dot(hid, lax.dynamic_slice(w_down, (0, s * shard), (hidden, shard))).astype(bf16) for s in roles(z)
    ]
    ffn_local = scatter_line(*down)
    out_full = middle + ffn_local
    g_down = t_dot(hid, cotm).astype(bf16)
    g_gu = t_dot(n2, dgu).astype(bf16)
    g_down, g_gu = lax.psum((g_down, g_gu), "dp")

    ga, dqkv, *back_parts, gag, qgg, kgg = call(
        attn_backward_kernel,
        [((seq_len, width), bf16), ((seq_len, qw + 2 * kw), bf16)] + parts
        + [((8, width), f32), ((8, hd), f32), ((8, hd), f32)],
        (
            info, *ga_parts, n1, gain_one, w_query, w_key, w_value, w_out, qg, kg, cos, sin,
            qpre, kpre, qrot, krot, val, mixed, stat,
        ),
        scratch=[
            ((seq_len, qw), bf16), ((seq_len, qw), f32), ((padded, kw), f32), ((padded, kw), f32),
            ((seq_len, shard), f32), ((seq_len, 128), f32),
        ],
        flops=2 * seq_len * width * (2 * qw + 2 * kw) + 10 * seq_len * seq_len * qw,
        bytes_accessed=16_000_000,
    )
    input_grad = (grad_middle + scatter_line(*back_parts)).astype(bf16)
    g_out = t_dot(mixed, ga).astype(bf16)
    g_qkv = t_dot(n1, dqkv).astype(bf16)
    (g_down, g_gu, g_out, g_qkv) = lax.optimization_barrier((g_down, g_gu, g_out, g_qkv))
    g_out, g_qkv = lax.psum((g_out, g_qkv), "dp")

    first_rank = (z == 0).astype(f32)
    totals = jnp.stack(
        [
            jnp.sum(valid * out_full * out_full),
            jnp.sum(valid * attn_local * attn_local),
            jnp.sum(valid * ffn_local * ffn_local),
            first_rank * jnp.sum(valid) * width,
        ]
    )
    small = jnp.concatenate(
        [jnp.sum(gag, axis=0), jnp.sum(gfg, axis=0), jnp.sum(qgg, axis=0), jnp.sum(kgg, axis=0), totals]
    )
    small = lax.psum(small, ("dp", "tensor"))
    mine = z * shard
    grad_attn_gain = lax.dynamic_slice(small, (mine,), (shard,))
    grad_ffn_gain = lax.dynamic_slice(small, (width + mine,), (shard,))
    rest = small[2 * width :]
    totals = rest[2 * hd :]
    stat_rms = jnp.sqrt(totals[:3] / totals[3])
    return (
        out_full.astype(bf16),
        input_grad,
        g_qkv[:, :qw].astype(f32),
        g_qkv[:, qw : qw + kw].astype(f32),
        g_qkv[:, qw + kw :].astype(f32),
        g_out.astype(f32),
        grad_attn_gain,
        grad_ffn_gain,
        rest[:hd],
        rest[hd : 2 * hd],
        g_gu[:, :hidden].astype(f32),
        g_gu[:, hidden:].astype(f32),
        g_down.astype(f32),
        stat_rms,
    )


def solution(mesh):
    rows, cols, first = P("dp", "tensor"), P(None, "tensor"), P("tensor", None)
    gain = P("tensor")
    return jax.shard_map(
        per_device,
        mesh=mesh,
        in_specs=(rows, P("dp"), cols, cols, cols, first, gain, gain, P(), P(), cols, cols, first, rows),
        out_specs=(rows, rows, cols, cols, cols, first, gain, gain, P(), P(), cols, cols, first, P()),
        check_vma=False,
    )
```

```python
import functools

import jax
import jax.numpy as jnp
from jax import lax
from jax.experimental import pallas as pl
from jax.experimental.pallas import tpu as pltpu
from jax.sharding import PartitionSpec as P

BLOCK = 256
NORM_EPSILON = 1e-06
ROPE_THETA = 1000000.0
LOG2E = 1.4426950408889634
NEG = -1e30
ROWS = 64
TAIL = 16
VMEM_BYTES = 60 * 1024 * 1024
SMALL_BYTES = 24 * 1024 * 1024

bf16 = jnp.bfloat16
f32 = jnp.float32


def dot(a, b):
    return jnp.dot(a, b, preferred_element_type=f32)


def dot_t(a, b):
    return lax.dot_general(a, b, (((1,), (1,)), ((), ())), preferred_element_type=f32)


def t_dot(a, b):
    return lax.dot_general(a, b, (((0,), (0,)), ((), ())), preferred_element_type=f32)


def row_loop(count, step, body):
    for start in range(0, count, step):
        body(pl.ds(start, step))


def rope_tables(length, width):
    half_width = width // 2
    frequency = ROPE_THETA ** (-(jnp.arange(half_width, dtype=f32) * (2.0 / width)))
    angles = jnp.arange(length, dtype=f32)[:, None] * frequency[None, :]
    cos, sin = jnp.cos(angles), jnp.sin(angles)
    return jnp.concatenate([cos, cos], axis=1), jnp.concatenate([-sin, sin], axis=1)


def query_units(seq_len):
    units = []
    start = 0
    while start < seq_len:
        rows = min(128, seq_len - start)
        keys = (start // BLOCK + 1) * BLOCK
        units.append((start, rows, keys))
        start += rows
    return units


def roles(z):
    low = z < 2
    return jnp.where(low, 2, 1), jnp.where(low, 3, 0), z + 1 - 2 * lax.rem(z, 2), z


def shard_slices(z, width):
    return [pl.ds(pl.multiple_of(shard * width, width), width) for shard in roles(z)]


def assemble(z, pieces, body):
    own, pair_mid, pair_end, across_mid, across_end, far_mid, far_end = pieces
    end = (z == 0) | (z == 3)

    @pl.when(end)
    def _():
        body((across_end, far_end, pair_end, own))

    @pl.when(jnp.logical_not(end))
    def _():
        body((across_mid, far_mid, pair_mid, own))


def key_bias(length, keys):
    slot = lax.broadcasted_iota(jnp.int32, (1, keys), 1)
    return jnp.where(slot < length, 0.0, NEG).astype(f32)


def row_scale(squares, width):
    return lax.rsqrt(jnp.sum(squares, axis=1, keepdims=True) * (1.0 / width) + NORM_EPSILON)


def copies(sources, targets, sems):
    pending = [pltpu.make_async_copy(a, b, sems.at[i]) for i, (a, b) in enumerate(zip(sources, targets))]
    for copy in pending:
        copy.start()
    return pending


def attn_forward_kernel(
    info_ref, x0, x1, x2, x3, x4, x5, qg_ref, kg_ref, wk_hbm, cos_hbm, sin_hbm, wv_hbm, wq_hbm, wo_hbm,
    p_across, p_far, p_pair, p_own, n1_hbm, qpre_hbm, kpre_hbm, qrot_hbm, krot_hbm, val_hbm, mixed_hbm, lse_hbm,
    r1_hbm, gain_hbm,
    wk_ref, cos_ref, sin_ref, wv_ref, wq_ref, wo_ref, n1_ref, qpre_ref, kpre_ref, qrot_ref, krot_ref, val_ref,
    mixed_ref, lse_ref, r1_ref, gain_ref, in_sems, out_sems,
):
    seq_len, width = n1_ref.shape
    hd = qg_ref.shape[1]
    heads = wq_ref.shape[1] // hd
    kvs = wk_ref.shape[1] // hd
    group = heads // kvs
    padded = krot_ref.shape[0]
    length, z = info_ref[0], info_ref[1]
    scale = hd ** (-0.5) * LOG2E
    slices = shard_slices(z, width // 4)
    pending = copies(
        (wk_hbm, cos_hbm, sin_hbm, wv_hbm, wq_hbm, wo_hbm), (wk_ref, cos_ref, sin_ref, wv_ref, wq_ref, wo_ref), in_sems
    )
    sent = []

    def put(source, target):
        copy = pltpu.make_async_copy(source, target, out_sems.at[len(sent)])
        copy.start()
        sent.append(copy)

    def normalise(refs):
        for ref, cols in zip(refs, slices):
            tail = ref[seq_len : seq_len + TAIL, :].astype(f32)
            gain_ref[:, cols] = tail[0:8] + tail[8:16]

        def norm(rows):
            xs = [ref[rows, :].astype(f32) for ref in refs]
            r1 = row_scale(sum(x * x for x in xs), width)
            r1_ref[rows, :] = jnp.broadcast_to(r1, (ROWS, 128))
            for x, cols in zip(xs, slices):
                n1_ref[rows, cols] = (x * r1 * gain_ref[0:1, cols]).astype(bf16)

        row_loop(seq_len, ROWS, norm)

    assemble(z, (x0, x1, x1, x2, x3, x4, x5), normalise)
    put(n1_ref, n1_hbm)
    put(r1_ref, r1_hbm)
    put(gain_ref, gain_hbm)

    def project(w_ref, pre_ref, rot_ref, g_ref):
        count = w_ref.shape[1]
        for c in range(0, count, 2 * hd):
            pre_ref[:, c : c + 2 * hd] = dot(n1_ref[...], w_ref[:, c : c + 2 * hd])

        def rotate(rows):
            cos, sin = cos_ref[rows, :], sin_ref[rows, :]
            for c in range(0, count, hd):
                v = pre_ref[rows, c : c + hd]
                v = v * row_scale(v * v, hd) * g_ref[...]
                rot_ref[rows, c : c + hd] = (v * cos + pltpu.roll(v, hd // 2, 1) * sin).astype(bf16)

        row_loop(seq_len, ROWS, rotate)

    for copy in pending:
        copy.wait()
    project(wk_ref, kpre_ref, krot_ref, kg_ref)
    val_ref[0:seq_len, :] = dot(n1_ref[...], wv_ref[...]).astype(bf16)
    if padded > seq_len:
        krot_ref[seq_len:padded, :] = jnp.zeros((padded - seq_len, kvs * hd), bf16)
        val_ref[seq_len:padded, :] = jnp.zeros((padded - seq_len, kvs * hd), bf16)
    put(kpre_ref, kpre_hbm)
    put(krot_ref, krot_hbm)
    put(val_ref, val_hbm)
    project(wq_ref, qpre_ref, qrot_ref, qg_ref)
    put(qpre_ref, qpre_hbm)
    put(qrot_ref, qrot_hbm)

    for start, rows, keys in query_units(seq_len):
        bias = key_bias(length, keys)
        for g in range(kvs):
            key = krot_ref[0:keys, g * hd : (g + 1) * hd]
            val = val_ref[0:keys, g * hd : (g + 1) * hd]
            first = g * group
            q = jnp.concatenate(
                [qrot_ref[start : start + rows, h * hd : (h + 1) * hd] for h in range(first, first + group)], axis=0
            )
            e = jnp.exp2(dot_t(q, key) * scale + bias)
            total = jnp.sum(e, axis=1, keepdims=True)
            mixed = dot(e.astype(bf16), val) * (1.0 / total)
            lse = jnp.log2(total)
            for r in range(group):
                h = first + r
                mixed_ref[start : start + rows, h * hd : (h + 1) * hd] = mixed[r * rows : (r + 1) * rows].astype(bf16)
                lse_ref[start : start + rows, h : h + 1] = lse[r * rows : (r + 1) * rows]

    put(mixed_ref, mixed_hbm)
    put(lse_ref, lse_hbm)
    for part_ref, cols in zip((p_across, p_far, p_pair, p_own), slices):
        part_ref[...] = dot(mixed_ref[...], wo_ref[:, cols]).astype(part_ref.dtype)
    for copy in sent:
        copy.wait()


def wide(column, width):
    return jnp.concatenate([column] * (width // column.shape[1]), axis=1)


def norm_back(grad_s, normed_ref, scale_ref, inner_s, gain, part_ref, cols, width, gain_grad_ref=None):
    seq_len, step = grad_s.shape
    inverse = 1.0 / gain
    total = jnp.zeros((8, step), f32)
    for start in range(0, seq_len, ROWS):
        rows = pl.ds(start, ROWS)
        grad = grad_s[rows, :]
        unit = normed_ref[rows, cols].astype(f32) * inverse
        coef = wide(inner_s[rows, :] * (1.0 / width), step)
        part_ref[rows, :] = (wide(scale_ref[rows, :], step) * (grad * gain - unit * coef)).astype(part_ref.dtype)
        if gain_grad_ref is not None:
            total = total + jnp.sum((grad * unit).reshape(ROWS // 8, 8, step), axis=0)
    if gain_grad_ref is not None:
        gain_grad_ref[:, cols] = total


def ffn_kernel(
    info_ref, m0, m1, m2, m3, m4, m5, gain_hbm, wg_hbm, wu_hbm, wd_hbm, c0, c1, c2, c3, c4, c5, c6,
    p_across, p_far, p_pair, p_own, gfg_ref, n2_hbm, cotm_hbm, hid_hbm, dgu_hbm,
    gain_ref, wg_ref, wu_ref, wd_ref, cot_s, n2_ref, cotm_ref, hid_ref, dgu_ref,
    gate_s, up_s, gh_s, inner_s, r2_s, in_sems, out_sems,
):
    seq_len, width = n2_ref.shape
    hidden = wg_ref.shape[1]
    length, z = info_ref[0], info_ref[1]
    step = gate_s.shape[1]
    shard = width // 4
    slices = shard_slices(z, shard)
    got_gain, got_wg, got_wu, got_wd = copies(
        (gain_hbm, wg_hbm, wu_hbm, wd_hbm), (gain_ref, wg_ref, wu_ref, wd_ref), in_sems
    )

    def fetch(refs):
        return [
            pltpu.make_async_copy(
                ref.at[pl.ds(0, seq_len), :], cot_s.at[:, pl.ds(k * shard, shard)], in_sems.at[4 + k]
            )
            for k, ref in enumerate(refs)
        ]

    def start_cot(refs):
        for copy in fetch(refs):
            copy.start()

    assemble(z, (c0, c1, c2, c3, c4, c5, c6), start_cot)
    got_gain.wait()

    def normalise(refs):
        def norm(rows):
            ms = [ref[rows, :].astype(f32) for ref in refs]
            r2 = row_scale(sum(m * m for m in ms), width)
            r2_s[rows, :] = jnp.broadcast_to(r2, (ROWS, 128))
            inner_s[rows, :] = jnp.zeros((ROWS, 128), f32)
            for m, cols in zip(ms, slices):
                n2_ref[rows, cols] = (m * r2 * gain_ref[1:2, cols]).astype(bf16)

        row_loop(seq_len, ROWS, norm)

    assemble(z, (m0, m1, m1, m2, m3, m4, m5), normalise)
    for copy in fetch((c0, c1, c2, c3)) + [got_wg, got_wu, got_wd]:
        copy.wait()

    def mask(rows):
        slot = rows.start + lax.broadcasted_iota(jnp.int32, (ROWS, 1), 0)
        for k, cols in enumerate(slices):
            cot = cot_s[rows, k * shard : (k + 1) * shard].astype(f32)
            cotm_ref[rows, cols] = jnp.where(slot < length, cot, 0.0).astype(bf16)

    row_loop(seq_len, ROWS, mask)

    for j in range(0, hidden, step):
        gate_s[...] = dot(n2_ref[...], wg_ref[:, j : j + step])
        up_s[...] = dot(n2_ref[...], wu_ref[:, j : j + step])
        gh_s[...] = dot_t(cotm_ref[...], wd_ref[j : j + step, :])

        def elementwise(rows):
            gate, up, gh = gate_s[rows, :], up_s[rows, :], gh_s[rows, :]
            sig = jax.nn.sigmoid(gate)
            silu = gate * sig
            hid_ref[rows, j : j + step] = (silu * up).astype(bf16)
            dg = (gh * up * (sig * (1.0 + gate * (1.0 - sig)))).astype(bf16)
            du = (gh * silu).astype(bf16)
            dgu_ref[rows, j : j + step] = dg
            dgu_ref[rows, hidden + j : hidden + j + step] = du
            inner = jnp.sum(dg.astype(f32) * gate + du.astype(f32) * up, axis=1, keepdims=True)
            inner_s[rows, :] += jnp.broadcast_to(inner, (ROWS, 128))

        row_loop(seq_len, ROWS, elementwise)

    sent = copies(
        (n2_ref, cotm_ref, hid_ref, dgu_ref), (n2_hbm, cotm_hbm, hid_hbm, dgu_hbm), out_sems
    )
    for part_ref, cols in zip((p_across, p_far, p_pair, p_own), slices):
        gate_s[...] = dot_t(dgu_ref[:, 0:hidden], wg_ref[cols, :]) + dot_t(
            dgu_ref[:, hidden : 2 * hidden], wu_ref[cols, :]
        )
        norm_back(gate_s, n2_ref, r2_s, inner_s, gain_ref[1:2, cols], part_ref, cols, width, gfg_ref)
    for copy in sent:
        copy.wait()


def share(grads_s, core, keep_hbm, give_hbm, sems):
    return copies(
        (grads_s.at[pl.ds(core * 4, 4)], grads_s.at[pl.ds((1 - core) * 4, 4)]), (keep_hbm, give_hbm), sems
    )


def ffn_grad_kernel(
    info_ref, n2_hbm, dgu_hbm, hid_hbm, cotm_hbm, wd_hbm,
    p_across, p_far, p_pair, p_own, keep_hbm, give_hbm,
    n2_ref, dgu_ref, hid_ref, cotm_ref, wd_ref, grads_ref, in_sems, out_sems,
):
    pending = copies(
        (n2_hbm, dgu_hbm, hid_hbm, cotm_hbm, wd_hbm), (n2_ref, dgu_ref, hid_ref, cotm_ref, wd_ref), in_sems
    )
    width, hidden = n2_ref.shape[1], hid_ref.shape[1]
    upper, lower = width // 8, hidden // 8
    rest = upper - lower
    pending[0].wait()
    pending[1].wait()
    for c in range(0, 2 * hidden, 256):
        grad = t_dot(n2_ref[...], dgu_ref[:, c : c + 256])
        for d in range(8):
            grads_ref[d, :, c : c + 256] = grad[d * upper : (d + 1) * upper].astype(bf16)
    for copy in pending[2:]:
        copy.wait()
    for c in range(0, width, 256):
        grad = t_dot(hid_ref[...], cotm_ref[:, c : c + 256])
        for d in range(8):
            block = grad[d * lower : (d + 1) * lower].astype(bf16)
            if c < hidden:
                grads_ref[d, 0:lower, 2 * hidden + c : 2 * hidden + c + 256] = block
            else:
                for k in range(lower // rest):
                    col = 2 * hidden + k * 256
                    grads_ref[d, lower:upper, col : col + 256] = block[k * rest : (k + 1) * rest]
    sent = share(grads_ref, info_ref[3], keep_hbm, give_hbm, out_sems)
    for part_ref, cols in zip((p_across, p_far, p_pair, p_own), shard_slices(info_ref[1], p_own.shape[1])):
        part_ref[...] = dot(hid_ref[...], wd_ref[:, cols]).astype(bf16)
    for copy in sent:
        copy.wait()


def chip_blocks_kernel(info_ref, keep_hbm, other_ref, b0, b1, b2, b3, keep_ref, sems):
    (got,) = copies((keep_hbm,), (keep_ref,), sems)
    got.wait()
    for k, out_ref in enumerate((b0, b1, b2, b3)):
        block = jnp.bitwise_xor(info_ref[2], k)
        out_ref[...] = (keep_ref[block].astype(f32) + other_ref[block].astype(f32)).astype(bf16)


def halves_kernel(info_ref, keep_hbm, other_hbm, to_x, to_y, keep_x, keep_y, keep_ref, other_ref, sems):
    for copy in copies((keep_hbm, other_hbm), (keep_ref, other_ref), sems):
        copy.wait()
    cols = to_x.shape[2]
    for out_ref, first, flips in ((to_x, 0, (1, 3)), (keep_x, 0, (0, 2)), (to_y, cols, (2, 3)), (keep_y, cols, (0, 1))):
        for i, flip in enumerate(flips):
            block = jnp.bitwise_xor(info_ref[2], flip)
            out_ref[i] = (
                keep_ref[block, :, first : first + cols].astype(f32) + other_ref[block, :, first : first + cols].astype(f32)
            ).astype(bf16)


def halve_kernel(info_ref, keep_x, keep_y, got_x, got_y, to_y, to_x, own_x, own_y):
    own_x[...] = (keep_x[0].astype(f32) + got_x[0].astype(f32)).astype(bf16)
    own_y[...] = (keep_y[0].astype(f32) + got_y[0].astype(f32)).astype(bf16)
    to_y[...] = (keep_x[1].astype(f32) + got_x[1].astype(f32)).astype(bf16)
    to_x[...] = (keep_y[1].astype(f32) + got_y[1].astype(f32)).astype(bf16)


def join_kernel(info_ref, own_x, own_y, from_y, from_x, left_ref, right_ref):
    left_ref[...] = (own_x[...].astype(f32) + from_y[...].astype(f32)).astype(bf16)
    right_ref[...] = (own_y[...].astype(f32) + from_x[...].astype(f32)).astype(bf16)


def unpack_ffn_kernel(info_ref, *refs):
    q, core = info_ref[2], info_ref[3]
    gate_ref, up_ref, down_ref = refs[8:]
    width, hidden = gate_ref.shape
    upper, lower = width // 8, hidden // 8
    rest = upper - lower
    cols = 3 * hidden // 2
    first = 2 * hidden - cols
    for half, (lefts, lefts_x, rights, rights_y) in ((core, refs[0:4]), (1 - core, refs[4:8])):
        for k in range(4):
            block = half * 4 + jnp.bitwise_xor(q, k)
            left, i = (lefts if k in (0, 2) else lefts_x), (0 if k in (0, 1) else 1)
            right, j = (rights if k in (0, 1) else rights_y), (0 if k in (0, 2) else 1)
            rows = pl.ds(pl.multiple_of(block * upper, upper), upper)
            gate_ref[rows, :] = left[i, :, 0:hidden].astype(f32)
            up_ref[rows, 0 : cols - hidden] = left[i, :, hidden:cols].astype(f32)
            up_ref[rows, cols - hidden : hidden] = right[j, :, 0:first].astype(f32)
            rows = pl.ds(pl.multiple_of(block * lower, lower), lower)
            down_ref[rows, 0:hidden] = right[j, 0:lower, first : first + hidden].astype(f32)
            for n in range(lower // rest):
                rows = pl.ds(pl.multiple_of(block * lower + n * rest, rest), rest)
                col = first + n * 256
                down_ref[rows, hidden:width] = right[j, lower:upper, col : col + 256].astype(f32)


def attn_backward_kernel(
    info_ref, g0, g1, g2, g3, g4, g5, qg_ref, kg_ref, wo_hbm, qrot_hbm, krot_hbm, val_hbm, mixed_hbm, lse_hbm,
    cos_hbm, sin_hbm, qpre_hbm, kpre_hbm, n1_hbm, wq_hbm, wk_hbm, wv_hbm, r1_hbm, gain_hbm,
    p_across, p_far, p_pair, p_own, gag_ref, qgg_ref, kgg_ref, keep_hbm, give_hbm,
    wo_ref, qrot_ref, krot_ref, val_ref, mixed_ref, lse_ref, cos_ref, sin_ref, qpre_ref, kpre_ref, n1_ref,
    wq_ref, wk_ref, wv_ref, r1_ref, gain_ref,
    ga_ref, gm_s, dq_s, dk_s, dv_s, dqkv_ref, inner_ref, acc_s, grads_ref, sems, out_sems,
):
    seq_len, width = ga_ref.shape
    hd = qg_ref.shape[1]
    qw, kw = qpre_ref.shape[1], kpre_ref.shape[1]
    heads, kvs = qw // hd, kw // hd
    group = heads // kvs
    length, z = info_ref[0], info_ref[1]
    scale = hd ** (-0.5)
    slices = shard_slices(z, width // 4)
    pending = copies(
        (
            wo_hbm, qrot_hbm, krot_hbm, val_hbm, mixed_hbm, lse_hbm, cos_hbm, sin_hbm, qpre_hbm, kpre_hbm, n1_hbm,
            wq_hbm, wk_hbm, wv_hbm, r1_hbm, gain_hbm,
        ),
        (
            wo_ref, qrot_ref, krot_ref, val_ref, mixed_ref, lse_ref, cos_ref, sin_ref, qpre_ref, kpre_ref, n1_ref,
            wq_ref, wk_ref, wv_ref, r1_ref, gain_ref,
        ),
        sems,
    )

    def collect(refs):
        for ref, cols in zip(refs, slices):
            ga_ref[:, cols] = ref[...]

    assemble(z, (g0, g1, g1, g2, g3, g4, g5), collect)

    pending[0].wait()
    for c in range(0, qw, 256):
        gm_s[:, c : c + 256] = dot_t(ga_ref[...], wo_ref[c : c + 256, :]).astype(bf16)
    dk_s[...] = jnp.zeros_like(dk_s)
    dv_s[...] = jnp.zeros_like(dv_s)
    for copy in pending[1:6]:
        copy.wait()

    for start, rows, keys in query_units(seq_len):
        bias = key_bias(length, keys)
        for g in range(kvs):
            first = g * group
            cols = slice(g * hd, (g + 1) * hd)
            key, val = krot_ref[0:keys, cols], val_ref[0:keys, cols]

            def stacked(ref):
                return jnp.concatenate(
                    [ref[start : start + rows, h * hd : (h + 1) * hd] for h in range(first, first + group)], axis=0
                )

            q, gm, mixed = stacked(qrot_ref), stacked(gm_s), stacked(mixed_ref)
            lse = jnp.concatenate(
                [lse_ref[start : start + rows, h : h + 1] for h in range(first, first + group)], axis=0
            )
            p = jnp.exp2(dot_t(q, key) * (scale * LOG2E) + bias - lse)
            delta = jnp.sum(gm.astype(f32) * mixed.astype(f32), axis=1, keepdims=True)
            ds = (p * (dot_t(gm, val) - delta)).astype(bf16)
            dv_s[0:keys, cols] += t_dot(p.astype(bf16), gm)
            dk_s[0:keys, cols] += t_dot(ds, q)
            dq = dot(ds, key)
            for r in range(group):
                h = first + r
                dq_s[start : start + rows, h * hd : (h + 1) * hd] = dq[r * rows : (r + 1) * rows]

    for copy in pending[6:]:
        copy.wait()
    ones = jnp.full((hd, hd), 1.0 / hd, bf16)

    def unrotate(rows, rot_s, pre_ref, g_ref, count, base, gain_sum):
        cos, sin = cos_ref[rows, :], sin_ref[rows, :]
        inner = jnp.zeros((ROWS, hd), f32)
        for c in range(0, count, hd):
            g = rot_s[rows, c : c + hd] * scale
            u = g * cos + pltpu.roll(g * sin, hd // 2, 1)
            v = pre_ref[rows, c : c + hd]
            r = lax.rsqrt(dot((v * v).astype(bf16), ones) + NORM_EPSILON)
            unit = v * r
            t = u * unit
            gain_sum = gain_sum + jnp.sum(t.reshape(ROWS // 8, 8, hd), axis=0)
            mean = dot((t * g_ref[...]).astype(bf16), ones)
            dqkv_ref[rows, base + c : base + c + hd] = (r * (u * g_ref[...] - unit * mean)).astype(bf16)
            inner = inner + (hd * NORM_EPSILON) * (r * r * mean)
        return inner, gain_sum

    qgs = kgs = jnp.zeros((8, hd), f32)
    for start in range(0, seq_len, ROWS):
        rows = pl.ds(start, ROWS)
        qi, qgs = unrotate(rows, dq_s, qpre_ref, qg_ref, qw, 0, qgs)
        ki, kgs = unrotate(rows, dk_s, kpre_ref, kg_ref, kw, qw, kgs)
        dv = dv_s[rows, :].astype(bf16)
        dqkv_ref[rows, qw + kw : qw + 2 * kw] = dv
        vi = jnp.sum(dv.astype(f32) * val_ref[rows, :].astype(f32), axis=1, keepdims=True)
        inner_ref[rows, :] = qi + ki + vi
    qgg_ref[...] = qgs
    kgg_ref[...] = kgs

    upper, lower = width // 8, qw // 8
    for c in range(0, width, 256):
        grad = t_dot(n1_ref[...], dqkv_ref[:, c : c + 256])
        out = t_dot(mixed_ref[...], ga_ref[:, c : c + 256])
        for d in range(8):
            grads_ref[d, 0:upper, c : c + 256] = grad[d * upper : (d + 1) * upper].astype(bf16)
            grads_ref[d, upper : upper + lower, c : c + 256] = out[d * lower : (d + 1) * lower].astype(bf16)
    sent = share(grads_ref, info_ref[3], keep_hbm, give_hbm, out_sems)
    for part_ref, cols in zip((p_across, p_far, p_pair, p_own), slices):
        acc_s[...] = (
            dot_t(dqkv_ref[:, 0:qw], wq_ref[cols, :])
            + dot_t(dqkv_ref[:, qw : qw + kw], wk_ref[cols, :])
            + dot_t(dqkv_ref[:, qw + kw : qw + 2 * kw], wv_ref[cols, :])
        )
        norm_back(acc_s, n1_ref, r1_ref, inner_ref, gain_ref[0:1, cols], part_ref, cols, width, gag_ref)
    for copy in sent:
        copy.wait()


def output_kernel(info_ref, middle_ref, attn_ref, own_ref, pair_ref, across_ref, out_ref, sums_ref):
    seq_len, shard = middle_ref.shape
    length = info_ref[0]
    sums = [jnp.zeros((8, shard), f32)] * 3
    for start in range(0, seq_len, ROWS):
        rows = pl.ds(start, ROWS)
        ffn = own_ref[rows, :].astype(f32) + (pair_ref[rows, :].astype(f32) + across_ref[rows, :].astype(f32))
        out = middle_ref[rows, :] + ffn
        out_ref[rows, :] = out.astype(bf16)
        slot = start + lax.broadcasted_iota(jnp.int32, (ROWS, 1), 0)
        for i, v in enumerate((out, attn_ref[rows, :], ffn)):
            v = jnp.where(slot < length, v, 0.0)
            sums[i] = sums[i] + jnp.sum((v * v).reshape(ROWS // 8, 8, shard), axis=0)
    for i in range(3):
        sums_ref[i : i + 1, :] = jnp.sum(sums[i], axis=0, keepdims=True)


def small_kernel(info_ref, gag_ref, gfg_ref, qgg_ref, kgg_ref, sums_ref, small_ref):
    hd, shard = qgg_ref.shape[1], sums_ref.shape[1]
    small_ref[...] = jnp.zeros(small_ref.shape, f32)
    small_ref[0:1, :] = jnp.sum(gag_ref[...], axis=0, keepdims=True)
    small_ref[1:2, :] = jnp.sum(gfg_ref[...], axis=0, keepdims=True)
    small_ref[2:3, 0:hd] = jnp.sum(qgg_ref[...], axis=0, keepdims=True)
    small_ref[2:3, hd : 2 * hd] = jnp.sum(kgg_ref[...], axis=0, keepdims=True)
    lane = lax.broadcasted_iota(jnp.int32, (1, 128), 1)
    totals = (info_ref[0] * shard).astype(f32) * (lane == 3).astype(f32)
    for i in range(3):
        totals = totals + jnp.sum(sums_ref[i : i + 1, :], axis=1, keepdims=True) * (lane == i).astype(f32)
    small_ref[2:3, 2 * hd : 2 * hd + 128] = totals


def block_kernel(info_ref, b0, b1, b2, b3, small_ref, out_ref):
    rows = b0.shape[0]
    out_ref[0:rows, :] = (
        (b0[...].astype(f32) + b1[...].astype(f32)) + (b2[...].astype(f32) + b3[...].astype(f32))
    ).astype(bf16)
    small = small_ref[...]
    high = small.astype(bf16)
    out_ref[rows : rows + TAIL, :] = jnp.concatenate([high, (small - high.astype(f32)).astype(bf16)], axis=0)


def unpack_kernel(info_ref, h0, h1, h2, h3, t0, t1, t2, t3, gq_ref, gk_ref, gv_ref, go_ref, small_ref):
    q, core = info_ref[2], info_ref[3]
    qw, kw = gq_ref.shape[1], gk_ref.shape[1]
    upper, lower = gq_ref.shape[0] // 8, go_ref.shape[0] // 8
    small = jnp.zeros(small_ref.shape, f32)
    for refs, half in (((h0, h1, h2, h3), core), ((t0, t1, t2, t3), 1 - core)):
        for k, ref in enumerate(refs):
            block = half * 4 + jnp.bitwise_xor(q, k)
            rows = pl.ds(pl.multiple_of(block * upper, upper), upper)
            gq_ref[rows, :] = ref[0:upper, 0:qw].astype(f32)
            gk_ref[rows, :] = ref[0:upper, qw : qw + kw].astype(f32)
            gv_ref[rows, :] = ref[0:upper, qw + kw : qw + 2 * kw].astype(f32)
            rows = pl.ds(pl.multiple_of(block * lower, lower), lower)
            go_ref[rows, :] = ref[upper : upper + lower, :].astype(f32)
            tail = ref[upper + lower : upper + lower + TAIL, :].astype(f32)
            small = small + (tail[0:8] + tail[8:16])
    small_ref[...] = small


SPECS = {
    "s": pl.BlockSpec(memory_space=pltpu.SMEM),
    "v": pl.BlockSpec(memory_space=pltpu.VMEM),
    "a": pl.BlockSpec(memory_space=pl.ANY),
}


def call(body, outs, args, scratch=(), sems=(), flops=0, bytes_accessed=0, limit=SMALL_BYTES):
    places, arrays = [], []
    for place, *group in args:
        places += [place] * len(group)
        arrays += group
    return pl.pallas_call(
        body,
        out_shape=[jax.ShapeDtypeStruct(s, d) for s, d, _ in outs],
        in_specs=[SPECS[p] for p in places],
        out_specs=[SPECS[p] for _, _, p in outs],
        scratch_shapes=[pltpu.VMEM(s, d) for s, d in scratch] + [pltpu.SemaphoreType.DMA((n,)) for n in sems],
        compiler_params=pltpu.CompilerParams(vmem_limit_bytes=limit),
        cost_estimate=pl.CostEstimate(flops=flops, bytes_accessed=bytes_accessed, transcendentals=0),
    )(*arrays)


PAIRS = ((0, 1), (1, 0), (2, 3), (3, 2))
MIDDLE = ((1, 2), (2, 1))
OUTWARD = ((1, 0), (2, 3))
INWARD = ((0, 1), (3, 2))
OUTWARD_TWO = ((2, 0), (1, 3))
INWARD_TWO = ((0, 2), (3, 1))


def send(rows, pairs):
    return lax.ppermute(rows, "tensor", pairs)


def hold(*values):
    return lax.optimization_barrier(values)


def gather_line(own):
    pair = send(own, PAIRS)
    across_mid = send(own, MIDDLE)
    far_end = send(pair, OUTWARD_TWO)
    far_mid = send(pair, MIDDLE)
    across_end = send(across_mid, OUTWARD)
    return own, pair, across_mid, across_end, far_mid, far_end


def pick(end, from_end, from_middle):
    return jnp.where(end, from_end, from_middle)


def scatter_first(parts):
    across, far, _, _ = parts
    return send(far, INWARD_TWO), send(far, MIDDLE), send(across, INWARD)


def scatter_last(parts, first):
    across, _, pair, own = parts
    two, three, one = first
    to_pair = (pair.astype(f32) + (two.astype(f32) + three.astype(f32))).astype(bf16)
    to_across = (across.astype(f32) + one.astype(f32)).astype(bf16)
    return own, send(to_pair, PAIRS), send(to_across, MIDDLE)


def add(a, b):
    return (a.astype(f32) + b.astype(f32)).astype(bf16)


def total(terms):
    own, pair, across = terms
    return own.astype(f32) + (pair.astype(f32) + across.astype(f32))


def split_rows(values):
    high = lax.optimization_barrier(values.astype(bf16))
    low = (values - high.astype(f32)).astype(bf16)
    return jnp.concatenate([high, low], axis=0)


def swap(values, bit):
    return lax.ppermute(values, "dp", [(i, i ^ bit) for i in range(8)])


def to_chips(keep, other, info):
    rows, width = keep.shape[1:]
    blocks = call(
        chip_blocks_kernel,
        [((rows, width), bf16, "v")] * 4,
        (("s", info), ("a", keep), ("v", other)),
        scratch=[((4, rows, width), bf16)],
        sems=(1,),
        bytes_accessed=12 * rows * width,
    )
    return [blocks[0]] + [swap(blocks[k], 2 * k) for k in (1, 2, 3)]


def from_chips(own):
    return [own] + [swap(own, 2 * k) for k in (1, 2, 3)]


def per_device(
    hidden_in, lengths, w_query, w_key, w_value, w_out, attn_gain, ffn_gain,
    query_gain, key_gain, w_gate, w_up, w_down, cotangent,
):
    seq_len, shard = hidden_in.shape
    width = w_query.shape[0]
    hd = query_gain.shape[0]
    qw, kw = w_query.shape[1], w_key.shape[1]
    hidden = w_gate.shape[1]
    padded = -(-seq_len // BLOCK) * BLOCK
    z = lax.axis_index("tensor").astype(jnp.int32)
    dp = lax.axis_index("dp").astype(jnp.int32)
    chips = lax.axis_size("dp") == 8
    q, core = (dp // 2, dp % 2) if chips else (0 * dp, 0 * dp)
    info = jnp.stack([lengths[0], z, q, core])
    parts = [((seq_len, shard), bf16, "v")] * 4

    end = (z == 0) | (z == 3)
    gains = jnp.concatenate([attn_gain[None], ffn_gain[None], jnp.zeros((6, shard), f32)], axis=0)
    x = jnp.concatenate([hidden_in, split_rows(gains)], axis=0)
    cot = jnp.concatenate([cotangent, jnp.zeros((TAIL, shard), bf16)], axis=0)
    x_pair, x_mid = send(x, PAIRS), send(x, MIDDLE)
    x_pair, x_mid, cot = hold(x_pair, x_mid, cot)
    x_end, x_far = send(pick(end, cot, x_mid), PAIRS), send(x_pair, MIDDLE)
    x_end, x_far, cot = hold(x_end, x_far, cot)
    x_last, cot_far = send(x_far, OUTWARD), send(x_end, MIDDLE)
    x_last, cot_far, x_end, cot = hold(x_last, cot_far, x_end, cot)
    cot_mid, cot_pair, cot_last = send(cot, MIDDLE), send(cot, OUTWARD), send(cot_far, OUTWARD)
    cos, sin = rope_tables(seq_len, hd)
    qg, kg = query_gain[None], key_gain[None]
    resid = hidden_in.astype(f32)
    valid = (jnp.arange(seq_len, dtype=jnp.int32) < lengths[0]).astype(f32)[:, None]

    saved = [
        ((seq_len, width), bf16), ((seq_len, qw), f32), ((seq_len, kw), f32), ((seq_len, qw), bf16),
        ((padded, kw), bf16), ((padded, kw), bf16), ((seq_len, qw), bf16), ((seq_len, 128), f32),
        ((seq_len, 128), f32), ((8, width), f32),
    ]
    weights = [((width, kw), bf16), ((width, kw), bf16), ((width, qw), bf16), ((qw, width), bf16)]
    tables = [((seq_len, hd), f32)] * 2
    *attn_parts, n1, qpre, kpre, qrot, krot, val, mixed, lse, r1, gain = call(
        attn_forward_kernel,
        parts + [(s, d, "a") for s, d in saved],
        (
            ("s", info), ("v", x, x_pair, x_mid, x_end, x_far, x_last, qg, kg),
            ("a", w_key, cos, sin, w_value, w_query, w_out),
        ),
        scratch=weights[:1] + tables + weights[1:] + saved,
        sems=(6, 10),
        limit=VMEM_BYTES,
        flops=2 * seq_len * width * (2 * qw + 2 * kw) + 4 * seq_len * seq_len * qw,
        bytes_accessed=14_000_000,
    )
    attn_parts, cot_mid, cot_pair, cot_last = hold(attn_parts, cot_mid, cot_pair, cot_last)
    across, far, pair, own = attn_parts
    two, three = send(far, INWARD_TWO), send(far, MIDDLE)
    one = send(pick(end, across, cot_mid[:seq_len]), PAIRS)
    zero_end = pick(end, jnp.zeros_like(one), one)
    attn_local = total(scatter_last(attn_parts, (two, three, zero_end)))
    middle = resid + attn_local
    shard_two, one = hold(middle.astype(bf16), one)
    m_parts = gather_line(shard_two)

    kept = [((seq_len, width), bf16), ((seq_len, width), bf16), ((seq_len, hidden), bf16), ((seq_len, 2 * hidden), bf16)]
    *ffn_parts, gfg, n2, cotm, hid, dgu = call(
        ffn_kernel,
        parts + [((8, width), f32, "v")] + [(s, d, "a") for s, d in kept],
        (
            ("s", info), ("v", *m_parts), ("a", gain, w_gate, w_up, w_down),
            ("a", cot, x_end, cot_pair, cot_mid, one, cot_far, cot_last),
        ),
        scratch=[((8, width), f32)] + [((width, hidden), bf16)] * 2 + [((hidden, width), bf16), ((seq_len, width), bf16)]
        + kept + [((seq_len, 256), f32)] * 3 + [((seq_len, 128), f32)] * 2,
        sems=(8, 4),
        limit=VMEM_BYTES,
        flops=2 * seq_len * width * hidden * 5,
        bytes_accessed=16_000_000,
    )
    grad_top = cotangent.astype(f32) * valid
    first = scatter_first(ffn_parts)
    blocks = ((4, width // 8, 3 * hidden), bf16, "a")
    *down_parts, ffn_keep, ffn_give = call(
        ffn_grad_kernel,
        parts + [blocks] * 2,
        (("s", info), ("a", n2, dgu, hid, cotm, w_down)),
        scratch=[kept[0], kept[3], kept[2], kept[1], ((hidden, width), bf16), ((8, width // 8, 3 * hidden), bf16)],
        sems=(5, 2),
        flops=2 * seq_len * width * hidden * 4,
        bytes_accessed=14_000_000,
    )
    first, ffn_keep, ffn_give = hold(first, ffn_keep, ffn_give)
    back = scatter_last(ffn_parts, first)
    if chips:
        ffn_other = swap(ffn_give, 1)
        cols = (width // 8, 3 * hidden // 2)
        to_x, to_y, keep_x, keep_y = call(
            halves_kernel,
            [((2, *cols), bf16, "v")] * 4,
            (("s", info), ("a", ffn_keep, ffn_other)),
            scratch=[((4, width // 8, 3 * hidden), bf16)] * 2,
            sems=(2,),
        )
        back, to_x, to_y, keep_x, keep_y = hold(back, to_x, to_y, keep_x, keep_y)
    grad_middle = grad_top + total(back)
    across, far, pair, own = down_parts
    ga = grad_middle.astype(bf16)
    ga_pair, ga_mid = send(ga, PAIRS), send(ga, MIDDLE)
    if chips:
        got_x, got_y = swap(to_x, 2), swap(to_y, 4)
    if chips:
        ga_pair, ga_mid, far, got_x, got_y = hold(ga_pair, ga_mid, far, got_x, got_y)
        to_y, to_x, own_x, own_y = call(
            halve_kernel, [(cols, bf16, "v")] * 4, (("s", info), ("v", keep_x, keep_y, got_x, got_y))
        )
        from_y, from_x = swap(to_y, 4), swap(to_x, 2)
    ga_end, ga_far = send(pick(end, far, ga_mid), PAIRS), send(ga_pair, MIDDLE)
    if chips:
        ga_end, ga_far, across, from_y, from_x = hold(ga_end, ga_far, across, from_y, from_x)
        left, right = call(
            join_kernel, [(cols, bf16, "v")] * 2, (("s", info), ("v", own_x, own_y, from_y, from_x))
        )
        left_y, right_x = swap(left, 4), swap(right, 2)
    ga_last = send(pick(end, across, ga_far), PAIRS)
    got_far = send(add(far, ga_end), MIDDLE)
    if chips:
        ga_last, got_far, left_y, right_x = hold(ga_last, got_far, left_y, right_x)
        lefts, rights = jnp.stack([left, left_y]), jnp.stack([right, right_x])
        lefts_x, rights_y = swap(lefts, 2), swap(rights, 4)
    ga_parts = (ga, ga_pair, ga_mid, ga_end, ga_far, ga_last)
    ffn_terms = (own, send(add(pair, got_far), PAIRS), send(add(across, ga_last), MIDDLE))

    blocks = (4, (width + qw) // 8, width)
    *back_parts, gag, qgg, kgg, keep, give = call(
        attn_backward_kernel,
        parts + [((8, width), f32, "v"), ((8, hd), f32, "v"), ((8, hd), f32, "v"), (blocks, bf16, "a"), (blocks, bf16, "a")],
        (
            ("s", info), ("v", *ga_parts, qg, kg),
            ("a", w_out, qrot, krot, val, mixed, lse, cos, sin, qpre, kpre, n1, w_query, w_key, w_value, r1, gain),
        ),
        scratch=[weights[3], saved[3], saved[4], saved[5], saved[6], saved[7], *tables, saved[1], saved[2], saved[0]]
        + [weights[2], weights[0], weights[1], saved[8], saved[9]]
        + [((seq_len, width), bf16), ((seq_len, qw), bf16), ((seq_len, qw), f32), ((padded, kw), f32), ((padded, kw), f32)]
        + [((seq_len, qw + 2 * kw), bf16), ((seq_len, 128), f32), ((seq_len, shard), f32), ((8, *blocks[1:]), bf16)],
        sems=(16, 2),
        limit=VMEM_BYTES,
        flops=2 * seq_len * width * (4 * qw + 4 * kw) + 10 * seq_len * seq_len * qw,
        bytes_accessed=20_000_000,
    )
    if chips:
        back_parts, ffn_terms, keep, give, lefts_x, rights_y = hold(back_parts, ffn_terms, keep, give, lefts_x, rights_y)
        blocks = to_chips(keep, swap(give, 1), info)
    out_rows, sums = call(
        output_kernel,
        [((seq_len, shard), bf16, "v"), ((8, shard), f32, "v")],
        (("s", info), ("v", middle, attn_local, *ffn_terms)),
        bytes_accessed=2_000_000,
    )
    small = call(small_kernel, [((8, width), f32, "v")], (("s", info), ("v", gag, gfg, qgg, kgg, sums)))[0]
    shapes = [(width, qw), (width, kw), (width, kw), (qw, width)]
    if chips:
        ffn_halves = (lefts, lefts_x, rights, rights_y)
        g_gate, g_up, g_down = call(
            unpack_ffn_kernel,
            [(s, f32, "v") for s in ((width, hidden), (width, hidden), (hidden, width))],
            (("s", info), ("v", *ffn_halves, *[swap(b, 1) for b in ffn_halves])),
            bytes_accessed=14_000_000,
        )
        small = small + send(small, PAIRS)
        small = small + send(small, ((0, 2), (2, 0), (1, 3), (3, 1)))
        small, back_parts = hold(small, back_parts)
        blocks, small, g_gate, g_up, g_down = hold(blocks, small, g_gate, g_up, g_down)
        own = call(
            block_kernel,
            [((blocks[0].shape[0] + TAIL, width), bf16, "v")],
            (("s", info), ("v", *blocks, small)),
            bytes_accessed=2_000_000,
        )[0]
        everyone = from_chips(own)
        back_terms = scatter_last(back_parts, scatter_first(back_parts))
        gq, gk, gv, go, small = call(
            unpack_kernel,
            [(s, f32, "v") for s in shapes] + [((8, width), f32, "v")],
            (("s", info), ("v", *everyone, *[swap(b, 1) for b in everyone])),
            bytes_accessed=9_000_000,
        )
    else:
        back_terms = scatter_last(back_parts, scatter_first(back_parts))
        grads, ffn_grads = lax.psum((jnp.concatenate([keep, give]), jnp.concatenate([ffn_keep, ffn_give])), "dp")
        small = lax.psum(small, ("dp", "tensor"))
        g_qkv = grads[:, : width // 8].reshape(width, width).astype(f32)
        gq, gk, gv = g_qkv[:, :qw], g_qkv[:, qw : qw + kw], g_qkv[:, qw + kw :]
        go = grads[:, width // 8 :].reshape(qw, width).astype(f32)
        g_gate = ffn_grads[:, :, :hidden].reshape(width, hidden).astype(f32)
        g_up = ffn_grads[:, :, hidden : 2 * hidden].reshape(width, hidden).astype(f32)
        folded = ffn_grads[:, :, 2 * hidden :]
        lower = hidden // 8
        tail = folded[:, lower:].reshape(8, width // 8 - lower, -1, 256).transpose(0, 2, 1, 3).reshape(8, lower, 256)
        g_down = jnp.concatenate([folded[:, :lower], tail], axis=2).reshape(hidden, width).astype(f32)
    input_grad = (grad_middle + total(back_terms)).astype(bf16)
    grad_attn_gain = lax.dynamic_slice(small[0], (z * shard,), (shard,))
    grad_ffn_gain = lax.dynamic_slice(small[1], (z * shard,), (shard,))
    totals = small[2, 2 * hd : 2 * hd + 4]
    return (
        out_rows,
        input_grad,
        gq,
        gk,
        gv,
        go,
        grad_attn_gain,
        grad_ffn_gain,
        small[2, :hd],
        small[2, hd : 2 * hd],
        g_gate,
        g_up,
        g_down,
        jnp.sqrt(totals[:3] / totals[3]),
    )


def solution(mesh):
    rows, cols, first = P("dp", "tensor"), P(None, "tensor"), P("tensor", None)
    gain = P("tensor")
    return jax.shard_map(
        per_device,
        mesh=mesh,
        in_specs=(rows, P("dp"), cols, cols, cols, first, gain, gain, P(), P(), cols, cols, first, rows),
        out_specs=(rows, rows, cols, cols, cols, first, gain, gain, P(), P(), cols, cols, first, P()),
        check_vma=False,
    )
```

```python
import functools

import jax
import jax.numpy as jnp
from jax import lax
from jax.experimental import pallas as pl
from jax.experimental.pallas import tpu as pltpu
from jax.sharding import PartitionSpec as P

BLOCK = 256
NORM_EPSILON = 1e-06
ROPE_THETA = 1000000.0
LOG2E = 1.4426950408889634
NEG = -1e30
ROWS = 64
TAIL = 16
FULL_BYTES = 60 * 1024 * 1024
VMEM_BYTES = 40 * 1024 * 1024
SMALL_BYTES = 24 * 1024 * 1024

bf16 = jnp.bfloat16
f32 = jnp.float32


def dot(a, b):
    return jnp.dot(a, b, preferred_element_type=f32)


def dot_t(a, b):
    return lax.dot_general(a, b, (((1,), (1,)), ((), ())), preferred_element_type=f32)


def t_dot(a, b):
    return lax.dot_general(a, b, (((0,), (0,)), ((), ())), preferred_element_type=f32)


def row_loop(count, step, body):
    for start in range(0, count, step):
        body(pl.ds(start, step))


def rope_tables(length, width):
    half_width = width // 2
    frequency = ROPE_THETA ** (-(jnp.arange(half_width, dtype=f32) * (2.0 / width)))
    angles = jnp.arange(length, dtype=f32)[:, None] * frequency[None, :]
    cos, sin = jnp.cos(angles), jnp.sin(angles)
    return jnp.concatenate([cos, cos], axis=1), jnp.concatenate([-sin, sin], axis=1)


def query_units(seq_len):
    units = []
    start = 0
    while start < seq_len:
        rows = min(128, seq_len - start)
        keys = (start // BLOCK + 1) * BLOCK
        units.append((start, rows, keys))
        start += rows
    return units


def roles(z):
    low = z < 2
    return jnp.where(low, 2, 1), jnp.where(low, 3, 0), z + 1 - 2 * lax.rem(z, 2), z


def shard_slices(z, width):
    return [pl.ds(pl.multiple_of(shard * width, width), width) for shard in roles(z)]


def assemble(z, pieces, body):
    own, pair_mid, pair_end, across_mid, across_end, far_mid, far_end = pieces
    end = (z == 0) | (z == 3)

    @pl.when(end)
    def _():
        body((across_end, far_end, pair_end, own))

    @pl.when(jnp.logical_not(end))
    def _():
        body((across_mid, far_mid, pair_mid, own))


def key_bias(length, keys):
    slot = lax.broadcasted_iota(jnp.int32, (1, keys), 1)
    return jnp.where(slot < length, 0.0, NEG).astype(f32)


def row_scale(squares, width):
    return lax.rsqrt(jnp.sum(squares, axis=1, keepdims=True) * (1.0 / width) + NORM_EPSILON)


def copies(sources, targets, sems):
    pending = [pltpu.make_async_copy(a, b, sems.at[i]) for i, (a, b) in enumerate(zip(sources, targets))]
    for copy in pending:
        copy.start()
    return pending


def attn_forward_kernel(
    info_ref, x0, x1, x2, x3, x4, x5, qg_ref, kg_ref, wk_hbm, cos_hbm, sin_hbm, wv_hbm, wq_hbm, wo_hbm,
    p_across, p_far, p_pair, p_own, n1_hbm, qpre_hbm, kpre_hbm, qrot_hbm, krot_hbm, val_hbm, mixed_hbm, lse_hbm,
    r1_hbm, gain_hbm,
    wk_ref, cos_ref, sin_ref, wv_ref, wq_ref, wo_ref, n1_ref, qpre_ref, kpre_ref, qrot_ref, krot_ref, val_ref,
    mixed_ref, lse_ref, r1_ref, gain_ref, in_sems, out_sems,
):
    seq_len, width = n1_ref.shape
    hd = qg_ref.shape[1]
    heads = wq_ref.shape[1] // hd
    kvs = wk_ref.shape[1] // hd
    group = heads // kvs
    padded = krot_ref.shape[0]
    length, z = info_ref[0], info_ref[1]
    scale = hd ** (-0.5) * LOG2E
    slices = shard_slices(z, width // 4)
    pending = copies(
        (wk_hbm, cos_hbm, sin_hbm, wv_hbm, wq_hbm, wo_hbm), (wk_ref, cos_ref, sin_ref, wv_ref, wq_ref, wo_ref), in_sems
    )
    sent = []

    def put(source, target):
        copy = pltpu.make_async_copy(source, target, out_sems.at[len(sent)])
        copy.start()
        sent.append(copy)

    def normalise(refs):
        for ref, cols in zip(refs, slices):
            tail = ref[seq_len : seq_len + TAIL, :].astype(f32)
            gain_ref[:, cols] = tail[0:8] + tail[8:16]

        def norm(rows):
            xs = [ref[rows, :].astype(f32) for ref in refs]
            r1 = row_scale(sum(x * x for x in xs), width)
            r1_ref[rows, :] = jnp.broadcast_to(r1, (ROWS, 128))
            for x, cols in zip(xs, slices):
                n1_ref[rows, cols] = (x * r1 * gain_ref[0:1, cols]).astype(bf16)

        row_loop(seq_len, ROWS, norm)

    assemble(z, (x0, x1, x1, x2, x3, x4, x5), normalise)
    put(n1_ref, n1_hbm)
    put(r1_ref, r1_hbm)
    put(gain_ref, gain_hbm)

    def project(w_ref, pre_ref, rot_ref, g_ref):
        count = w_ref.shape[1]
        for c in range(0, count, 2 * hd):
            pre_ref[:, c : c + 2 * hd] = dot(n1_ref[...], w_ref[:, c : c + 2 * hd])

        def rotate(rows):
            cos, sin = cos_ref[rows, :], sin_ref[rows, :]
            for c in range(0, count, hd):
                v = pre_ref[rows, c : c + hd]
                v = v * row_scale(v * v, hd) * g_ref[...]
                rot_ref[rows, c : c + hd] = (v * cos + pltpu.roll(v, hd // 2, 1) * sin).astype(bf16)

        row_loop(seq_len, ROWS, rotate)

    for copy in pending:
        copy.wait()
    project(wk_ref, kpre_ref, krot_ref, kg_ref)
    val_ref[0:seq_len, :] = dot(n1_ref[...], wv_ref[...]).astype(bf16)
    if padded > seq_len:
        krot_ref[seq_len:padded, :] = jnp.zeros((padded - seq_len, kvs * hd), bf16)
        val_ref[seq_len:padded, :] = jnp.zeros((padded - seq_len, kvs * hd), bf16)
    put(kpre_ref, kpre_hbm)
    put(krot_ref, krot_hbm)
    put(val_ref, val_hbm)
    project(wq_ref, qpre_ref, qrot_ref, qg_ref)
    put(qpre_ref, qpre_hbm)
    put(qrot_ref, qrot_hbm)

    for start, rows, keys in query_units(seq_len):
        bias = key_bias(length, keys)
        for g in range(kvs):
            key = krot_ref[0:keys, g * hd : (g + 1) * hd]
            val = val_ref[0:keys, g * hd : (g + 1) * hd]
            first = g * group
            q = jnp.concatenate(
                [qrot_ref[start : start + rows, h * hd : (h + 1) * hd] for h in range(first, first + group)], axis=0
            )
            e = jnp.exp2(dot_t(q, key) * scale + bias)
            total = jnp.sum(e, axis=1, keepdims=True)
            mixed = dot(e.astype(bf16), val) * (1.0 / total)
            lse = jnp.log2(total)
            for r in range(group):
                h = first + r
                mixed_ref[start : start + rows, h * hd : (h + 1) * hd] = mixed[r * rows : (r + 1) * rows].astype(bf16)
                lse_ref[start : start + rows, h : h + 1] = lse[r * rows : (r + 1) * rows]

    put(mixed_ref, mixed_hbm)
    put(lse_ref, lse_hbm)
    for part_ref, cols in zip((p_across, p_far, p_pair, p_own), slices):
        part_ref[...] = dot(mixed_ref[...], wo_ref[:, cols]).astype(part_ref.dtype)
    for copy in sent:
        copy.wait()


def wide(column, width):
    return jnp.concatenate([column] * (width // column.shape[1]), axis=1)


def norm_back(grad_s, normed_ref, scale_ref, inner_s, gain, part_ref, cols, width, gain_grad_ref=None):
    seq_len, step = grad_s.shape
    inverse = 1.0 / gain
    total = jnp.zeros((8, step), f32)
    for start in range(0, seq_len, ROWS):
        rows = pl.ds(start, ROWS)
        grad = grad_s[rows, :]
        unit = normed_ref[rows, cols].astype(f32) * inverse
        coef = wide(inner_s[rows, :] * (1.0 / width), step)
        part_ref[rows, :] = (wide(scale_ref[rows, :], step) * (grad * gain - unit * coef)).astype(part_ref.dtype)
        if gain_grad_ref is not None:
            total = total + jnp.sum((grad * unit).reshape(ROWS // 8, 8, step), axis=0)
    if gain_grad_ref is not None:
        gain_grad_ref[:, cols] = total


def ffn_kernel(
    info_ref, m0, m1, m2, m3, m4, m5, gain_hbm, wg_hbm, wu_hbm, wd_hbm, c0, c1, c2, c3, c4, c5, c6,
    p_across, p_far, p_pair, p_own, gfg_ref, n2_hbm, cotm_hbm, hid_hbm, dgu_hbm,
    gain_ref, wg_ref, wu_ref, wd_ref, cot_s, n2_ref, cotm_ref, hid_ref, dgu_ref,
    gate_s, up_s, gh_s, inner_s, r2_s, in_sems, out_sems,
):
    seq_len, width = n2_ref.shape
    hidden = wg_ref.shape[1]
    length, z = info_ref[0], info_ref[1]
    step = gate_s.shape[1]
    shard = width // 4
    slices = shard_slices(z, shard)
    got_gain, got_wg, got_wu, got_wd = copies(
        (gain_hbm, wg_hbm, wu_hbm, wd_hbm), (gain_ref, wg_ref, wu_ref, wd_ref), in_sems
    )

    def fetch(refs):
        return [
            pltpu.make_async_copy(
                ref.at[pl.ds(0, seq_len), :], cot_s.at[:, pl.ds(k * shard, shard)], in_sems.at[4 + k]
            )
            for k, ref in enumerate(refs)
        ]

    def start_cot(refs):
        for copy in fetch(refs):
            copy.start()

    assemble(z, (c0, c1, c2, c3, c4, c5, c6), start_cot)
    got_gain.wait()

    def normalise(refs):
        def norm(rows):
            ms = [ref[rows, :].astype(f32) for ref in refs]
            r2 = row_scale(sum(m * m for m in ms), width)
            r2_s[rows, :] = jnp.broadcast_to(r2, (ROWS, 128))
            inner_s[rows, :] = jnp.zeros((ROWS, 128), f32)
            for m, cols in zip(ms, slices):
                n2_ref[rows, cols] = (m * r2 * gain_ref[1:2, cols]).astype(bf16)

        row_loop(seq_len, ROWS, norm)

    assemble(z, (m0, m1, m1, m2, m3, m4, m5), normalise)
    for copy in fetch((c0, c1, c2, c3)) + [got_wg, got_wu, got_wd]:
        copy.wait()

    def mask(rows):
        slot = rows.start + lax.broadcasted_iota(jnp.int32, (ROWS, 1), 0)
        for k, cols in enumerate(slices):
            cot = cot_s[rows, k * shard : (k + 1) * shard].astype(f32)
            cotm_ref[rows, cols] = jnp.where(slot < length, cot, 0.0).astype(bf16)

    row_loop(seq_len, ROWS, mask)

    for j in range(0, hidden, step):
        gate_s[...] = dot(n2_ref[...], wg_ref[:, j : j + step])
        up_s[...] = dot(n2_ref[...], wu_ref[:, j : j + step])
        gh_s[...] = dot_t(cotm_ref[...], wd_ref[j : j + step, :])

        def elementwise(rows):
            gate, up, gh = gate_s[rows, :], up_s[rows, :], gh_s[rows, :]
            sig = jax.nn.sigmoid(gate)
            silu = gate * sig
            hid_ref[rows, j : j + step] = (silu * up).astype(bf16)
            dg = (gh * up * (sig * (1.0 + gate * (1.0 - sig)))).astype(bf16)
            du = (gh * silu).astype(bf16)
            dgu_ref[rows, j : j + step] = dg
            dgu_ref[rows, hidden + j : hidden + j + step] = du
            inner = jnp.sum(dg.astype(f32) * gate + du.astype(f32) * up, axis=1, keepdims=True)
            inner_s[rows, :] += jnp.broadcast_to(inner, (ROWS, 128))

        row_loop(seq_len, ROWS, elementwise)

    sent = copies(
        (n2_ref, cotm_ref, hid_ref, dgu_ref), (n2_hbm, cotm_hbm, hid_hbm, dgu_hbm), out_sems
    )
    for part_ref, cols in zip((p_across, p_far, p_pair, p_own), slices):
        gate_s[...] = dot_t(dgu_ref[:, 0:hidden], wg_ref[cols, :]) + dot_t(
            dgu_ref[:, hidden : 2 * hidden], wu_ref[cols, :]
        )
        norm_back(gate_s, n2_ref, r2_s, inner_s, gain_ref[1:2, cols], part_ref, cols, width, gfg_ref)
    for copy in sent:
        copy.wait()


def share(grads_s, core, keep_hbm, give_hbm, sems):
    return copies(
        (grads_s.at[pl.ds(core * 4, 4)], grads_s.at[pl.ds((1 - core) * 4, 4)]), (keep_hbm, give_hbm), sems
    )


def ffn_grad_kernel(
    info_ref, n2_hbm, dgu_hbm, hid_hbm, cotm_hbm, wd_hbm,
    p_across, p_far, p_pair, p_own, keep_hbm, give_hbm,
    n2_ref, dgu_ref, hid_ref, cotm_ref, wd_ref, grads_ref, in_sems, out_sems,
):
    pending = copies(
        (n2_hbm, dgu_hbm, hid_hbm, cotm_hbm, wd_hbm), (n2_ref, dgu_ref, hid_ref, cotm_ref, wd_ref), in_sems
    )
    width, hidden = n2_ref.shape[1], hid_ref.shape[1]
    upper, lower = width // 8, hidden // 8
    rest = upper - lower
    pending[0].wait()
    pending[1].wait()
    for c in range(0, 2 * hidden, 256):
        grad = t_dot(n2_ref[...], dgu_ref[:, c : c + 256])
        for d in range(8):
            grads_ref[d, :, c : c + 256] = grad[d * upper : (d + 1) * upper].astype(bf16)
    for copy in pending[2:]:
        copy.wait()
    for c in range(0, width, 256):
        grad = t_dot(hid_ref[...], cotm_ref[:, c : c + 256])
        for d in range(8):
            block = grad[d * lower : (d + 1) * lower].astype(bf16)
            if c < hidden:
                grads_ref[d, 0:lower, 2 * hidden + c : 2 * hidden + c + 256] = block
            else:
                for k in range(lower // rest):
                    col = 2 * hidden + k * 256
                    grads_ref[d, lower:upper, col : col + 256] = block[k * rest : (k + 1) * rest]
    sent = share(grads_ref, info_ref[3], keep_hbm, give_hbm, out_sems)
    for part_ref, cols in zip((p_across, p_far, p_pair, p_own), shard_slices(info_ref[1], p_own.shape[1])):
        part_ref[...] = dot(hid_ref[...], wd_ref[:, cols]).astype(bf16)
    for copy in sent:
        copy.wait()


def halves_kernel(info_ref, keep_hbm, other_hbm, to_x, to_y, keep_x, keep_y, keep_ref, other_ref, sems):
    for copy in copies((keep_hbm, other_hbm), (keep_ref, other_ref), sems):
        copy.wait()
    cols = to_x.shape[2]
    for out_ref, first, flips in ((to_x, 0, (1, 3)), (keep_x, 0, (0, 2)), (to_y, cols, (2, 3)), (keep_y, cols, (0, 1))):
        for i, flip in enumerate(flips):
            block = jnp.bitwise_xor(info_ref[2], flip)
            out_ref[i] = (
                keep_ref[block, :, first : first + cols].astype(f32) + other_ref[block, :, first : first + cols].astype(f32)
            ).astype(bf16)


def halve_kernel(info_ref, keep_x, keep_y, got_x, got_y, to_y, to_x, own_x, own_y):
    own_x[...] = (keep_x[0].astype(f32) + got_x[0].astype(f32)).astype(bf16)
    own_y[...] = (keep_y[0].astype(f32) + got_y[0].astype(f32)).astype(bf16)
    to_y[...] = (keep_x[1].astype(f32) + got_x[1].astype(f32)).astype(bf16)
    to_x[...] = (keep_y[1].astype(f32) + got_y[1].astype(f32)).astype(bf16)


def join_kernel(info_ref, own_x, own_y, from_y, from_x, left_ref, right_ref):
    left_ref[...] = (own_x[...].astype(f32) + from_y[...].astype(f32)).astype(bf16)
    right_ref[...] = (own_y[...].astype(f32) + from_x[...].astype(f32)).astype(bf16)


def unpack_ffn_kernel(info_ref, *refs):
    q, core = info_ref[2], info_ref[3]
    gate_ref, up_ref, down_ref = refs[8:]
    width, hidden = gate_ref.shape
    upper, lower = width // 8, hidden // 8
    rest = upper - lower
    cols = 3 * hidden // 2
    first = 2 * hidden - cols
    for half, (lefts, lefts_x, rights, rights_y) in ((core, refs[0:4]), (1 - core, refs[4:8])):
        for k in range(4):
            block = half * 4 + jnp.bitwise_xor(q, k)
            left, i = (lefts if k in (0, 2) else lefts_x), (0 if k in (0, 1) else 1)
            right, j = (rights if k in (0, 1) else rights_y), (0 if k in (0, 2) else 1)
            rows = pl.ds(pl.multiple_of(block * upper, upper), upper)
            gate_ref[rows, :] = left[i, :, 0:hidden].astype(f32)
            up_ref[rows, 0 : cols - hidden] = left[i, :, hidden:cols].astype(f32)
            up_ref[rows, cols - hidden : hidden] = right[j, :, 0:first].astype(f32)
            rows = pl.ds(pl.multiple_of(block * lower, lower), lower)
            down_ref[rows, 0:hidden] = right[j, 0:lower, first : first + hidden].astype(f32)
            for n in range(lower // rest):
                rows = pl.ds(pl.multiple_of(block * lower + n * rest, rest), rest)
                col = first + n * 256
                down_ref[rows, hidden:width] = right[j, lower:upper, col : col + 256].astype(f32)


def attn_backward_kernel(
    info_ref, g0, g1, g2, g3, g4, g5, qg_ref, kg_ref, wo_hbm, qrot_hbm, krot_hbm, val_hbm, mixed_hbm, lse_hbm,
    cos_hbm, sin_hbm, qpre_hbm, kpre_hbm, n1_hbm, wq_hbm, wk_hbm, wv_hbm, r1_hbm, gain_hbm,
    p_across, p_far, p_pair, p_own, gag_ref, qgg_ref, kgg_ref, keep_hbm, give_hbm,
    wo_ref, qrot_ref, krot_ref, val_ref, mixed_ref, lse_ref, cos_ref, sin_ref, qpre_ref, kpre_ref, n1_ref,
    wq_ref, wk_ref, wv_ref, r1_ref, gain_ref,
    ga_ref, gm_s, dq_s, dk_s, dv_s, dqkv_ref, inner_ref, acc_s, grads_ref, sems, out_sems,
):
    seq_len, width = ga_ref.shape
    hd = qg_ref.shape[1]
    qw, kw = qpre_ref.shape[1], kpre_ref.shape[1]
    heads, kvs = qw // hd, kw // hd
    group = heads // kvs
    length, z = info_ref[0], info_ref[1]
    scale = hd ** (-0.5)
    slices = shard_slices(z, width // 4)
    pending = copies(
        (
            wo_hbm, qrot_hbm, krot_hbm, val_hbm, mixed_hbm, lse_hbm, cos_hbm, sin_hbm, qpre_hbm, kpre_hbm, n1_hbm,
            wq_hbm, wk_hbm, wv_hbm, r1_hbm, gain_hbm,
        ),
        (
            wo_ref, qrot_ref, krot_ref, val_ref, mixed_ref, lse_ref, cos_ref, sin_ref, qpre_ref, kpre_ref, n1_ref,
            wq_ref, wk_ref, wv_ref, r1_ref, gain_ref,
        ),
        sems,
    )

    def collect(refs):
        for ref, cols in zip(refs, slices):
            ga_ref[:, cols] = ref[...]

    assemble(z, (g0, g1, g1, g2, g3, g4, g5), collect)

    pending[0].wait()
    for c in range(0, qw, 256):
        gm_s[:, c : c + 256] = dot_t(ga_ref[...], wo_ref[c : c + 256, :]).astype(bf16)
    dk_s[...] = jnp.zeros_like(dk_s)
    dv_s[...] = jnp.zeros_like(dv_s)
    for copy in pending[1:6]:
        copy.wait()

    for start, rows, keys in query_units(seq_len):
        bias = key_bias(length, keys)
        for g in range(kvs):
            first = g * group
            cols = slice(g * hd, (g + 1) * hd)
            key, val = krot_ref[0:keys, cols], val_ref[0:keys, cols]

            def stacked(ref):
                return jnp.concatenate(
                    [ref[start : start + rows, h * hd : (h + 1) * hd] for h in range(first, first + group)], axis=0
                )

            q, gm, mixed = stacked(qrot_ref), stacked(gm_s), stacked(mixed_ref)
            lse = jnp.concatenate(
                [lse_ref[start : start + rows, h : h + 1] for h in range(first, first + group)], axis=0
            )
            p = jnp.exp2(dot_t(q, key) * (scale * LOG2E) + bias - lse)
            delta = jnp.sum(gm.astype(f32) * mixed.astype(f32), axis=1, keepdims=True)
            ds = (p * (dot_t(gm, val) - delta)).astype(bf16)
            dv_s[0:keys, cols] += t_dot(p.astype(bf16), gm)
            dk_s[0:keys, cols] += t_dot(ds, q)
            dq = dot(ds, key)
            for r in range(group):
                h = first + r
                dq_s[start : start + rows, h * hd : (h + 1) * hd] = dq[r * rows : (r + 1) * rows]

    for copy in pending[6:]:
        copy.wait()
    ones = jnp.full((hd, hd), 1.0 / hd, bf16)

    def unrotate(rows, rot_s, pre_ref, g_ref, count, base, gain_sum):
        cos, sin = cos_ref[rows, :], sin_ref[rows, :]
        inner = jnp.zeros((ROWS, hd), f32)
        for c in range(0, count, hd):
            g = rot_s[rows, c : c + hd] * scale
            u = g * cos + pltpu.roll(g * sin, hd // 2, 1)
            v = pre_ref[rows, c : c + hd]
            r = lax.rsqrt(dot((v * v).astype(bf16), ones) + NORM_EPSILON)
            unit = v * r
            t = u * unit
            gain_sum = gain_sum + jnp.sum(t.reshape(ROWS // 8, 8, hd), axis=0)
            mean = dot((t * g_ref[...]).astype(bf16), ones)
            dqkv_ref[rows, base + c : base + c + hd] = (r * (u * g_ref[...] - unit * mean)).astype(bf16)
            inner = inner + (hd * NORM_EPSILON) * (r * r * mean)
        return inner, gain_sum

    qgs = kgs = jnp.zeros((8, hd), f32)
    for start in range(0, seq_len, ROWS):
        rows = pl.ds(start, ROWS)
        qi, qgs = unrotate(rows, dq_s, qpre_ref, qg_ref, qw, 0, qgs)
        ki, kgs = unrotate(rows, dk_s, kpre_ref, kg_ref, kw, qw, kgs)
        dv = dv_s[rows, :].astype(bf16)
        dqkv_ref[rows, qw + kw : qw + 2 * kw] = dv
        vi = jnp.sum(dv.astype(f32) * val_ref[rows, :].astype(f32), axis=1, keepdims=True)
        inner_ref[rows, :] = qi + ki + vi
    qgg_ref[...] = qgs
    kgg_ref[...] = kgs

    upper, lower = width // 8, qw // 8
    for c in range(0, width, 256):
        grad = t_dot(n1_ref[...], dqkv_ref[:, c : c + 256])
        out = t_dot(mixed_ref[...], ga_ref[:, c : c + 256])
        for d in range(8):
            grads_ref[d, 0:upper, c : c + 256] = grad[d * upper : (d + 1) * upper].astype(bf16)
            grads_ref[d, upper : upper + lower, c : c + 256] = out[d * lower : (d + 1) * lower].astype(bf16)
    sent = share(grads_ref, info_ref[3], keep_hbm, give_hbm, out_sems)
    for part_ref, cols in zip((p_across, p_far, p_pair, p_own), slices):
        acc_s[...] = (
            dot_t(dqkv_ref[:, 0:qw], wq_ref[cols, :])
            + dot_t(dqkv_ref[:, qw : qw + kw], wk_ref[cols, :])
            + dot_t(dqkv_ref[:, qw + kw : qw + 2 * kw], wv_ref[cols, :])
        )
        norm_back(acc_s, n1_ref, r1_ref, inner_ref, gain_ref[0:1, cols], part_ref, cols, width, gag_ref)
    for copy in sent:
        copy.wait()


def output_kernel(info_ref, middle_ref, attn_ref, own_ref, pair_ref, across_ref, out_ref, sums_ref):
    seq_len, shard = middle_ref.shape
    length = info_ref[0]
    sums = [jnp.zeros((8, shard), f32)] * 3
    for start in range(0, seq_len, ROWS):
        rows = pl.ds(start, ROWS)
        ffn = own_ref[rows, :].astype(f32) + (pair_ref[rows, :].astype(f32) + across_ref[rows, :].astype(f32))
        out = middle_ref[rows, :] + ffn
        out_ref[rows, :] = out.astype(bf16)
        slot = start + lax.broadcasted_iota(jnp.int32, (ROWS, 1), 0)
        for i, v in enumerate((out, attn_ref[rows, :], ffn)):
            v = jnp.where(slot < length, v, 0.0)
            sums[i] = sums[i] + jnp.sum((v * v).reshape(ROWS // 8, 8, shard), axis=0)
    for i in range(3):
        sums_ref[i : i + 1, :] = jnp.sum(sums[i], axis=0, keepdims=True)


def small_kernel(info_ref, gag_ref, gfg_ref, qgg_ref, kgg_ref, sums_ref, small_ref):
    hd, shard = qgg_ref.shape[1], sums_ref.shape[1]
    small_ref[...] = jnp.zeros(small_ref.shape, f32)
    small_ref[0:1, :] = jnp.sum(gag_ref[...], axis=0, keepdims=True)
    small_ref[1:2, :] = jnp.sum(gfg_ref[...], axis=0, keepdims=True)
    small_ref[2:3, 0:hd] = jnp.sum(qgg_ref[...], axis=0, keepdims=True)
    small_ref[2:3, hd : 2 * hd] = jnp.sum(kgg_ref[...], axis=0, keepdims=True)
    lane = lax.broadcasted_iota(jnp.int32, (1, 128), 1)
    totals = (info_ref[0] * shard).astype(f32) * (lane == 3).astype(f32)
    for i in range(3):
        totals = totals + jnp.sum(sums_ref[i : i + 1, :], axis=1, keepdims=True) * (lane == i).astype(f32)
    small_ref[2:3, 2 * hd : 2 * hd + 128] = totals


def block_kernel(info_ref, own_x, own_y, from_y, from_x, small_ref, left_ref, right_ref):
    rows, cols = own_x.shape
    small = small_ref[...]
    high = small.astype(bf16)
    tail = jnp.concatenate([high, (small - high.astype(f32)).astype(bf16)], axis=0)
    for a, b, out_ref, first in ((own_x, from_y, left_ref, 0), (own_y, from_x, right_ref, cols)):
        out_ref[0:rows, :] = (a[...].astype(f32) + b[...].astype(f32)).astype(bf16)
        out_ref[rows : rows + TAIL, :] = tail[:, first : first + cols]


def unpack_kernel(info_ref, *refs):
    q, core = info_ref[2], info_ref[3]
    gq_ref, gk_ref, gv_ref, go_ref, ag_ref, fg_ref, qg_ref, kg_ref, rms_ref, small_ref = refs[8:]
    cols, kw = gq_ref.shape[1], gk_ref.shape[1]
    upper, lower = gq_ref.shape[0] // 8, go_ref.shape[0] // 8
    for half, (lefts, lefts_x, rights, rights_y) in ((core, refs[0:4]), (1 - core, refs[4:8])):
        for k in range(4):
            block = half * 4 + jnp.bitwise_xor(q, k)
            left, i = (lefts if k in (0, 2) else lefts_x), (0 if k in (0, 1) else 1)
            right, j = (rights if k in (0, 1) else rights_y), (0 if k in (0, 2) else 1)
            rows = pl.ds(pl.multiple_of(block * upper, upper), upper)
            gq_ref[rows, :] = left[i, 0:upper, :].astype(f32)
            gk_ref[rows, :] = right[j, 0:upper, 0:kw].astype(f32)
            gv_ref[rows, :] = right[j, 0:upper, kw : 2 * kw].astype(f32)
            rows = pl.ds(pl.multiple_of(block * lower, lower), lower)
            go_ref[rows, 0:cols] = left[i, upper : upper + lower, :].astype(f32)
            go_ref[rows, cols : 2 * cols] = right[j, upper : upper + lower, :].astype(f32)
    for first, group in ((0, (0, 1, 4, 5)), (cols, (2, 3, 6, 7))):
        total = jnp.zeros((8, cols), f32)
        for n in group:
            for i in range(2):
                tail = refs[n][i, upper + lower : upper + lower + TAIL, :].astype(f32)
                total = total + (tail[0:8] + tail[8:16])
        small_ref[:, first : first + cols] = total
    shard, hd = ag_ref.shape[1], qg_ref.shape[1]
    mine = pl.ds(pl.multiple_of(info_ref[1] * shard, shard), shard)
    ag_ref[...] = small_ref[0:1, mine]
    fg_ref[...] = small_ref[1:2, mine]
    qg_ref[...] = small_ref[2:3, 0:hd]
    kg_ref[...] = small_ref[2:3, hd : 2 * hd]
    totals = small_ref[2:3, 2 * hd : 2 * hd + 128]
    lane = lax.broadcasted_iota(jnp.int32, (1, 128), 1)
    count = jnp.sum(jnp.where(lane == 3, totals, 0.0), axis=1, keepdims=True)
    rms_ref[...] = jnp.sqrt(totals / count)


SPECS = {
    "s": pl.BlockSpec(memory_space=pltpu.SMEM),
    "v": pl.BlockSpec(memory_space=pltpu.VMEM),
    "a": pl.BlockSpec(memory_space=pl.ANY),
}


def call(body, outs, args, scratch=(), sems=(), flops=0, bytes_accessed=0, limit=SMALL_BYTES):
    places, arrays = [], []
    for place, *group in args:
        places += [place] * len(group)
        arrays += group
    return pl.pallas_call(
        body,
        out_shape=[jax.ShapeDtypeStruct(s, d) for s, d, _ in outs],
        in_specs=[SPECS[p] for p in places],
        out_specs=[SPECS[p] for _, _, p in outs],
        scratch_shapes=[pltpu.VMEM(s, d) for s, d in scratch] + [pltpu.SemaphoreType.DMA((n,)) for n in sems],
        compiler_params=pltpu.CompilerParams(vmem_limit_bytes=limit),
        cost_estimate=pl.CostEstimate(flops=flops, bytes_accessed=bytes_accessed, transcendentals=0),
    )(*arrays)


PAIRS = ((0, 1), (1, 0), (2, 3), (3, 2))
MIDDLE = ((1, 2), (2, 1))
OUTWARD = ((1, 0), (2, 3))
INWARD = ((0, 1), (3, 2))
OUTWARD_TWO = ((2, 0), (1, 3))
INWARD_TWO = ((0, 2), (3, 1))


def send(rows, pairs):
    return lax.ppermute(rows, "tensor", pairs)


def hold(*values):
    return lax.optimization_barrier(values)


def gather_line(own):
    pair = send(own, PAIRS)
    across_mid = send(own, MIDDLE)
    far_end = send(pair, OUTWARD_TWO)
    far_mid = send(pair, MIDDLE)
    across_end = send(across_mid, OUTWARD)
    return own, pair, across_mid, across_end, far_mid, far_end


def pick(end, from_end, from_middle):
    return jnp.where(end, from_end, from_middle)


def scatter_first(parts):
    across, far, _, _ = parts
    return send(far, INWARD_TWO), send(far, MIDDLE), send(across, INWARD)


def scatter_last(parts, first):
    across, _, pair, own = parts
    two, three, one = first
    to_pair = (pair.astype(f32) + (two.astype(f32) + three.astype(f32))).astype(bf16)
    to_across = (across.astype(f32) + one.astype(f32)).astype(bf16)
    return own, send(to_pair, PAIRS), send(to_across, MIDDLE)


def add(a, b):
    return (a.astype(f32) + b.astype(f32)).astype(bf16)


def total(terms):
    own, pair, across = terms
    return own.astype(f32) + (pair.astype(f32) + across.astype(f32))


def split_rows(values):
    high = lax.optimization_barrier(values.astype(bf16))
    low = (values - high.astype(f32)).astype(bf16)
    return jnp.concatenate([high, low], axis=0)


def swap(values, bit):
    return lax.ppermute(values, "dp", [(i, i ^ bit) for i in range(8)])


def halve(keep, other, info):
    _, rows, width = keep.shape
    return call(
        halves_kernel,
        [((2, rows, width // 2), bf16, "v")] * 4,
        (("s", info), ("a", keep, other)),
        scratch=[((4, rows, width), bf16)] * 2,
        sems=(2,),
    )


def halve_again(keep_x, keep_y, got_x, got_y, info):
    return call(
        halve_kernel, [(keep_x.shape[1:], bf16, "v")] * 4, (("s", info), ("v", keep_x, keep_y, got_x, got_y))
    )


def per_device(
    hidden_in, lengths, w_query, w_key, w_value, w_out, attn_gain, ffn_gain,
    query_gain, key_gain, w_gate, w_up, w_down, cotangent,
):
    seq_len, shard = hidden_in.shape
    width = w_query.shape[0]
    hd = query_gain.shape[0]
    qw, kw = w_query.shape[1], w_key.shape[1]
    hidden = w_gate.shape[1]
    padded = -(-seq_len // BLOCK) * BLOCK
    z = lax.axis_index("tensor").astype(jnp.int32)
    dp = lax.axis_index("dp").astype(jnp.int32)
    chips = lax.axis_size("dp") == 8
    q, core = (dp // 2, dp % 2) if chips else (0 * dp, 0 * dp)
    info = jnp.stack([lengths[0], z, q, core])
    parts = [((seq_len, shard), bf16, "v")] * 4

    end = (z == 0) | (z == 3)
    gains = jnp.concatenate([attn_gain[None], ffn_gain[None], jnp.zeros((6, shard), f32)], axis=0)
    x = jnp.concatenate([hidden_in, split_rows(gains)], axis=0)
    cot = jnp.concatenate([cotangent, jnp.zeros((TAIL, shard), bf16)], axis=0)
    x_pair, x_mid = send(x, PAIRS), send(x, MIDDLE)
    x_pair, x_mid, cot = hold(x_pair, x_mid, cot)
    x_end, x_far = send(pick(end, cot, x_mid), PAIRS), send(x_pair, MIDDLE)
    x_end, x_far, cot = hold(x_end, x_far, cot)
    x_last, cot_far = send(x_far, OUTWARD), send(x_end, MIDDLE)
    x_last, cot_far, x_end, cot = hold(x_last, cot_far, x_end, cot)
    cot_mid, cot_pair, cot_last = send(cot, MIDDLE), send(cot, OUTWARD), send(cot_far, OUTWARD)
    cos, sin = rope_tables(seq_len, hd)
    qg, kg = query_gain[None], key_gain[None]
    resid = hidden_in.astype(f32)
    valid = (jnp.arange(seq_len, dtype=jnp.int32) < lengths[0]).astype(f32)[:, None]

    saved = [
        ((seq_len, width), bf16), ((seq_len, qw), f32), ((seq_len, kw), f32), ((seq_len, qw), bf16),
        ((padded, kw), bf16), ((padded, kw), bf16), ((seq_len, qw), bf16), ((seq_len, 128), f32),
        ((seq_len, 128), f32), ((8, width), f32),
    ]
    weights = [((width, kw), bf16), ((width, kw), bf16), ((width, qw), bf16), ((qw, width), bf16)]
    tables = [((seq_len, hd), f32)] * 2
    *attn_parts, n1, qpre, kpre, qrot, krot, val, mixed, lse, r1, gain = call(
        attn_forward_kernel,
        parts + [(s, d, "a") for s, d in saved],
        (
            ("s", info), ("v", x, x_pair, x_mid, x_end, x_far, x_last, qg, kg),
            ("a", w_key, cos, sin, w_value, w_query, w_out),
        ),
        scratch=weights[:1] + tables + weights[1:] + saved,
        sems=(6, 10),
        limit=FULL_BYTES,
        flops=2 * seq_len * width * (2 * qw + 2 * kw) + 4 * seq_len * seq_len * qw,
        bytes_accessed=14_000_000,
    )
    attn_parts, cot_mid, cot_pair, cot_last = hold(attn_parts, cot_mid, cot_pair, cot_last)
    across, far, pair, own = attn_parts
    two = send(far, INWARD_TWO)
    one, three = hold(pick(end, across, cot_mid[:seq_len]), far)
    three, one = send(three, MIDDLE), send(one, PAIRS)
    zero_end = pick(end, jnp.zeros_like(one), one)
    pair = lax.optimization_barrier(pair.astype(f32) + two.astype(f32))
    attn_local = total(scatter_last((across, far, pair, own), (jnp.zeros_like(two), three, zero_end)))
    middle = resid + attn_local
    shard_two, one = hold(middle.astype(bf16), one)
    m_parts = gather_line(shard_two)

    kept = [((seq_len, width), bf16), ((seq_len, width), bf16), ((seq_len, hidden), bf16), ((seq_len, 2 * hidden), bf16)]
    *ffn_parts, gfg, n2, cotm, hid, dgu = call(
        ffn_kernel,
        parts + [((8, width), f32, "v")] + [(s, d, "a") for s, d in kept],
        (
            ("s", info), ("v", *m_parts), ("a", gain, w_gate, w_up, w_down),
            ("a", cot, x_end, cot_pair, cot_mid, one, cot_far, cot_last),
        ),
        scratch=[((8, width), f32)] + [((width, hidden), bf16)] * 2 + [((hidden, width), bf16), ((seq_len, width), bf16)]
        + kept + [((seq_len, 256), f32)] * 3 + [((seq_len, 128), f32)] * 2,
        sems=(8, 4),
        limit=VMEM_BYTES,
        flops=2 * seq_len * width * hidden * 5,
        bytes_accessed=16_000_000,
    )
    grad_top = cotangent.astype(f32) * valid
    first = scatter_first(ffn_parts)
    blocks = ((4, width // 8, 3 * hidden), bf16, "a")
    *down_parts, ffn_keep, ffn_give = call(
        ffn_grad_kernel,
        parts + [blocks] * 2,
        (("s", info), ("a", n2, dgu, hid, cotm, w_down)),
        scratch=[kept[0], kept[3], kept[2], kept[1], ((hidden, width), bf16), ((8, width // 8, 3 * hidden), bf16)],
        sems=(5, 2),
        limit=VMEM_BYTES,
        flops=2 * seq_len * width * hidden * 4,
        bytes_accessed=14_000_000,
    )
    first, ffn_keep, ffn_give = hold(first, ffn_keep, ffn_give)
    back = scatter_last(ffn_parts, first)
    if chips:
        ffn_other = swap(ffn_give, 1)
        cols = (width // 8, 3 * hidden // 2)
        to_x, to_y, keep_x, keep_y = halve(ffn_keep, ffn_other, info)
        back, to_x, to_y, keep_x, keep_y = hold(back, to_x, to_y, keep_x, keep_y)
    grad_middle = grad_top + total(back)
    ga = grad_middle.astype(bf16)
    across, far, pair, own = down_parts
    ga_pair, ga_mid = send(ga, PAIRS), send(ga, MIDDLE)
    if chips:
        got_x, got_y = swap(to_x, 2), swap(to_y, 4)
        ga_pair, ga_mid, far, got_x, got_y = hold(ga_pair, ga_mid, far, got_x, got_y)
        to_y, to_x, own_x, own_y = halve_again(keep_x, keep_y, got_x, got_y, info)
        from_y, from_x = swap(to_y, 4), swap(to_x, 2)
    ga_end, ga_far = send(pick(end, far, ga_mid), PAIRS), send(ga_pair, MIDDLE)
    if chips:
        ga_end, ga_far, across, from_y, from_x = hold(ga_end, ga_far, across, from_y, from_x)
        left, right = call(
            join_kernel, [(cols, bf16, "v")] * 2, (("s", info), ("v", own_x, own_y, from_y, from_x))
        )
        left_y, right_x = swap(left, 4), swap(right, 2)
    ga_last = send(pick(end, across, ga_far), PAIRS)
    got_far = send(add(far, ga_end), MIDDLE)
    if chips:
        ga_last, got_far, left_y, right_x = hold(ga_last, got_far, left_y, right_x)
        lefts, rights = jnp.stack([left, left_y]), jnp.stack([right, right_x])
        lefts_x, rights_y = swap(lefts, 2), swap(rights, 4)
    ga_parts = (ga, ga_pair, ga_mid, ga_end, ga_far, ga_last)
    ffn_terms = (own, send(add(pair, got_far), PAIRS), send(add(across, ga_last), MIDDLE))

    blocks = (4, (width + qw) // 8, width)
    *back_parts, gag, qgg, kgg, keep, give = call(
        attn_backward_kernel,
        parts + [((8, width), f32, "v"), ((8, hd), f32, "v"), ((8, hd), f32, "v"), (blocks, bf16, "a"), (blocks, bf16, "a")],
        (
            ("s", info), ("v", *ga_parts, qg, kg),
            ("a", w_out, qrot, krot, val, mixed, lse, cos, sin, qpre, kpre, n1, w_query, w_key, w_value, r1, gain),
        ),
        scratch=[weights[3], saved[3], saved[4], saved[5], saved[6], saved[7], *tables, saved[1], saved[2], saved[0]]
        + [weights[2], weights[0], weights[1], saved[8], saved[9]]
        + [((seq_len, width), bf16), ((seq_len, qw), bf16), ((seq_len, qw), f32), ((padded, kw), f32), ((padded, kw), f32)]
        + [((seq_len, qw + 2 * kw), bf16), ((seq_len, 128), f32), ((seq_len, shard), f32), ((8, *blocks[1:]), bf16)],
        sems=(16, 2),
        limit=VMEM_BYTES,
        flops=2 * seq_len * width * (4 * qw + 4 * kw) + 10 * seq_len * seq_len * qw,
        bytes_accessed=20_000_000,
    )
    across, far, pair, own = back_parts
    if chips:
        far, ffn_terms, keep, give, lefts_x, rights_y = hold(far, ffn_terms, keep, give, lefts_x, rights_y)
        other = swap(give, 1)
    out_rows, sums = call(
        output_kernel,
        [((seq_len, shard), bf16, "v"), ((8, shard), f32, "v")],
        (("s", info), ("v", middle, attn_local, *ffn_terms)),
        bytes_accessed=2_000_000,
    )
    small = call(small_kernel, [((8, width), f32, "v")], (("s", info), ("v", gag, gfg, qgg, kgg, sums)))[0]
    shapes = [(width, qw), (width, kw), (width, kw), (qw, width)]
    if chips:
        other, small = hold(other, small)
        to_x, to_y, keep_x, keep_y = halve(keep, other, info)
        got_x, got_y = swap(to_x, 2), swap(to_y, 4)
        small = small + send(small, PAIRS)
        small = small + send(small, ((0, 2), (2, 0), (1, 3), (3, 1)))
        got_x, got_y, small, far, across = hold(got_x, got_y, small, far, across)
        to_y, to_x, own_x, own_y = halve_again(keep_x, keep_y, got_x, got_y, info)
        from_y, from_x, two = hold(swap(to_y, 4), swap(to_x, 2), send(far, INWARD_TWO))
        late_left, late_right = call(
            block_kernel,
            [((own_x.shape[0] + TAIL, own_x.shape[1]), bf16, "v")] * 2,
            (("s", info), ("v", own_x, own_y, from_y, from_x, small)),
        )
        late_left, late_right, far, across = hold(late_left, late_right, far, across)
        three, one = send(far, MIDDLE), send(across, INWARD)
        left_y, right_x, three, one = hold(swap(late_left, 4), swap(late_right, 2), three, one)
        late_lefts, late_rights = jnp.stack([late_left, left_y]), jnp.stack([late_right, right_x])
        back_terms = scatter_last((across, far, pair, own), (two, three, one))
        ffn_halves = (lefts, lefts_x, rights, rights_y)
        g_gate, g_up, g_down = call(
            unpack_ffn_kernel,
            [(s, f32, "v") for s in ((width, hidden), (width, hidden), (hidden, width))],
            (("s", info), ("v", *ffn_halves, *[swap(b, 1) for b in ffn_halves])),
            bytes_accessed=14_000_000,
        )
        late = (late_lefts, swap(late_lefts, 2), late_rights, swap(late_rights, 4))
        late, back_terms, g_gate, g_up, g_down = hold(late, back_terms, g_gate, g_up, g_down)
        everyone = [*late, *[swap(b, 1) for b in late]]
        gq, gk, gv, go, ag, fg, qgg, kgg, rms = call(
            unpack_kernel,
            [(s, f32, "v") for s in shapes + [(1, shard), (1, shard), (1, hd), (1, hd), (1, 128)]],
            (("s", info), ("v", *everyone)),
            scratch=[((8, width), f32)],
            bytes_accessed=9_000_000,
        )
    else:
        back_terms = scatter_last(back_parts, scatter_first(back_parts))
        grads, ffn_grads = lax.psum((jnp.concatenate([keep, give]), jnp.concatenate([ffn_keep, ffn_give])), "dp")
        small = lax.psum(small, ("dp", "tensor"))
        ag, fg = [lax.dynamic_slice(small, (i, z * shard), (1, shard)) for i in (0, 1)]
        qgg, kgg = small[2:3, :hd], small[2:3, hd : 2 * hd]
        totals = small[2:3, 2 * hd : 2 * hd + 4]
        rms = jnp.sqrt(totals / totals[:, 3:])
        g_qkv = grads[:, : width // 8].reshape(width, width).astype(f32)
        gq, gk, gv = g_qkv[:, :qw], g_qkv[:, qw : qw + kw], g_qkv[:, qw + kw :]
        go = grads[:, width // 8 :].reshape(qw, width).astype(f32)
        g_gate = ffn_grads[:, :, :hidden].reshape(width, hidden).astype(f32)
        g_up = ffn_grads[:, :, hidden : 2 * hidden].reshape(width, hidden).astype(f32)
        folded = ffn_grads[:, :, 2 * hidden :]
        lower = hidden // 8
        tail = folded[:, lower:].reshape(8, width // 8 - lower, -1, 256).transpose(0, 2, 1, 3).reshape(8, lower, 256)
        g_down = jnp.concatenate([folded[:, :lower], tail], axis=2).reshape(hidden, width).astype(f32)
    input_grad = (grad_middle + total(back_terms)).astype(bf16)
    return (
        out_rows,
        input_grad,
        gq,
        gk,
        gv,
        go,
        ag[0],
        fg[0],
        qgg[0],
        kgg[0],
        g_gate,
        g_up,
        g_down,
        rms[0, :3],
    )


def solution(mesh):
    rows, cols, first = P("dp", "tensor"), P(None, "tensor"), P("tensor", None)
    gain = P("tensor")
    return jax.shard_map(
        per_device,
        mesh=mesh,
        in_specs=(rows, P("dp"), cols, cols, cols, first, gain, gain, P(), P(), cols, cols, first, rows),
        out_specs=(rows, rows, cols, cols, cols, first, gain, gain, P(), P(), cols, cols, first, P()),
        check_vma=False,
    )
```

```python
import functools

import jax
import jax.numpy as jnp
from jax import lax
from jax.experimental import pallas as pl
from jax.experimental.pallas import tpu as pltpu
from jax.sharding import PartitionSpec as P

BLOCK = 256
NORM_EPSILON = 1e-06
ROPE_THETA = 1000000.0
LOG2E = 1.4426950408889634
NEG = -1e30
ROWS = 64
TAIL = 16
FULL_BYTES = 60 * 1024 * 1024
VMEM_BYTES = 40 * 1024 * 1024
SMALL_BYTES = 24 * 1024 * 1024

bf16 = jnp.bfloat16
f32 = jnp.float32


def dot(a, b):
    return jnp.dot(a, b, preferred_element_type=f32)


def dot_t(a, b):
    return lax.dot_general(a, b, (((1,), (1,)), ((), ())), preferred_element_type=f32)


def t_dot(a, b):
    return lax.dot_general(a, b, (((0,), (0,)), ((), ())), preferred_element_type=f32)


def row_loop(count, step, body):
    for start in range(0, count, step):
        body(pl.ds(start, step))


def rope_tables(length, width):
    half_width = width // 2
    frequency = ROPE_THETA ** (-(jnp.arange(half_width, dtype=f32) * (2.0 / width)))
    angles = jnp.arange(length, dtype=f32)[:, None] * frequency[None, :]
    cos, sin = jnp.cos(angles), jnp.sin(angles)
    return jnp.concatenate([cos, cos], axis=1), jnp.concatenate([-sin, sin], axis=1)


def query_units(seq_len):
    units = []
    start = 0
    while start < seq_len:
        rows = min(128, seq_len - start)
        keys = (start // BLOCK + 1) * BLOCK
        units.append((start, rows, keys))
        start += rows
    return units


def roles(z):
    low = z < 2
    return jnp.where(low, 2, 1), jnp.where(low, 3, 0), z + 1 - 2 * lax.rem(z, 2), z


def shard_slices(z, width):
    return [pl.ds(pl.multiple_of(shard * width, width), width) for shard in roles(z)]


def assemble(z, pieces, body):
    own, pair_mid, pair_end, across_mid, across_end, far_mid, far_end = pieces
    end = (z == 0) | (z == 3)

    @pl.when(end)
    def _():
        body((across_end, far_end, pair_end, own))

    @pl.when(jnp.logical_not(end))
    def _():
        body((across_mid, far_mid, pair_mid, own))


def key_bias(length, keys):
    slot = lax.broadcasted_iota(jnp.int32, (1, keys), 1)
    return jnp.where(slot < length, 0.0, NEG).astype(f32)


def row_scale(squares, width):
    return lax.rsqrt(jnp.sum(squares, axis=1, keepdims=True) * (1.0 / width) + NORM_EPSILON)


def pack_kernel(info_ref, x_ref, ag_ref, fg_ref, out_ref):
    seq_len, shard = x_ref.shape
    out_ref[0:seq_len, :] = x_ref[...]
    gains = jnp.concatenate([ag_ref[...], fg_ref[...], jnp.zeros((6, shard), f32)], axis=0)
    high = gains.astype(bf16)
    out_ref[seq_len : seq_len + TAIL, :] = jnp.concatenate([high, (gains - high.astype(f32)).astype(bf16)], axis=0)


def copies(sources, targets, sems):
    pending = [pltpu.make_async_copy(a, b, sems.at[i]) for i, (a, b) in enumerate(zip(sources, targets))]
    for copy in pending:
        copy.start()
    return pending


def attn_forward_kernel(
    info_ref, x0, x1, x2, x3, x4, x5, qg_ref, kg_ref, wk_hbm, cos_hbm, sin_hbm, wv_hbm, wq_hbm, wo_hbm,
    p_across, p_far, p_pair, p_own, n1_hbm, qpre_hbm, kpre_hbm, qrot_hbm, krot_hbm, val_hbm, mixed_hbm, lse_hbm,
    r1_hbm, gain_hbm,
    wk_ref, cos_ref, sin_ref, wv_ref, wq_ref, wo_ref, n1_ref, qpre_ref, kpre_ref, qrot_ref, krot_ref, val_ref,
    mixed_ref, lse_ref, r1_ref, gain_ref, in_sems, out_sems,
):
    seq_len, width = n1_ref.shape
    hd = qg_ref.shape[1]
    heads = wq_ref.shape[1] // hd
    kvs = wk_ref.shape[1] // hd
    group = heads // kvs
    padded = krot_ref.shape[0]
    length, z = info_ref[0], info_ref[1]
    scale = hd ** (-0.5) * LOG2E
    slices = shard_slices(z, width // 4)
    pending = copies(
        (wk_hbm, cos_hbm, sin_hbm, wv_hbm, wq_hbm, wo_hbm), (wk_ref, cos_ref, sin_ref, wv_ref, wq_ref, wo_ref), in_sems
    )
    sent = []

    def put(source, target):
        copy = pltpu.make_async_copy(source, target, out_sems.at[len(sent)])
        copy.start()
        sent.append(copy)

    def normalise(refs):
        for ref, cols in zip(refs, slices):
            tail = ref[seq_len : seq_len + TAIL, :].astype(f32)
            gain_ref[:, cols] = tail[0:8] + tail[8:16]

        def norm(rows):
            xs = [ref[rows, :].astype(f32) for ref in refs]
            r1 = row_scale(sum(x * x for x in xs), width)
            r1_ref[rows, :] = jnp.broadcast_to(r1, (ROWS, 128))
            for x, cols in zip(xs, slices):
                n1_ref[rows, cols] = (x * r1 * gain_ref[0:1, cols]).astype(bf16)

        row_loop(seq_len, ROWS, norm)

    assemble(z, (x0, x1, x1, x2, x3, x4, x5), normalise)
    put(n1_ref, n1_hbm)
    put(r1_ref, r1_hbm)
    put(gain_ref, gain_hbm)

    def project(w_ref, pre_ref, rot_ref, g_ref):
        count = w_ref.shape[1]
        for c in range(0, count, 2 * hd):
            pre_ref[:, c : c + 2 * hd] = dot(n1_ref[...], w_ref[:, c : c + 2 * hd])

        def rotate(rows):
            cos, sin = cos_ref[rows, :], sin_ref[rows, :]
            for c in range(0, count, hd):
                v = pre_ref[rows, c : c + hd]
                v = v * row_scale(v * v, hd) * g_ref[...]
                rot_ref[rows, c : c + hd] = (v * cos + pltpu.roll(v, hd // 2, 1) * sin).astype(bf16)

        row_loop(seq_len, ROWS, rotate)

    for copy in pending:
        copy.wait()
    project(wk_ref, kpre_ref, krot_ref, kg_ref)
    val_ref[0:seq_len, :] = dot(n1_ref[...], wv_ref[...]).astype(bf16)
    if padded > seq_len:
        krot_ref[seq_len:padded, :] = jnp.zeros((padded - seq_len, kvs * hd), bf16)
        val_ref[seq_len:padded, :] = jnp.zeros((padded - seq_len, kvs * hd), bf16)
    put(kpre_ref, kpre_hbm)
    put(krot_ref, krot_hbm)
    put(val_ref, val_hbm)
    project(wq_ref, qpre_ref, qrot_ref, qg_ref)
    put(qpre_ref, qpre_hbm)
    put(qrot_ref, qrot_hbm)

    for start, rows, keys in query_units(seq_len):
        bias = key_bias(length, keys)
        for g in range(kvs):
            key = krot_ref[0:keys, g * hd : (g + 1) * hd]
            val = val_ref[0:keys, g * hd : (g + 1) * hd]
            first = g * group
            q = jnp.concatenate(
                [qrot_ref[start : start + rows, h * hd : (h + 1) * hd] for h in range(first, first + group)], axis=0
            )
            e = jnp.exp2(dot_t(q, key) * scale + bias)
            total = jnp.sum(e, axis=1, keepdims=True)
            mixed = dot(e.astype(bf16), val) * (1.0 / total)
            lse = jnp.log2(total)
            for r in range(group):
                h = first + r
                mixed_ref[start : start + rows, h * hd : (h + 1) * hd] = mixed[r * rows : (r + 1) * rows].astype(bf16)
                lse_ref[start : start + rows, h : h + 1] = lse[r * rows : (r + 1) * rows]

    put(mixed_ref, mixed_hbm)
    put(lse_ref, lse_hbm)
    for part_ref, cols in zip((p_across, p_far, p_pair, p_own), slices):
        part_ref[...] = dot(mixed_ref[...], wo_ref[:, cols]).astype(part_ref.dtype)
    for copy in sent:
        copy.wait()


def wide(column, width):
    return jnp.concatenate([column] * (width // column.shape[1]), axis=1)


def norm_back(grad_s, normed_ref, scale_ref, inner_s, gain, part_ref, cols, width, gain_grad_ref=None):
    seq_len, step = grad_s.shape
    inverse = 1.0 / gain
    total = jnp.zeros((8, step), f32)
    for start in range(0, seq_len, ROWS):
        rows = pl.ds(start, ROWS)
        grad = grad_s[rows, :]
        unit = normed_ref[rows, cols].astype(f32) * inverse
        coef = wide(inner_s[rows, :] * (1.0 / width), step)
        part_ref[rows, :] = (wide(scale_ref[rows, :], step) * (grad * gain - unit * coef)).astype(part_ref.dtype)
        if gain_grad_ref is not None:
            total = total + jnp.sum((grad * unit).reshape(ROWS // 8, 8, step), axis=0)
    if gain_grad_ref is not None:
        gain_grad_ref[:, cols] = total


def ffn_kernel(
    info_ref, m0, m1, m2, m3, m4, m5, gain_hbm, wg_hbm, wu_hbm, wd_hbm, c0, c1, c2, c3, c4, c5, c6,
    p_across, p_far, p_pair, p_own, gfg_ref, n2_hbm, cotm_hbm, hid_hbm, dgu_hbm,
    gain_ref, wg_ref, wu_ref, wd_ref, cot_s, n2_ref, cotm_ref, hid_ref, dgu_ref,
    gate_s, up_s, gh_s, inner_s, r2_s, in_sems, out_sems,
):
    seq_len, width = n2_ref.shape
    hidden = wg_ref.shape[1]
    length, z = info_ref[0], info_ref[1]
    step = gate_s.shape[1]
    shard = width // 4
    slices = shard_slices(z, shard)
    got_gain, got_wg, got_wu, got_wd = copies(
        (gain_hbm, wg_hbm, wu_hbm, wd_hbm), (gain_ref, wg_ref, wu_ref, wd_ref), in_sems
    )

    def fetch(refs):
        return [
            pltpu.make_async_copy(
                ref.at[pl.ds(0, seq_len), :], cot_s.at[:, pl.ds(k * shard, shard)], in_sems.at[4 + k]
            )
            for k, ref in enumerate(refs)
        ]

    def start_cot(refs):
        for copy in fetch(refs):
            copy.start()

    assemble(z, (c0, c1, c2, c3, c4, c5, c6), start_cot)
    got_gain.wait()

    def normalise(refs):
        def norm(rows):
            ms = [ref[rows, :].astype(f32) for ref in refs]
            r2 = row_scale(sum(m * m for m in ms), width)
            r2_s[rows, :] = jnp.broadcast_to(r2, (ROWS, 128))
            inner_s[rows, :] = jnp.zeros((ROWS, 128), f32)
            for m, cols in zip(ms, slices):
                n2_ref[rows, cols] = (m * r2 * gain_ref[1:2, cols]).astype(bf16)

        row_loop(seq_len, ROWS, norm)

    assemble(z, (m0, m1, m1, m2, m3, m4, m5), normalise)
    for copy in fetch((c0, c1, c2, c3)) + [got_wg, got_wu, got_wd]:
        copy.wait()

    def mask(rows):
        slot = rows.start + lax.broadcasted_iota(jnp.int32, (ROWS, 1), 0)
        for k, cols in enumerate(slices):
            cot = cot_s[rows, k * shard : (k + 1) * shard].astype(f32)
            cotm_ref[rows, cols] = jnp.where(slot < length, cot, 0.0).astype(bf16)

    row_loop(seq_len, ROWS, mask)

    for j in range(0, hidden, step):
        gate_s[...] = dot(n2_ref[...], wg_ref[:, j : j + step])
        up_s[...] = dot(n2_ref[...], wu_ref[:, j : j + step])
        gh_s[...] = dot_t(cotm_ref[...], wd_ref[j : j + step, :])

        def elementwise(rows):
            gate, up, gh = gate_s[rows, :], up_s[rows, :], gh_s[rows, :]
            sig = jax.nn.sigmoid(gate)
            silu = gate * sig
            hid_ref[rows, j : j + step] = (silu * up).astype(bf16)
            dg = (gh * up * (sig * (1.0 + gate * (1.0 - sig)))).astype(bf16)
            du = (gh * silu).astype(bf16)
            dgu_ref[rows, j : j + step] = dg
            dgu_ref[rows, hidden + j : hidden + j + step] = du
            inner = jnp.sum(dg.astype(f32) * gate + du.astype(f32) * up, axis=1, keepdims=True)
            inner_s[rows, :] += jnp.broadcast_to(inner, (ROWS, 128))

        row_loop(seq_len, ROWS, elementwise)

    sent = copies(
        (n2_ref, cotm_ref, hid_ref, dgu_ref), (n2_hbm, cotm_hbm, hid_hbm, dgu_hbm), out_sems
    )
    for part_ref, cols in zip((p_across, p_far, p_pair, p_own), slices):
        gate_s[...] = dot_t(dgu_ref[:, 0:hidden], wg_ref[cols, :]) + dot_t(
            dgu_ref[:, hidden : 2 * hidden], wu_ref[cols, :]
        )
        norm_back(gate_s, n2_ref, r2_s, inner_s, gain_ref[1:2, cols], part_ref, cols, width, gfg_ref)
    for copy in sent:
        copy.wait()


def share(grads_s, core, keep_hbm, give_hbm, sems):
    return copies(
        (grads_s.at[pl.ds(core * 4, 4)], grads_s.at[pl.ds((1 - core) * 4, 4)]), (keep_hbm, give_hbm), sems
    )


def ffn_grad_kernel(
    info_ref, n2_hbm, dgu_hbm, hid_hbm, cotm_hbm, wd_hbm,
    p_across, p_far, p_pair, p_own, keep_hbm, give_hbm,
    n2_ref, dgu_ref, hid_ref, cotm_ref, wd_ref, grads_ref, in_sems, out_sems,
):
    pending = copies(
        (n2_hbm, dgu_hbm, hid_hbm, cotm_hbm, wd_hbm), (n2_ref, dgu_ref, hid_ref, cotm_ref, wd_ref), in_sems
    )
    width, hidden = n2_ref.shape[1], hid_ref.shape[1]
    upper, lower = width // 8, hidden // 8
    rest = upper - lower
    pending[0].wait()
    pending[1].wait()
    for c in range(0, 2 * hidden, 256):
        grad = t_dot(n2_ref[...], dgu_ref[:, c : c + 256])
        for d in range(8):
            grads_ref[d, :, c : c + 256] = grad[d * upper : (d + 1) * upper].astype(bf16)
    for copy in pending[2:]:
        copy.wait()
    for c in range(0, width, 256):
        grad = t_dot(hid_ref[...], cotm_ref[:, c : c + 256])
        for d in range(8):
            block = grad[d * lower : (d + 1) * lower].astype(bf16)
            if c < hidden:
                grads_ref[d, 0:lower, 2 * hidden + c : 2 * hidden + c + 256] = block
            else:
                for k in range(lower // rest):
                    col = 2 * hidden + k * 256
                    grads_ref[d, lower:upper, col : col + 256] = block[k * rest : (k + 1) * rest]
    sent = share(grads_ref, info_ref[3], keep_hbm, give_hbm, out_sems)
    for part_ref, cols in zip((p_across, p_far, p_pair, p_own), shard_slices(info_ref[1], p_own.shape[1])):
        part_ref[...] = dot(hid_ref[...], wd_ref[:, cols]).astype(bf16)
    for copy in sent:
        copy.wait()


def halves_kernel(
    info_ref, keep_hbm, other_hbm, on_x, to_x, on_y, to_y, keep_on_x, keep_x, keep_on_y, keep_y, keep_ref, other_ref, sems
):
    for copy in copies((keep_hbm, other_hbm), (keep_ref, other_ref), sems):
        copy.wait()
    cols = to_x.shape[1]
    for out_ref, first, flip in (
        (on_x, 0, 3), (to_x, 0, 1), (keep_on_x, 0, 2), (keep_x, 0, 0),
        (on_y, cols, 3), (to_y, cols, 2), (keep_on_y, cols, 1), (keep_y, cols, 0),
    ):
        block = jnp.bitwise_xor(info_ref[2], flip)
        out_ref[...] = (
            keep_ref[block, :, first : first + cols].astype(f32) + other_ref[block, :, first : first + cols].astype(f32)
        ).astype(bf16)


def pass_kernel(info_ref, keep_on_x, got_on_x, keep_on_y, got_on_y, to_y, to_x):
    to_y[...] = (keep_on_x[...].astype(f32) + got_on_x[...].astype(f32)).astype(bf16)
    to_x[...] = (keep_on_y[...].astype(f32) + got_on_y[...].astype(f32)).astype(bf16)


def join_kernel(info_ref, keep_x, got_x, from_y, keep_y, got_y, from_x, left_ref, right_ref):
    left_ref[...] = (keep_x[...].astype(f32) + (got_x[...].astype(f32) + from_y[...].astype(f32))).astype(bf16)
    right_ref[...] = (keep_y[...].astype(f32) + (got_y[...].astype(f32) + from_x[...].astype(f32))).astype(bf16)


def unpack_ffn_kernel(info_ref, *refs):
    q, core = info_ref[2], info_ref[3]
    gate_ref, up_ref, down_ref = refs[8:]
    width, hidden = gate_ref.shape
    upper, lower = width // 8, hidden // 8
    rest = upper - lower
    cols = 3 * hidden // 2
    first = 2 * hidden - cols
    for half, (lefts, lefts_x, rights, rights_y) in ((core, refs[0:4]), (1 - core, refs[4:8])):
        for k in range(4):
            block = half * 4 + jnp.bitwise_xor(q, k)
            left, i = (lefts if k in (0, 2) else lefts_x), (0 if k in (0, 1) else 1)
            right, j = (rights if k in (0, 1) else rights_y), (0 if k in (0, 2) else 1)
            rows = pl.ds(pl.multiple_of(block * upper, upper), upper)
            gate_ref[rows, :] = left[i, :, 0:hidden].astype(f32)
            up_ref[rows, 0 : cols - hidden] = left[i, :, hidden:cols].astype(f32)
            up_ref[rows, cols - hidden : hidden] = right[j, :, 0:first].astype(f32)
            rows = pl.ds(pl.multiple_of(block * lower, lower), lower)
            down_ref[rows, 0:hidden] = right[j, 0:lower, first : first + hidden].astype(f32)
            for n in range(lower // rest):
                rows = pl.ds(pl.multiple_of(block * lower + n * rest, rest), rest)
                col = first + n * 256
                down_ref[rows, hidden:width] = right[j, lower:upper, col : col + 256].astype(f32)


def attn_backward_kernel(
    info_ref, g0, g1, g2, g3, g4, g5, qg_ref, kg_ref, wo_hbm, qrot_hbm, krot_hbm, val_hbm, mixed_hbm, lse_hbm,
    cos_hbm, sin_hbm, qpre_hbm, kpre_hbm, n1_hbm, wq_hbm, wk_hbm, wv_hbm, r1_hbm, gain_hbm,
    p_across, p_far, p_pair, p_own, gag_ref, qgg_ref, kgg_ref, keep_hbm, give_hbm,
    wo_ref, qrot_ref, krot_ref, val_ref, mixed_ref, lse_ref, cos_ref, sin_ref, qpre_ref, kpre_ref, n1_ref,
    wq_ref, wk_ref, wv_ref, r1_ref, gain_ref,
    ga_ref, gm_s, dq_s, dk_s, dv_s, dqkv_ref, inner_ref, acc_s, grads_ref, sems, out_sems,
):
    seq_len, width = ga_ref.shape
    hd = qg_ref.shape[1]
    qw, kw = qpre_ref.shape[1], kpre_ref.shape[1]
    heads, kvs = qw // hd, kw // hd
    group = heads // kvs
    length, z = info_ref[0], info_ref[1]
    scale = hd ** (-0.5)
    slices = shard_slices(z, width // 4)
    pending = copies(
        (
            wo_hbm, qrot_hbm, krot_hbm, val_hbm, mixed_hbm, lse_hbm, cos_hbm, sin_hbm, qpre_hbm, kpre_hbm, n1_hbm,
            wq_hbm, wk_hbm, wv_hbm, r1_hbm, gain_hbm,
        ),
        (
            wo_ref, qrot_ref, krot_ref, val_ref, mixed_ref, lse_ref, cos_ref, sin_ref, qpre_ref, kpre_ref, n1_ref,
            wq_ref, wk_ref, wv_ref, r1_ref, gain_ref,
        ),
        sems,
    )

    def collect(refs):
        for ref, cols in zip(refs, slices):
            ga_ref[:, cols] = ref[...]

    assemble(z, (g0, g1, g1, g2, g3, g4, g5), collect)

    pending[0].wait()
    for c in range(0, qw, 256):
        gm_s[:, c : c + 256] = dot_t(ga_ref[...], wo_ref[c : c + 256, :]).astype(bf16)
    dk_s[...] = jnp.zeros_like(dk_s)
    dv_s[...] = jnp.zeros_like(dv_s)
    for copy in pending[1:6]:
        copy.wait()

    for start, rows, keys in query_units(seq_len):
        bias = key_bias(length, keys)
        for g in range(kvs):
            first = g * group
            cols = slice(g * hd, (g + 1) * hd)
            key, val = krot_ref[0:keys, cols], val_ref[0:keys, cols]

            def stacked(ref):
                return jnp.concatenate(
                    [ref[start : start + rows, h * hd : (h + 1) * hd] for h in range(first, first + group)], axis=0
                )

            q, gm, mixed = stacked(qrot_ref), stacked(gm_s), stacked(mixed_ref)
            lse = jnp.concatenate(
                [lse_ref[start : start + rows, h : h + 1] for h in range(first, first + group)], axis=0
            )
            p = jnp.exp2(dot_t(q, key) * (scale * LOG2E) + bias - lse)
            delta = jnp.sum(gm.astype(f32) * mixed.astype(f32), axis=1, keepdims=True)
            ds = (p * (dot_t(gm, val) - delta)).astype(bf16)
            dv_s[0:keys, cols] += t_dot(p.astype(bf16), gm)
            dk_s[0:keys, cols] += t_dot(ds, q)
            dq = dot(ds, key)
            for r in range(group):
                h = first + r
                dq_s[start : start + rows, h * hd : (h + 1) * hd] = dq[r * rows : (r + 1) * rows]

    for copy in pending[6:]:
        copy.wait()
    ones = jnp.full((hd, hd), 1.0 / hd, bf16)

    def unrotate(rows, rot_s, pre_ref, g_ref, count, base, gain_sum):
        cos, sin = cos_ref[rows, :], sin_ref[rows, :]
        inner = jnp.zeros((ROWS, hd), f32)
        for c in range(0, count, hd):
            g = rot_s[rows, c : c + hd] * scale
            u = g * cos + pltpu.roll(g * sin, hd // 2, 1)
            v = pre_ref[rows, c : c + hd]
            r = lax.rsqrt(dot((v * v).astype(bf16), ones) + NORM_EPSILON)
            unit = v * r
            t = u * unit
            gain_sum = gain_sum + jnp.sum(t.reshape(ROWS // 8, 8, hd), axis=0)
            mean = dot((t * g_ref[...]).astype(bf16), ones)
            dqkv_ref[rows, base + c : base + c + hd] = (r * (u * g_ref[...] - unit * mean)).astype(bf16)
            inner = inner + (hd * NORM_EPSILON) * (r * r * mean)
        return inner, gain_sum

    qgs = kgs = jnp.zeros((8, hd), f32)
    for start in range(0, seq_len, ROWS):
        rows = pl.ds(start, ROWS)
        qi, qgs = unrotate(rows, dq_s, qpre_ref, qg_ref, qw, 0, qgs)
        ki, kgs = unrotate(rows, dk_s, kpre_ref, kg_ref, kw, qw, kgs)
        dv = dv_s[rows, :].astype(bf16)
        dqkv_ref[rows, qw + kw : qw + 2 * kw] = dv
        vi = jnp.sum(dv.astype(f32) * val_ref[rows, :].astype(f32), axis=1, keepdims=True)
        inner_ref[rows, :] = qi + ki + vi
    qgg_ref[...] = qgs
    kgg_ref[...] = kgs

    upper, lower = width // 8, qw // 8
    for c in range(0, width, 256):
        grad = t_dot(n1_ref[...], dqkv_ref[:, c : c + 256])
        out = t_dot(mixed_ref[...], ga_ref[:, c : c + 256])
        for d in range(8):
            grads_ref[d, 0:upper, c : c + 256] = grad[d * upper : (d + 1) * upper].astype(bf16)
            grads_ref[d, upper : upper + lower, c : c + 256] = out[d * lower : (d + 1) * lower].astype(bf16)
    sent = share(grads_ref, info_ref[3], keep_hbm, give_hbm, out_sems)
    for part_ref, cols in zip((p_across, p_far, p_pair, p_own), slices):
        acc_s[...] = (
            dot_t(dqkv_ref[:, 0:qw], wq_ref[cols, :])
            + dot_t(dqkv_ref[:, qw : qw + kw], wk_ref[cols, :])
            + dot_t(dqkv_ref[:, qw + kw : qw + 2 * kw], wv_ref[cols, :])
        )
        norm_back(acc_s, n1_ref, r1_ref, inner_ref, gain_ref[0:1, cols], part_ref, cols, width, gag_ref)
    for copy in sent:
        copy.wait()


def output_kernel(info_ref, middle_ref, attn_ref, own_ref, pair_ref, across_ref, out_ref, sums_ref):
    seq_len, shard = middle_ref.shape
    length = info_ref[0]
    sums = [jnp.zeros((8, shard), f32)] * 3
    for start in range(0, seq_len, ROWS):
        rows = pl.ds(start, ROWS)
        ffn = own_ref[rows, :].astype(f32) + (pair_ref[rows, :].astype(f32) + across_ref[rows, :].astype(f32))
        out = middle_ref[rows, :] + ffn
        out_ref[rows, :] = out.astype(bf16)
        slot = start + lax.broadcasted_iota(jnp.int32, (ROWS, 1), 0)
        for i, v in enumerate((out, attn_ref[rows, :], ffn)):
            v = jnp.where(slot < length, v, 0.0)
            sums[i] = sums[i] + jnp.sum((v * v).reshape(ROWS // 8, 8, shard), axis=0)
    for i in range(3):
        sums_ref[i : i + 1, :] = jnp.sum(sums[i], axis=0, keepdims=True)


def small_kernel(info_ref, gag_ref, gfg_ref, qgg_ref, kgg_ref, sums_ref, small_ref):
    hd, shard = qgg_ref.shape[1], sums_ref.shape[1]
    small_ref[...] = jnp.zeros(small_ref.shape, f32)
    small_ref[0:1, :] = jnp.sum(gag_ref[...], axis=0, keepdims=True)
    small_ref[1:2, :] = jnp.sum(gfg_ref[...], axis=0, keepdims=True)
    small_ref[2:3, 0:hd] = jnp.sum(qgg_ref[...], axis=0, keepdims=True)
    small_ref[2:3, hd : 2 * hd] = jnp.sum(kgg_ref[...], axis=0, keepdims=True)
    lane = lax.broadcasted_iota(jnp.int32, (1, 128), 1)
    totals = (info_ref[0] * shard).astype(f32) * (lane == 3).astype(f32)
    for i in range(3):
        totals = totals + jnp.sum(sums_ref[i : i + 1, :], axis=1, keepdims=True) * (lane == i).astype(f32)
    small_ref[2:3, 2 * hd : 2 * hd + 128] = totals


def block_kernel(info_ref, keep_x, got_x, from_y, keep_y, got_y, from_x, small_ref, left_ref, right_ref):
    rows, cols = keep_x.shape
    small = small_ref[...]
    high = small.astype(bf16)
    tail = jnp.concatenate([high, (small - high.astype(f32)).astype(bf16)], axis=0)
    for a, b, c, out_ref, first in ((keep_x, got_x, from_y, left_ref, 0), (keep_y, got_y, from_x, right_ref, cols)):
        out_ref[0:rows, :] = (a[...].astype(f32) + (b[...].astype(f32) + c[...].astype(f32))).astype(bf16)
        out_ref[rows : rows + TAIL, :] = tail[:, first : first + cols]


def unpack_kernel(info_ref, *refs):
    q, core = info_ref[2], info_ref[3]
    gq_ref, gk_ref, gv_ref, go_ref, ag_ref, fg_ref, qg_ref, kg_ref, rms_ref, small_ref = refs[8:]
    cols, kw = gq_ref.shape[1], gk_ref.shape[1]
    upper, lower = gq_ref.shape[0] // 8, go_ref.shape[0] // 8
    for half, (lefts, lefts_x, rights, rights_y) in ((core, refs[0:4]), (1 - core, refs[4:8])):
        for k in range(4):
            block = half * 4 + jnp.bitwise_xor(q, k)
            left, i = (lefts if k in (0, 2) else lefts_x), (0 if k in (0, 1) else 1)
            right, j = (rights if k in (0, 1) else rights_y), (0 if k in (0, 2) else 1)
            rows = pl.ds(pl.multiple_of(block * upper, upper), upper)
            gq_ref[rows, :] = left[i, 0:upper, :].astype(f32)
            gk_ref[rows, :] = right[j, 0:upper, 0:kw].astype(f32)
            gv_ref[rows, :] = right[j, 0:upper, kw : 2 * kw].astype(f32)
            rows = pl.ds(pl.multiple_of(block * lower, lower), lower)
            go_ref[rows, 0:cols] = left[i, upper : upper + lower, :].astype(f32)
            go_ref[rows, cols : 2 * cols] = right[j, upper : upper + lower, :].astype(f32)
    for first, group in ((0, (0, 1, 4, 5)), (cols, (2, 3, 6, 7))):
        total = jnp.zeros((8, cols), f32)
        for n in group:
            for i in range(2):
                tail = refs[n][i, upper + lower : upper + lower + TAIL, :].astype(f32)
                total = total + (tail[0:8] + tail[8:16])
        small_ref[:, first : first + cols] = total
    shard, hd = ag_ref.shape[1], qg_ref.shape[1]
    mine = pl.ds(pl.multiple_of(info_ref[1] * shard, shard), shard)
    ag_ref[...] = small_ref[0:1, mine]
    fg_ref[...] = small_ref[1:2, mine]
    qg_ref[...] = small_ref[2:3, 0:hd]
    kg_ref[...] = small_ref[2:3, hd : 2 * hd]
    totals = small_ref[2:3, 2 * hd : 2 * hd + 128]
    lane = lax.broadcasted_iota(jnp.int32, (1, 128), 1)
    count = jnp.sum(jnp.where(lane == 3, totals, 0.0), axis=1, keepdims=True)
    rms_ref[...] = jnp.sqrt(totals / count)


SPECS = {
    "s": pl.BlockSpec(memory_space=pltpu.SMEM),
    "v": pl.BlockSpec(memory_space=pltpu.VMEM),
    "a": pl.BlockSpec(memory_space=pl.ANY),
}


def call(body, outs, args, scratch=(), sems=(), flops=0, bytes_accessed=0, limit=SMALL_BYTES):
    places, arrays = [], []
    for place, *group in args:
        places += [place] * len(group)
        arrays += group
    return pl.pallas_call(
        body,
        out_shape=[jax.ShapeDtypeStruct(s, d) for s, d, _ in outs],
        in_specs=[SPECS[p] for p in places],
        out_specs=[SPECS[p] for _, _, p in outs],
        scratch_shapes=[pltpu.VMEM(s, d) for s, d in scratch] + [pltpu.SemaphoreType.DMA((n,)) for n in sems],
        compiler_params=pltpu.CompilerParams(vmem_limit_bytes=limit),
        cost_estimate=pl.CostEstimate(flops=flops, bytes_accessed=bytes_accessed, transcendentals=0),
    )(*arrays)


PAIRS = ((0, 1), (1, 0), (2, 3), (3, 2))
MIDDLE = ((1, 2), (2, 1))
OUTWARD = ((1, 0), (2, 3))
INWARD = ((0, 1), (3, 2))
OUTWARD_TWO = ((2, 0), (1, 3))
INWARD_TWO = ((0, 2), (3, 1))


def send(rows, pairs):
    return lax.ppermute(rows, "tensor", pairs)


def hold(*values):
    return lax.optimization_barrier(values)


def gather_line(own):
    pair = send(own, PAIRS)
    across_mid = send(own, MIDDLE)
    far_end = send(pair, OUTWARD_TWO)
    far_mid = send(pair, MIDDLE)
    across_end = send(across_mid, OUTWARD)
    return own, pair, across_mid, across_end, far_mid, far_end


def pick(end, from_end, from_middle):
    return jnp.where(end, from_end, from_middle)


def scatter_first(parts):
    across, far, _, _ = parts
    return send(far, INWARD_TWO), send(far, MIDDLE), send(across, INWARD)


def scatter_last(parts, first):
    across, _, pair, own = parts
    two, three, one = first
    to_pair = (pair.astype(f32) + (two.astype(f32) + three.astype(f32))).astype(bf16)
    to_across = (across.astype(f32) + one.astype(f32)).astype(bf16)
    return own, send(to_pair, PAIRS), send(to_across, MIDDLE)


def add(a, b):
    return (a.astype(f32) + b.astype(f32)).astype(bf16)


def total(terms):
    own, pair, across = terms
    return own.astype(f32) + (pair.astype(f32) + across.astype(f32))


def swap(values, bit):
    return lax.ppermute(values, "dp", [(i, i ^ bit) for i in range(8)])


def halve(keep, other, info):
    _, rows, width = keep.shape
    return call(
        halves_kernel,
        [((rows, width // 2), bf16, "v")] * 8,
        (("s", info), ("a", keep, other)),
        scratch=[((4, rows, width), bf16)] * 2,
        sems=(2,),
    )


def pass_on(keep_on_x, got_on_x, keep_on_y, got_on_y, info):
    return call(
        pass_kernel, [(keep_on_x.shape, bf16, "v")] * 2, (("s", info), ("v", keep_on_x, got_on_x, keep_on_y, got_on_y))
    )


def per_device(
    hidden_in, lengths, w_query, w_key, w_value, w_out, attn_gain, ffn_gain,
    query_gain, key_gain, w_gate, w_up, w_down, cotangent,
):
    seq_len, shard = hidden_in.shape
    width = w_query.shape[0]
    hd = query_gain.shape[0]
    qw, kw = w_query.shape[1], w_key.shape[1]
    hidden = w_gate.shape[1]
    padded = -(-seq_len // BLOCK) * BLOCK
    z = lax.axis_index("tensor").astype(jnp.int32)
    dp = lax.axis_index("dp").astype(jnp.int32)
    chips = lax.axis_size("dp") == 8
    q, core = (dp // 2, dp % 2) if chips else (0 * dp, 0 * dp)
    info = jnp.stack([lengths[0], z, q, core])
    parts = [((seq_len, shard), bf16, "v")] * 4

    end = (z == 0) | (z == 3)
    x = call(
        pack_kernel,
        [((seq_len + TAIL, shard), bf16, "v")],
        (("s", lengths), ("v", hidden_in, attn_gain[None], ffn_gain[None])),
    )[0]
    cot = jnp.concatenate([cotangent, jnp.zeros((TAIL, shard), bf16)], axis=0)
    x_pair, x_mid = send(x, PAIRS), send(x, MIDDLE)
    x_pair, x_mid, cot = hold(x_pair, x_mid, cot)
    x_end, x_far = send(pick(end, cot, x_mid), PAIRS), send(x_pair, MIDDLE)
    x_end, x_far, cot = hold(x_end, x_far, cot)
    x_last, cot_far = send(x_far, OUTWARD), send(x_end, MIDDLE)
    x_last, cot_far, x_end, cot = hold(x_last, cot_far, x_end, cot)
    cot_mid, cot_pair, cot_last = send(cot, MIDDLE), send(cot, OUTWARD), send(cot_far, OUTWARD)
    cos, sin = rope_tables(seq_len, hd)
    qg, kg = query_gain[None], key_gain[None]
    resid = hidden_in.astype(f32)
    valid = (jnp.arange(seq_len, dtype=jnp.int32) < lengths[0]).astype(f32)[:, None]

    saved = [
        ((seq_len, width), bf16), ((seq_len, qw), f32), ((seq_len, kw), f32), ((seq_len, qw), bf16),
        ((padded, kw), bf16), ((padded, kw), bf16), ((seq_len, qw), bf16), ((seq_len, 128), f32),
        ((seq_len, 128), f32), ((8, width), f32),
    ]
    weights = [((width, kw), bf16), ((width, kw), bf16), ((width, qw), bf16), ((qw, width), bf16)]
    tables = [((seq_len, hd), f32)] * 2
    *attn_parts, n1, qpre, kpre, qrot, krot, val, mixed, lse, r1, gain = call(
        attn_forward_kernel,
        parts + [(s, d, "a") for s, d in saved],
        (
            ("s", info), ("v", x, x_pair, x_mid, x_end, x_far, x_last, qg, kg),
            ("a", w_key, cos, sin, w_value, w_query, w_out),
        ),
        scratch=weights[:1] + tables + weights[1:] + saved,
        sems=(6, 10),
        limit=FULL_BYTES,
        flops=2 * seq_len * width * (2 * qw + 2 * kw) + 4 * seq_len * seq_len * qw,
        bytes_accessed=14_000_000,
    )
    attn_parts, cot_mid, cot_pair, cot_last = hold(attn_parts, cot_mid, cot_pair, cot_last)
    across, far, pair, own = attn_parts
    two = send(far, INWARD_TWO)
    one, three = hold(pick(end, across, cot_mid[:seq_len]), far)
    three, one = send(three, MIDDLE), send(one, PAIRS)
    zero_end = pick(end, jnp.zeros_like(one), one)
    pair = lax.optimization_barrier(pair.astype(f32) + two.astype(f32))
    attn_local = total(scatter_last((across, far, pair, own), (jnp.zeros_like(two), three, zero_end)))
    middle = resid + attn_local
    shard_two, one = hold(middle.astype(bf16), one)
    m_parts = gather_line(shard_two)

    kept = [((seq_len, width), bf16), ((seq_len, width), bf16), ((seq_len, hidden), bf16), ((seq_len, 2 * hidden), bf16)]
    *ffn_parts, gfg, n2, cotm, hid, dgu = call(
        ffn_kernel,
        parts + [((8, width), f32, "v")] + [(s, d, "a") for s, d in kept],
        (
            ("s", info), ("v", *m_parts), ("a", gain, w_gate, w_up, w_down),
            ("a", cot, x_end, cot_pair, cot_mid, one, cot_far, cot_last),
        ),
        scratch=[((8, width), f32)] + [((width, hidden), bf16)] * 2 + [((hidden, width), bf16), ((seq_len, width), bf16)]
        + kept + [((seq_len, 256), f32)] * 3 + [((seq_len, 128), f32)] * 2,
        sems=(8, 4),
        limit=VMEM_BYTES,
        flops=2 * seq_len * width * hidden * 5,
        bytes_accessed=16_000_000,
    )
    grad_top = cotangent.astype(f32) * valid
    first = scatter_first(ffn_parts)
    blocks = ((4, width // 8, 3 * hidden), bf16, "a")
    *down_parts, ffn_keep, ffn_give = call(
        ffn_grad_kernel,
        parts + [blocks] * 2,
        (("s", info), ("a", n2, dgu, hid, cotm, w_down)),
        scratch=[kept[0], kept[3], kept[2], kept[1], ((hidden, width), bf16), ((8, width // 8, 3 * hidden), bf16)],
        sems=(5, 2),
        limit=VMEM_BYTES,
        flops=2 * seq_len * width * hidden * 4,
        bytes_accessed=14_000_000,
    )
    first, ffn_keep, ffn_give = hold(first, ffn_keep, ffn_give)
    back = scatter_last(ffn_parts, first)
    if chips:
        ffn_other = swap(ffn_give, 1)
        halves = halve(ffn_keep, ffn_other, info)
        back, halves = hold(back, halves)
        on_x, to_x, on_y, to_y, keep_on_x, keep_x, keep_on_y, keep_y = halves
    grad_middle = grad_top + total(back)
    ga = grad_middle.astype(bf16)
    across, far, pair, own = down_parts
    ga_pair, ga_mid = send(ga, PAIRS), send(ga, MIDDLE)
    if chips:
        got_on_x, got_on_y = swap(on_x, 2), swap(on_y, 4)
        got_x, got_y = swap(to_x, 2), swap(to_y, 4)
        to_y, to_x = pass_on(keep_on_x, got_on_x, keep_on_y, got_on_y, info)
        ga_pair, ga_mid, far, to_y, to_x = hold(ga_pair, ga_mid, far, to_y, to_x)
        from_y, from_x = swap(to_y, 4), swap(to_x, 2)
    ga_end, ga_far = send(pick(end, far, ga_mid), PAIRS), send(ga_pair, MIDDLE)
    if chips:
        left, right = call(
            join_kernel,
            [((width // 8, 3 * hidden // 2), bf16, "v")] * 2,
            (("s", info), ("v", keep_x, got_x, from_y, keep_y, got_y, from_x)),
        )
        ga_end, ga_far, across, left, right = hold(ga_end, ga_far, across, left, right)
        left_y, right_x = swap(left, 4), swap(right, 2)
    ga_last = send(pick(end, across, ga_far), PAIRS)
    got_far = send(add(far, ga_end), MIDDLE)
    if chips:
        ga_last, got_far, left_y, right_x = hold(ga_last, got_far, left_y, right_x)
        lefts, rights = jnp.stack([left, left_y]), jnp.stack([right, right_x])
        lefts_x, rights_y = swap(lefts, 2), swap(rights, 4)
    ga_parts = (ga, ga_pair, ga_mid, ga_end, ga_far, ga_last)
    ffn_terms = (own, send(add(pair, got_far), PAIRS), send(add(across, ga_last), MIDDLE))

    blocks = (4, (width + qw) // 8, width)
    *back_parts, gag, qgg, kgg, keep, give = call(
        attn_backward_kernel,
        parts + [((8, width), f32, "v"), ((8, hd), f32, "v"), ((8, hd), f32, "v"), (blocks, bf16, "a"), (blocks, bf16, "a")],
        (
            ("s", info), ("v", *ga_parts, qg, kg),
            ("a", w_out, qrot, krot, val, mixed, lse, cos, sin, qpre, kpre, n1, w_query, w_key, w_value, r1, gain),
        ),
        scratch=[weights[3], saved[3], saved[4], saved[5], saved[6], saved[7], *tables, saved[1], saved[2], saved[0]]
        + [weights[2], weights[0], weights[1], saved[8], saved[9]]
        + [((seq_len, width), bf16), ((seq_len, qw), bf16), ((seq_len, qw), f32), ((padded, kw), f32), ((padded, kw), f32)]
        + [((seq_len, qw + 2 * kw), bf16), ((seq_len, 128), f32), ((seq_len, shard), f32), ((8, *blocks[1:]), bf16)],
        sems=(16, 2),
        limit=VMEM_BYTES,
        flops=2 * seq_len * width * (4 * qw + 4 * kw) + 10 * seq_len * seq_len * qw,
        bytes_accessed=20_000_000,
    )
    across, far, pair, own = back_parts
    if chips:
        far, ffn_terms, keep, give, lefts_x, rights_y = hold(far, ffn_terms, keep, give, lefts_x, rights_y)
        other = swap(give, 1)
    out_rows, sums = call(
        output_kernel,
        [((seq_len, shard), bf16, "v"), ((8, shard), f32, "v")],
        (("s", info), ("v", middle, attn_local, *ffn_terms)),
        bytes_accessed=2_000_000,
    )
    small = call(small_kernel, [((8, width), f32, "v")], (("s", info), ("v", gag, gfg, qgg, kgg, sums)))[0]
    shapes = [(width, qw), (width, kw), (width, kw), (qw, width)]
    if chips:
        other, small = hold(other, small)
        on_x, to_x, on_y, to_y, keep_on_x, keep_x, keep_on_y, keep_y = halve(keep, other, info)
        got_on_x, got_on_y = swap(on_x, 2), swap(on_y, 4)
        got_x, got_y = swap(to_x, 2), swap(to_y, 4)
        small = small + send(small, PAIRS)
        small = small + send(small, ((0, 2), (2, 0), (1, 3), (3, 1)))
        to_y, to_x = pass_on(keep_on_x, got_on_x, keep_on_y, got_on_y, info)
        to_y, to_x, small, far, across = hold(to_y, to_x, small, far, across)
        from_y, from_x, two = swap(to_y, 4), swap(to_x, 2), send(far, INWARD_TWO)
        late_left, late_right = call(
            block_kernel,
            [((keep_x.shape[0] + TAIL, keep_x.shape[1]), bf16, "v")] * 2,
            (("s", info), ("v", keep_x, got_x, from_y, keep_y, got_y, from_x, small)),
        )
        late_left, late_right, far, across = hold(late_left, late_right, far, across)
        three, one = send(far, MIDDLE), send(across, INWARD)
        left_y, right_x, two, three, one = hold(swap(late_left, 4), swap(late_right, 2), two, three, one)
        late_lefts, late_rights = jnp.stack([late_left, left_y]), jnp.stack([late_right, right_x])
        back_terms = scatter_last((across, far, pair, own), (two, three, one))
        ffn_halves = (lefts, lefts_x, rights, rights_y)
        g_gate, g_up, g_down = call(
            unpack_ffn_kernel,
            [(s, f32, "v") for s in ((width, hidden), (width, hidden), (hidden, width))],
            (("s", info), ("v", *ffn_halves, *[swap(b, 1) for b in ffn_halves])),
            bytes_accessed=14_000_000,
        )
        late = (late_lefts, swap(late_lefts, 2), late_rights, swap(late_rights, 4))
        late, back_terms, g_gate, g_up, g_down = hold(late, back_terms, g_gate, g_up, g_down)
        everyone = [*late, *[swap(b, 1) for b in late]]
        gq, gk, gv, go, ag, fg, qgg, kgg, rms = call(
            unpack_kernel,
            [(s, f32, "v") for s in shapes + [(1, shard), (1, shard), (1, hd), (1, hd), (1, 128)]],
            (("s", info), ("v", *everyone)),
            scratch=[((8, width), f32)],
            bytes_accessed=9_000_000,
        )
    else:
        back_terms = scatter_last(back_parts, scatter_first(back_parts))
        grads, ffn_grads = lax.psum((jnp.concatenate([keep, give]), jnp.concatenate([ffn_keep, ffn_give])), "dp")
        small = lax.psum(small, ("dp", "tensor"))
        ag, fg = [lax.dynamic_slice(small, (i, z * shard), (1, shard)) for i in (0, 1)]
        qgg, kgg = small[2:3, :hd], small[2:3, hd : 2 * hd]
        totals = small[2:3, 2 * hd : 2 * hd + 4]
        rms = jnp.sqrt(totals / totals[:, 3:])
        g_qkv = grads[:, : width // 8].reshape(width, width).astype(f32)
        gq, gk, gv = g_qkv[:, :qw], g_qkv[:, qw : qw + kw], g_qkv[:, qw + kw :]
        go = grads[:, width // 8 :].reshape(qw, width).astype(f32)
        g_gate = ffn_grads[:, :, :hidden].reshape(width, hidden).astype(f32)
        g_up = ffn_grads[:, :, hidden : 2 * hidden].reshape(width, hidden).astype(f32)
        folded = ffn_grads[:, :, 2 * hidden :]
        lower = hidden // 8
        tail = folded[:, lower:].reshape(8, width // 8 - lower, -1, 256).transpose(0, 2, 1, 3).reshape(8, lower, 256)
        g_down = jnp.concatenate([folded[:, :lower], tail], axis=2).reshape(hidden, width).astype(f32)
    input_grad = (grad_middle + total(back_terms)).astype(bf16)
    return (
        out_rows,
        input_grad,
        gq,
        gk,
        gv,
        go,
        ag[0],
        fg[0],
        qgg[0],
        kgg[0],
        g_gate,
        g_up,
        g_down,
        rms[0, :3],
    )


def solution(mesh):
    rows, cols, first = P("dp", "tensor"), P(None, "tensor"), P("tensor", None)
    gain = P("tensor")
    return jax.shard_map(
        per_device,
        mesh=mesh,
        in_specs=(rows, P("dp"), cols, cols, cols, first, gain, gain, P(), P(), cols, cols, first, rows),
        out_specs=(rows, rows, cols, cols, cols, first, gain, gain, P(), P(), cols, cols, first, P()),
        check_vma=False,
    )
```

```python
import functools

import jax
import jax.numpy as jnp
from jax import lax
from jax.experimental import pallas as pl
from jax.experimental.pallas import tpu as pltpu
from jax.sharding import PartitionSpec as P

BLOCK = 256
NORM_EPSILON = 1e-06
ROPE_THETA = 1000000.0
LOG2E = 1.4426950408889634
NEG = -1e30
ROWS = 64
TAIL = 16
FULL_BYTES = 44 * 1024 * 1024
VMEM_BYTES = 40 * 1024 * 1024
SMALL_BYTES = 24 * 1024 * 1024

bf16 = jnp.bfloat16
f32 = jnp.float32


def dot(a, b):
    return jnp.dot(a, b, preferred_element_type=f32)


def dot_t(a, b):
    return lax.dot_general(a, b, (((1,), (1,)), ((), ())), preferred_element_type=f32)


def t_dot(a, b):
    return lax.dot_general(a, b, (((0,), (0,)), ((), ())), preferred_element_type=f32)


def row_loop(count, step, body):
    for start in range(0, count, step):
        body(pl.ds(start, step))


def rope_tables(length, width):
    half_width = width // 2
    frequency = ROPE_THETA ** (-(jnp.arange(half_width, dtype=f32) * (2.0 / width)))
    angles = jnp.arange(length, dtype=f32)[:, None] * frequency[None, :]
    cos, sin = jnp.cos(angles), jnp.sin(angles)
    return jnp.concatenate([cos, cos], axis=1), jnp.concatenate([-sin, sin], axis=1)


def query_units(seq_len):
    units = []
    start = 0
    while start < seq_len:
        rows = min(128, seq_len - start)
        keys = (start // BLOCK + 1) * BLOCK
        units.append((start, rows, keys))
        start += rows
    return units


def roles(z):
    low = z < 2
    return jnp.where(low, 2, 1), jnp.where(low, 3, 0), z + 1 - 2 * lax.rem(z, 2), z


def shard_slices(z, width):
    return [pl.ds(pl.multiple_of(shard * width, width), width) for shard in roles(z)]


def assemble(z, pieces, body):
    own, pair_mid, pair_end, across_mid, across_end, far_mid, far_end = pieces
    end = (z == 0) | (z == 3)

    @pl.when(end)
    def _():
        body((across_end, far_end, pair_end, own))

    @pl.when(jnp.logical_not(end))
    def _():
        body((across_mid, far_mid, pair_mid, own))


def key_bias(length, keys):
    slot = lax.broadcasted_iota(jnp.int32, (1, keys), 1)
    return jnp.where(slot < length, 0.0, NEG).astype(f32)


def row_scale(squares, width):
    return lax.rsqrt(jnp.sum(squares, axis=1, keepdims=True) * (1.0 / width) + NORM_EPSILON)


def pack_kernel(info_ref, x_ref, ag_ref, fg_ref, out_ref):
    seq_len, shard = x_ref.shape
    out_ref[0:seq_len, :] = x_ref[...]
    gains = jnp.concatenate([ag_ref[...], fg_ref[...], jnp.zeros((6, shard), f32)], axis=0)
    high = gains.astype(bf16)
    out_ref[seq_len : seq_len + TAIL, :] = jnp.concatenate([high, (gains - high.astype(f32)).astype(bf16)], axis=0)


def copies(sources, targets, sems):
    pending = [pltpu.make_async_copy(a, b, sems.at[i]) for i, (a, b) in enumerate(zip(sources, targets))]
    for copy in pending:
        copy.start()
    return pending


def attn_forward_kernel(
    info_ref, x0, x1, x2, x3, x4, x5, qg_ref, kg_ref, wk_hbm, cos_hbm, sin_hbm, wv_hbm, wq_hbm, wo_hbm,
    p_across, p_far, p_pair, p_own, n1_hbm, qpre_hbm, kpre_hbm, qrot_hbm, krot_hbm, val_hbm, mixed_hbm, lse_hbm,
    r1_hbm, gain_hbm,
    wk_ref, cos_ref, sin_ref, wv_ref, wq_ref, wo_ref, n1_ref, qpre_ref, kpre_ref, qrot_ref, krot_ref, val_ref,
    mixed_ref, lse_ref, r1_ref, gain_ref, in_sems, out_sems,
):
    seq_len, width = n1_ref.shape
    hd = qg_ref.shape[1]
    heads = wq_ref.shape[1] // hd
    kvs = wk_ref.shape[1] // hd
    group = heads // kvs
    padded = krot_ref.shape[0]
    length, z = info_ref[0], info_ref[1]
    scale = hd ** (-0.5) * LOG2E
    slices = shard_slices(z, width // 4)
    pending = copies(
        (wk_hbm, cos_hbm, sin_hbm, wv_hbm, wq_hbm, wo_hbm), (wk_ref, cos_ref, sin_ref, wv_ref, wq_ref, wo_ref), in_sems
    )
    sent = []

    def put(source, target):
        copy = pltpu.make_async_copy(source, target, out_sems.at[len(sent)])
        copy.start()
        sent.append(copy)

    def normalise(refs):
        for ref, cols in zip(refs, slices):
            tail = ref[seq_len : seq_len + TAIL, :].astype(f32)
            gain_ref[:, cols] = tail[0:8] + tail[8:16]

        def norm(rows):
            xs = [ref[rows, :].astype(f32) for ref in refs]
            r1 = row_scale(sum(x * x for x in xs), width)
            r1_ref[rows, :] = jnp.broadcast_to(r1, (ROWS, 128))
            for x, cols in zip(xs, slices):
                n1_ref[rows, cols] = (x * r1 * gain_ref[0:1, cols]).astype(bf16)

        row_loop(seq_len, ROWS, norm)

    assemble(z, (x0, x1, x1, x2, x3, x4, x5), normalise)
    put(n1_ref, n1_hbm)
    put(r1_ref, r1_hbm)
    put(gain_ref, gain_hbm)

    def project(w_ref, pre_ref, rot_ref, g_ref):
        count = w_ref.shape[1]
        for c in range(0, count, 2 * hd):
            pre_ref[:, c : c + 2 * hd] = dot(n1_ref[...], w_ref[:, c : c + 2 * hd])

        def rotate(rows):
            cos, sin = cos_ref[rows, :], sin_ref[rows, :]
            for c in range(0, count, hd):
                v = pre_ref[rows, c : c + hd]
                v = v * row_scale(v * v, hd) * g_ref[...]
                rot_ref[rows, c : c + hd] = (v * cos + pltpu.roll(v, hd // 2, 1) * sin).astype(bf16)

        row_loop(seq_len, ROWS, rotate)

    for copy in pending:
        copy.wait()
    project(wk_ref, kpre_ref, krot_ref, kg_ref)
    val_ref[0:seq_len, :] = dot(n1_ref[...], wv_ref[...]).astype(bf16)
    if padded > seq_len:
        krot_ref[seq_len:padded, :] = jnp.zeros((padded - seq_len, kvs * hd), bf16)
        val_ref[seq_len:padded, :] = jnp.zeros((padded - seq_len, kvs * hd), bf16)
    put(kpre_ref, kpre_hbm)
    put(krot_ref, krot_hbm)
    put(val_ref, val_hbm)
    project(wq_ref, qpre_ref, qrot_ref, qg_ref)
    put(qpre_ref, qpre_hbm)
    put(qrot_ref, qrot_hbm)

    for start, rows, keys in query_units(seq_len):
        bias = key_bias(length, keys)
        for g in range(kvs):
            key = krot_ref[0:keys, g * hd : (g + 1) * hd]
            val = val_ref[0:keys, g * hd : (g + 1) * hd]
            first = g * group
            q = jnp.concatenate(
                [qrot_ref[start : start + rows, h * hd : (h + 1) * hd] for h in range(first, first + group)], axis=0
            )
            e = jnp.exp2(dot_t(q, key) * scale + bias)
            total = jnp.sum(e, axis=1, keepdims=True)
            mixed = dot(e.astype(bf16), val) * (1.0 / total)
            lse = jnp.log2(total)
            for r in range(group):
                h = first + r
                mixed_ref[start : start + rows, h * hd : (h + 1) * hd] = mixed[r * rows : (r + 1) * rows].astype(bf16)
                lse_ref[start : start + rows, h : h + 1] = lse[r * rows : (r + 1) * rows]

    put(mixed_ref, mixed_hbm)
    put(lse_ref, lse_hbm)
    for part_ref, cols in zip((p_across, p_far, p_pair, p_own), slices):
        part_ref[...] = dot(mixed_ref[...], wo_ref[:, cols]).astype(part_ref.dtype)
    for copy in sent:
        copy.wait()


def wide(column, width):
    return jnp.concatenate([column] * (width // column.shape[1]), axis=1)


def norm_back(grad_s, normed_ref, scale_ref, inner_s, gain, part_ref, cols, width, gain_grad_ref=None):
    seq_len, step = grad_s.shape
    inverse = 1.0 / gain
    total = jnp.zeros((8, step), f32)
    for start in range(0, seq_len, ROWS):
        rows = pl.ds(start, ROWS)
        grad = grad_s[rows, :]
        unit = normed_ref[rows, cols].astype(f32) * inverse
        coef = wide(inner_s[rows, :] * (1.0 / width), step)
        part_ref[rows, :] = (wide(scale_ref[rows, :], step) * (grad * gain - unit * coef)).astype(part_ref.dtype)
        if gain_grad_ref is not None:
            total = total + jnp.sum((grad * unit).reshape(ROWS // 8, 8, step), axis=0)
    if gain_grad_ref is not None:
        gain_grad_ref[:, cols] = total


def ffn_kernel(
    info_ref, m0, m1, m2, m3, m4, m5, gain_hbm, wg_hbm, wu_hbm, wd_hbm, c0, c1, c2, c3, c4, c5, c6,
    p_across, p_far, p_pair, p_own, gfg_ref, n2_hbm, cotm_hbm, hid_hbm, dgu_hbm,
    gain_ref, wg_ref, wu_ref, wd_ref, cot_s, n2_ref, cotm_ref, hid_ref, dgu_ref,
    gate_s, up_s, gh_s, inner_s, r2_s, in_sems, out_sems,
):
    seq_len, width = n2_ref.shape
    hidden = wg_ref.shape[1]
    length, z = info_ref[0], info_ref[1]
    step = gate_s.shape[1]
    shard = width // 4
    slices = shard_slices(z, shard)
    got_gain, got_wg, got_wu, got_wd = copies(
        (gain_hbm, wg_hbm, wu_hbm, wd_hbm), (gain_ref, wg_ref, wu_ref, wd_ref), in_sems
    )

    def fetch(refs):
        return [
            pltpu.make_async_copy(
                ref.at[pl.ds(0, seq_len), :], cot_s.at[:, pl.ds(k * shard, shard)], in_sems.at[4 + k]
            )
            for k, ref in enumerate(refs)
        ]

    def start_cot(refs):
        for copy in fetch(refs):
            copy.start()

    assemble(z, (c0, c1, c2, c3, c4, c5, c6), start_cot)
    got_gain.wait()

    def normalise(refs):
        def norm(rows):
            ms = [ref[rows, :].astype(f32) for ref in refs]
            r2 = row_scale(sum(m * m for m in ms), width)
            r2_s[rows, :] = jnp.broadcast_to(r2, (ROWS, 128))
            inner_s[rows, :] = jnp.zeros((ROWS, 128), f32)
            for m, cols in zip(ms, slices):
                n2_ref[rows, cols] = (m * r2 * gain_ref[1:2, cols]).astype(bf16)

        row_loop(seq_len, ROWS, norm)

    assemble(z, (m0, m1, m1, m2, m3, m4, m5), normalise)
    for copy in fetch((c0, c1, c2, c3)) + [got_wg, got_wu, got_wd]:
        copy.wait()

    def mask(rows):
        slot = rows.start + lax.broadcasted_iota(jnp.int32, (ROWS, 1), 0)
        for k, cols in enumerate(slices):
            cot = cot_s[rows, k * shard : (k + 1) * shard].astype(f32)
            cotm_ref[rows, cols] = jnp.where(slot < length, cot, 0.0).astype(bf16)

    row_loop(seq_len, ROWS, mask)

    for j in range(0, hidden, step):
        gate_s[...] = dot(n2_ref[...], wg_ref[:, j : j + step])
        up_s[...] = dot(n2_ref[...], wu_ref[:, j : j + step])
        gh_s[...] = dot_t(cotm_ref[...], wd_ref[j : j + step, :])

        def elementwise(rows):
            gate, up, gh = gate_s[rows, :], up_s[rows, :], gh_s[rows, :]
            sig = jax.nn.sigmoid(gate)
            silu = gate * sig
            hid_ref[rows, j : j + step] = (silu * up).astype(bf16)
            dg = (gh * up * (sig * (1.0 + gate * (1.0 - sig)))).astype(bf16)
            du = (gh * silu).astype(bf16)
            dgu_ref[rows, j : j + step] = dg
            dgu_ref[rows, hidden + j : hidden + j + step] = du
            inner = jnp.sum(dg.astype(f32) * gate + du.astype(f32) * up, axis=1, keepdims=True)
            inner_s[rows, :] += jnp.broadcast_to(inner, (ROWS, 128))

        row_loop(seq_len, ROWS, elementwise)

    sent = copies(
        (n2_ref, cotm_ref, hid_ref, dgu_ref), (n2_hbm, cotm_hbm, hid_hbm, dgu_hbm), out_sems
    )
    for part_ref, cols in zip((p_across, p_far, p_pair, p_own), slices):
        gate_s[...] = dot_t(dgu_ref[:, 0:hidden], wg_ref[cols, :]) + dot_t(
            dgu_ref[:, hidden : 2 * hidden], wu_ref[cols, :]
        )
        norm_back(gate_s, n2_ref, r2_s, inner_s, gain_ref[1:2, cols], part_ref, cols, width, gfg_ref)
    for copy in sent:
        copy.wait()


def share(grads_s, core, keep_hbm, give_hbm, sems):
    return copies(
        (grads_s.at[pl.ds(core * 4, 4)], grads_s.at[pl.ds((1 - core) * 4, 4)]), (keep_hbm, give_hbm), sems
    )


def ffn_grad_kernel(
    info_ref, n2_hbm, dgu_hbm, hid_hbm, cotm_hbm, wd_hbm,
    p_across, p_far, p_pair, p_own, keep_hbm, give_hbm,
    n2_ref, dgu_ref, hid_ref, cotm_ref, wd_ref, grads_ref, in_sems, out_sems,
):
    pending = copies(
        (n2_hbm, dgu_hbm, hid_hbm, cotm_hbm, wd_hbm), (n2_ref, dgu_ref, hid_ref, cotm_ref, wd_ref), in_sems
    )
    width, hidden = n2_ref.shape[1], hid_ref.shape[1]
    upper, lower = width // 8, hidden // 8
    rest = upper - lower
    pending[0].wait()
    pending[1].wait()
    for c in range(0, 2 * hidden, 256):
        grad = t_dot(n2_ref[...], dgu_ref[:, c : c + 256])
        for d in range(8):
            grads_ref[d, :, c : c + 256] = grad[d * upper : (d + 1) * upper].astype(bf16)
    for copy in pending[2:]:
        copy.wait()
    for c in range(0, width, 256):
        grad = t_dot(hid_ref[...], cotm_ref[:, c : c + 256])
        for d in range(8):
            block = grad[d * lower : (d + 1) * lower].astype(bf16)
            if c < hidden:
                grads_ref[d, 0:lower, 2 * hidden + c : 2 * hidden + c + 256] = block
            else:
                for k in range(lower // rest):
                    col = 2 * hidden + k * 256
                    grads_ref[d, lower:upper, col : col + 256] = block[k * rest : (k + 1) * rest]
    sent = share(grads_ref, info_ref[3], keep_hbm, give_hbm, out_sems)
    for part_ref, cols in zip((p_across, p_far, p_pair, p_own), shard_slices(info_ref[1], p_own.shape[1])):
        part_ref[...] = dot(hid_ref[...], wd_ref[:, cols]).astype(bf16)
    for copy in sent:
        copy.wait()


def halves_kernel(
    info_ref, keep_hbm, other_hbm, on_x, to_x, on_y, to_y, keep_on_x, keep_x, keep_on_y, keep_y, keep_ref, other_ref, sems
):
    for copy in copies((keep_hbm, other_hbm), (keep_ref, other_ref), sems):
        copy.wait()
    cols = to_x.shape[1]
    for out_ref, first, flip in (
        (on_x, 0, 3), (to_x, 0, 1), (keep_on_x, 0, 2), (keep_x, 0, 0),
        (on_y, cols, 3), (to_y, cols, 2), (keep_on_y, cols, 1), (keep_y, cols, 0),
    ):
        block = jnp.bitwise_xor(info_ref[2], flip)
        out_ref[...] = (
            keep_ref[block, :, first : first + cols].astype(f32) + other_ref[block, :, first : first + cols].astype(f32)
        ).astype(bf16)


def pass_kernel(info_ref, keep_on_x, got_on_x, keep_on_y, got_on_y, to_y, to_x):
    to_y[...] = (keep_on_x[...].astype(f32) + got_on_x[...].astype(f32)).astype(bf16)
    to_x[...] = (keep_on_y[...].astype(f32) + got_on_y[...].astype(f32)).astype(bf16)


def join_kernel(info_ref, keep_x, got_x, from_y, keep_y, got_y, from_x, left_ref, right_ref):
    left_ref[...] = (keep_x[...].astype(f32) + (got_x[...].astype(f32) + from_y[...].astype(f32))).astype(bf16)
    right_ref[...] = (keep_y[...].astype(f32) + (got_y[...].astype(f32) + from_x[...].astype(f32))).astype(bf16)


def unpack_ffn_kernel(info_ref, *refs):
    q, core = info_ref[2], info_ref[3]
    gate_ref, up_ref, down_ref = refs[8:]
    width, hidden = gate_ref.shape
    upper, lower = width // 8, hidden // 8
    rest = upper - lower
    cols = 3 * hidden // 2
    first = 2 * hidden - cols
    for half, (lefts, lefts_x, rights, rights_y) in ((core, refs[0:4]), (1 - core, refs[4:8])):
        for k in range(4):
            block = half * 4 + jnp.bitwise_xor(q, k)
            left, i = (lefts if k in (0, 2) else lefts_x), (0 if k in (0, 1) else 1)
            right, j = (rights if k in (0, 1) else rights_y), (0 if k in (0, 2) else 1)
            rows = pl.ds(pl.multiple_of(block * upper, upper), upper)
            gate_ref[rows, :] = left[i, :, 0:hidden].astype(f32)
            up_ref[rows, 0 : cols - hidden] = left[i, :, hidden:cols].astype(f32)
            up_ref[rows, cols - hidden : hidden] = right[j, :, 0:first].astype(f32)
            rows = pl.ds(pl.multiple_of(block * lower, lower), lower)
            down_ref[rows, 0:hidden] = right[j, 0:lower, first : first + hidden].astype(f32)
            for n in range(lower // rest):
                rows = pl.ds(pl.multiple_of(block * lower + n * rest, rest), rest)
                col = first + n * 256
                down_ref[rows, hidden:width] = right[j, lower:upper, col : col + 256].astype(f32)


def attn_backward_kernel(
    info_ref, g0, g1, g2, g3, g4, g5, qg_ref, kg_ref, wo_hbm, qrot_hbm, krot_hbm, val_hbm, mixed_hbm, lse_hbm,
    cos_hbm, sin_hbm, qpre_hbm, kpre_hbm, n1_hbm, wq_hbm, wk_hbm, wv_hbm, r1_hbm, gain_hbm,
    p_across, p_far, p_pair, p_own, gag_ref, qgg_ref, kgg_ref, keep_hbm, give_hbm,
    wo_ref, qrot_ref, krot_ref, val_ref, mixed_ref, lse_ref, cos_ref, sin_ref, qpre_ref, kpre_ref, n1_ref,
    wq_ref, wk_ref, wv_ref, r1_ref, gain_ref,
    ga_ref, gm_s, dq_s, dk_s, dv_s, dqkv_ref, inner_ref, acc_s, grads_ref, sems, out_sems,
):
    seq_len, width = ga_ref.shape
    hd = qg_ref.shape[1]
    qw, kw = qpre_ref.shape[1], kpre_ref.shape[1]
    heads, kvs = qw // hd, kw // hd
    group = heads // kvs
    length, z = info_ref[0], info_ref[1]
    scale = hd ** (-0.5)
    slices = shard_slices(z, width // 4)
    pending = copies(
        (
            wo_hbm, qrot_hbm, krot_hbm, val_hbm, mixed_hbm, lse_hbm, cos_hbm, sin_hbm, qpre_hbm, kpre_hbm, n1_hbm,
            wq_hbm, wk_hbm, wv_hbm, r1_hbm, gain_hbm,
        ),
        (
            wo_ref, qrot_ref, krot_ref, val_ref, mixed_ref, lse_ref, cos_ref, sin_ref, qpre_ref, kpre_ref, n1_ref,
            wq_ref, wk_ref, wv_ref, r1_ref, gain_ref,
        ),
        sems,
    )

    def collect(refs):
        for ref, cols in zip(refs, slices):
            ga_ref[:, cols] = ref[...]

    assemble(z, (g0, g1, g1, g2, g3, g4, g5), collect)

    pending[0].wait()
    for c in range(0, qw, 256):
        gm_s[:, c : c + 256] = dot_t(ga_ref[...], wo_ref[c : c + 256, :]).astype(bf16)
    dk_s[...] = jnp.zeros_like(dk_s)
    dv_s[...] = jnp.zeros_like(dv_s)
    for copy in pending[1:6]:
        copy.wait()

    for start, rows, keys in query_units(seq_len):
        bias = key_bias(length, keys)
        for g in range(kvs):
            first = g * group
            cols = slice(g * hd, (g + 1) * hd)
            key, val = krot_ref[0:keys, cols], val_ref[0:keys, cols]

            def stacked(ref):
                return jnp.concatenate(
                    [ref[start : start + rows, h * hd : (h + 1) * hd] for h in range(first, first + group)], axis=0
                )

            q, gm, mixed = stacked(qrot_ref), stacked(gm_s), stacked(mixed_ref)
            lse = jnp.concatenate(
                [lse_ref[start : start + rows, h : h + 1] for h in range(first, first + group)], axis=0
            )
            p = jnp.exp2(dot_t(q, key) * (scale * LOG2E) + bias - lse)
            delta = jnp.sum(gm.astype(f32) * mixed.astype(f32), axis=1, keepdims=True)
            ds = (p * (dot_t(gm, val) - delta)).astype(bf16)
            dv_s[0:keys, cols] += t_dot(p.astype(bf16), gm)
            dk_s[0:keys, cols] += t_dot(ds, q)
            dq = dot(ds, key)
            for r in range(group):
                h = first + r
                dq_s[start : start + rows, h * hd : (h + 1) * hd] = dq[r * rows : (r + 1) * rows]

    for copy in pending[6:]:
        copy.wait()
    ones = jnp.full((hd, hd), 1.0 / hd, bf16)

    def unrotate(rows, rot_s, pre_ref, g_ref, count, base, gain_sum):
        cos, sin = cos_ref[rows, :], sin_ref[rows, :]
        inner = jnp.zeros((ROWS, hd), f32)
        for c in range(0, count, hd):
            g = rot_s[rows, c : c + hd] * scale
            u = g * cos + pltpu.roll(g * sin, hd // 2, 1)
            v = pre_ref[rows, c : c + hd]
            r = lax.rsqrt(dot((v * v).astype(bf16), ones) + NORM_EPSILON)
            unit = v * r
            t = u * unit
            gain_sum = gain_sum + jnp.sum(t.reshape(ROWS // 8, 8, hd), axis=0)
            mean = dot((t * g_ref[...]).astype(bf16), ones)
            dqkv_ref[rows, base + c : base + c + hd] = (r * (u * g_ref[...] - unit * mean)).astype(bf16)
            inner = inner + (hd * NORM_EPSILON) * (r * r * mean)
        return inner, gain_sum

    qgs = kgs = jnp.zeros((8, hd), f32)
    for start in range(0, seq_len, ROWS):
        rows = pl.ds(start, ROWS)
        qi, qgs = unrotate(rows, dq_s, qpre_ref, qg_ref, qw, 0, qgs)
        ki, kgs = unrotate(rows, dk_s, kpre_ref, kg_ref, kw, qw, kgs)
        dv = dv_s[rows, :].astype(bf16)
        dqkv_ref[rows, qw + kw : qw + 2 * kw] = dv
        vi = jnp.sum(dv.astype(f32) * val_ref[rows, :].astype(f32), axis=1, keepdims=True)
        inner_ref[rows, :] = qi + ki + vi
    qgg_ref[...] = qgs
    kgg_ref[...] = kgs

    upper, lower = width // 8, qw // 8
    for c in range(0, width, 256):
        grad = t_dot(n1_ref[...], dqkv_ref[:, c : c + 256])
        out = t_dot(mixed_ref[...], ga_ref[:, c : c + 256])
        for d in range(8):
            grads_ref[d, 0:upper, c : c + 256] = grad[d * upper : (d + 1) * upper].astype(bf16)
            grads_ref[d, upper : upper + lower, c : c + 256] = out[d * lower : (d + 1) * lower].astype(bf16)
    sent = share(grads_ref, info_ref[3], keep_hbm, give_hbm, out_sems)
    for part_ref, cols in zip((p_across, p_far, p_pair, p_own), slices):
        acc_s[...] = (
            dot_t(dqkv_ref[:, 0:qw], wq_ref[cols, :])
            + dot_t(dqkv_ref[:, qw : qw + kw], wk_ref[cols, :])
            + dot_t(dqkv_ref[:, qw + kw : qw + 2 * kw], wv_ref[cols, :])
        )
        norm_back(acc_s, n1_ref, r1_ref, inner_ref, gain_ref[0:1, cols], part_ref, cols, width, gag_ref)
    for copy in sent:
        copy.wait()


def output_kernel(info_ref, middle_ref, attn_ref, own_ref, pair_ref, across_ref, out_ref, sums_ref):
    seq_len, shard = middle_ref.shape
    length = info_ref[0]
    sums = [jnp.zeros((8, shard), f32)] * 3
    for start in range(0, seq_len, ROWS):
        rows = pl.ds(start, ROWS)
        ffn = own_ref[rows, :].astype(f32) + (pair_ref[rows, :].astype(f32) + across_ref[rows, :].astype(f32))
        out = middle_ref[rows, :] + ffn
        out_ref[rows, :] = out.astype(bf16)
        slot = start + lax.broadcasted_iota(jnp.int32, (ROWS, 1), 0)
        for i, v in enumerate((out, attn_ref[rows, :], ffn)):
            v = jnp.where(slot < length, v, 0.0)
            sums[i] = sums[i] + jnp.sum((v * v).reshape(ROWS // 8, 8, shard), axis=0)
    for i in range(3):
        sums_ref[i : i + 1, :] = jnp.sum(sums[i], axis=0, keepdims=True)


def small_kernel(info_ref, gag_ref, gfg_ref, qgg_ref, kgg_ref, sums_ref, small_ref):
    hd, shard = qgg_ref.shape[1], sums_ref.shape[1]
    small_ref[...] = jnp.zeros(small_ref.shape, f32)
    small_ref[0:1, :] = jnp.sum(gag_ref[...], axis=0, keepdims=True)
    small_ref[1:2, :] = jnp.sum(gfg_ref[...], axis=0, keepdims=True)
    small_ref[2:3, 0:hd] = jnp.sum(qgg_ref[...], axis=0, keepdims=True)
    small_ref[2:3, hd : 2 * hd] = jnp.sum(kgg_ref[...], axis=0, keepdims=True)
    lane = lax.broadcasted_iota(jnp.int32, (1, 128), 1)
    totals = (info_ref[0] * shard).astype(f32) * (lane == 3).astype(f32)
    for i in range(3):
        totals = totals + jnp.sum(sums_ref[i : i + 1, :], axis=1, keepdims=True) * (lane == i).astype(f32)
    small_ref[2:3, 2 * hd : 2 * hd + 128] = totals


def block_kernel(info_ref, keep_x, got_x, from_y, keep_y, got_y, from_x, small_ref, left_ref, right_ref):
    rows, cols = keep_x.shape
    small = small_ref[...]
    high = small.astype(bf16)
    tail = jnp.concatenate([high, (small - high.astype(f32)).astype(bf16)], axis=0)
    for a, b, c, out_ref, first in ((keep_x, got_x, from_y, left_ref, 0), (keep_y, got_y, from_x, right_ref, cols)):
        out_ref[0:rows, :] = (a[...].astype(f32) + (b[...].astype(f32) + c[...].astype(f32))).astype(bf16)
        out_ref[rows : rows + TAIL, :] = tail[:, first : first + cols]


def unpack_kernel(info_ref, *refs):
    q, core = info_ref[2], info_ref[3]
    gq_ref, gk_ref, gv_ref, go_ref, ag_ref, fg_ref, qg_ref, kg_ref, rms_ref, small_ref = refs[8:]
    cols, kw = gq_ref.shape[1], gk_ref.shape[1]
    upper, lower = gq_ref.shape[0] // 8, go_ref.shape[0] // 8
    for half, (lefts, lefts_x, rights, rights_y) in ((core, refs[0:4]), (1 - core, refs[4:8])):
        for k in range(4):
            block = half * 4 + jnp.bitwise_xor(q, k)
            left, i = (lefts if k in (0, 2) else lefts_x), (0 if k in (0, 1) else 1)
            right, j = (rights if k in (0, 1) else rights_y), (0 if k in (0, 2) else 1)
            rows = pl.ds(pl.multiple_of(block * upper, upper), upper)
            gq_ref[rows, :] = left[i, 0:upper, :].astype(f32)
            gk_ref[rows, :] = right[j, 0:upper, 0:kw].astype(f32)
            gv_ref[rows, :] = right[j, 0:upper, kw : 2 * kw].astype(f32)
            rows = pl.ds(pl.multiple_of(block * lower, lower), lower)
            go_ref[rows, 0:cols] = left[i, upper : upper + lower, :].astype(f32)
            go_ref[rows, cols : 2 * cols] = right[j, upper : upper + lower, :].astype(f32)
    for first, group in ((0, (0, 1, 4, 5)), (cols, (2, 3, 6, 7))):
        total = jnp.zeros((8, cols), f32)
        for n in group:
            for i in range(2):
                tail = refs[n][i, upper + lower : upper + lower + TAIL, :].astype(f32)
                total = total + (tail[0:8] + tail[8:16])
        small_ref[:, first : first + cols] = total
    shard, hd = ag_ref.shape[1], qg_ref.shape[1]
    mine = pl.ds(pl.multiple_of(info_ref[1] * shard, shard), shard)
    ag_ref[...] = small_ref[0:1, mine]
    fg_ref[...] = small_ref[1:2, mine]
    qg_ref[...] = small_ref[2:3, 0:hd]
    kg_ref[...] = small_ref[2:3, hd : 2 * hd]
    totals = small_ref[2:3, 2 * hd : 2 * hd + 128]
    lane = lax.broadcasted_iota(jnp.int32, (1, 128), 1)
    count = jnp.sum(jnp.where(lane == 3, totals, 0.0), axis=1, keepdims=True)
    rms_ref[...] = jnp.sqrt(totals / count)


SPECS = {
    "s": pl.BlockSpec(memory_space=pltpu.SMEM),
    "v": pl.BlockSpec(memory_space=pltpu.VMEM),
    "a": pl.BlockSpec(memory_space=pl.ANY),
}


def call(body, outs, args, scratch=(), sems=(), flops=0, bytes_accessed=0, limit=SMALL_BYTES):
    places, arrays = [], []
    for place, *group in args:
        places += [place] * len(group)
        arrays += group
    return pl.pallas_call(
        body,
        out_shape=[jax.ShapeDtypeStruct(s, d) for s, d, _ in outs],
        in_specs=[SPECS[p] for p in places],
        out_specs=[SPECS[p] for _, _, p in outs],
        scratch_shapes=[pltpu.VMEM(s, d) for s, d in scratch] + [pltpu.SemaphoreType.DMA((n,)) for n in sems],
        compiler_params=pltpu.CompilerParams(vmem_limit_bytes=limit),
        cost_estimate=pl.CostEstimate(flops=flops, bytes_accessed=bytes_accessed, transcendentals=0),
    )(*arrays)


PAIRS = ((0, 1), (1, 0), (2, 3), (3, 2))
MIDDLE = ((1, 2), (2, 1))
OUTWARD = ((1, 0), (2, 3))
INWARD = ((0, 1), (3, 2))
OUTWARD_TWO = ((2, 0), (1, 3))
INWARD_TWO = ((0, 2), (3, 1))


def send(rows, pairs):
    return lax.ppermute(rows, "tensor", pairs)


def hold(*values):
    return lax.optimization_barrier(values)


def gather_line(own):
    pair = send(own, PAIRS)
    across_mid = send(own, MIDDLE)
    far_end = send(pair, OUTWARD_TWO)
    far_mid = send(pair, MIDDLE)
    across_end = send(across_mid, OUTWARD)
    return own, pair, across_mid, across_end, far_mid, far_end


def pick(end, from_end, from_middle):
    return jnp.where(end, from_end, from_middle)


def scatter_first(parts):
    across, far, _, _ = parts
    return send(far, INWARD_TWO), send(far, MIDDLE), send(across, INWARD)


def scatter_last(parts, first):
    across, _, pair, own = parts
    two, three, one = first
    to_pair = (pair.astype(f32) + (two.astype(f32) + three.astype(f32))).astype(bf16)
    to_across = (across.astype(f32) + one.astype(f32)).astype(bf16)
    return own, send(to_pair, PAIRS), send(to_across, MIDDLE)


def add(a, b):
    return (a.astype(f32) + b.astype(f32)).astype(bf16)


def total(terms):
    own, pair, across = terms
    return own.astype(f32) + (pair.astype(f32) + across.astype(f32))


def swap(values, bit):
    return lax.ppermute(values, "dp", [(i, i ^ bit) for i in range(8)])


def halve(keep, other, info):
    _, rows, width = keep.shape
    return call(
        halves_kernel,
        [((rows, width // 2), bf16, "v")] * 8,
        (("s", info), ("a", keep, other)),
        scratch=[((4, rows, width), bf16)] * 2,
        sems=(2,),
    )


def pass_on(keep_on_x, got_on_x, keep_on_y, got_on_y, info):
    return call(
        pass_kernel, [(keep_on_x.shape, bf16, "v")] * 2, (("s", info), ("v", keep_on_x, got_on_x, keep_on_y, got_on_y))
    )


def per_device(
    hidden_in, lengths, w_query, w_key, w_value, w_out, attn_gain, ffn_gain,
    query_gain, key_gain, w_gate, w_up, w_down, cotangent,
):
    seq_len, shard = hidden_in.shape
    width = w_query.shape[0]
    hd = query_gain.shape[0]
    qw, kw = w_query.shape[1], w_key.shape[1]
    hidden = w_gate.shape[1]
    padded = -(-seq_len // BLOCK) * BLOCK
    z = lax.axis_index("tensor").astype(jnp.int32)
    dp = lax.axis_index("dp").astype(jnp.int32)
    chips = lax.axis_size("dp") == 8
    q, core = (dp // 2, dp % 2) if chips else (0 * dp, 0 * dp)
    info = jnp.stack([lengths[0], z, q, core])
    parts = [((seq_len, shard), bf16, "v")] * 4

    end = (z == 0) | (z == 3)
    x = call(
        pack_kernel,
        [((seq_len + TAIL, shard), bf16, "v")],
        (("s", lengths), ("v", hidden_in, attn_gain[None], ffn_gain[None])),
    )[0]
    cot = jnp.concatenate([cotangent, jnp.zeros((TAIL, shard), bf16)], axis=0)
    x_pair, x_mid = send(x, PAIRS), send(x, MIDDLE)
    x_pair, x_mid, cot = hold(x_pair, x_mid, cot)
    x_end, x_far = send(pick(end, cot, x_mid), PAIRS), send(x_pair, MIDDLE)
    x_end, x_far, cot = hold(x_end, x_far, cot)
    x_last, cot_far = send(x_far, OUTWARD), send(x_end, MIDDLE)
    x_last, cot_far, x_end, cot = hold(x_last, cot_far, x_end, cot)
    cot_mid, cot_pair, cot_last = send(cot, MIDDLE), send(cot, OUTWARD), send(cot_far, OUTWARD)
    cos, sin = rope_tables(seq_len, hd)
    qg, kg = query_gain[None], key_gain[None]
    resid = hidden_in.astype(f32)
    valid = (jnp.arange(seq_len, dtype=jnp.int32) < lengths[0]).astype(f32)[:, None]

    saved = [
        ((seq_len, width), bf16), ((seq_len, qw), f32), ((seq_len, kw), f32), ((seq_len, qw), bf16),
        ((padded, kw), bf16), ((padded, kw), bf16), ((seq_len, qw), bf16), ((seq_len, 128), f32),
        ((seq_len, 128), f32), ((8, width), f32),
    ]
    weights = [((width, kw), bf16), ((width, kw), bf16), ((width, qw), bf16), ((qw, width), bf16)]
    tables = [((seq_len, hd), f32)] * 2
    *attn_parts, n1, qpre, kpre, qrot, krot, val, mixed, lse, r1, gain = call(
        attn_forward_kernel,
        parts + [(s, d, "a") for s, d in saved],
        (
            ("s", info), ("v", x, x_pair, x_mid, x_end, x_far, x_last, qg, kg),
            ("a", w_key, cos, sin, w_value, w_query, w_out),
        ),
        scratch=weights[:1] + tables + weights[1:] + saved,
        sems=(6, 10),
        limit=FULL_BYTES,
        flops=2 * seq_len * width * (2 * qw + 2 * kw) + 4 * seq_len * seq_len * qw,
        bytes_accessed=14_000_000,
    )
    attn_parts, cot_mid, cot_pair, cot_last = hold(attn_parts, cot_mid, cot_pair, cot_last)
    across, far, pair, own = attn_parts
    two = send(far, INWARD_TWO)
    one, three = hold(pick(end, across, cot_mid[:seq_len]), far)
    three, one = send(three, MIDDLE), send(one, PAIRS)
    zero_end = pick(end, jnp.zeros_like(one), one)
    pair = lax.optimization_barrier(pair.astype(f32) + two.astype(f32))
    attn_local = total(scatter_last((across, far, pair, own), (jnp.zeros_like(two), three, zero_end)))
    middle = resid + attn_local
    shard_two, one = hold(middle.astype(bf16), one)
    m_parts = gather_line(shard_two)

    kept = [((seq_len, width), bf16), ((seq_len, width), bf16), ((seq_len, hidden), bf16), ((seq_len, 2 * hidden), bf16)]
    *ffn_parts, gfg, n2, cotm, hid, dgu = call(
        ffn_kernel,
        parts + [((8, width), f32, "v")] + [(s, d, "a") for s, d in kept],
        (
            ("s", info), ("v", *m_parts), ("a", gain, w_gate, w_up, w_down),
            ("a", cot, x_end, cot_pair, cot_mid, one, cot_far, cot_last),
        ),
        scratch=[((8, width), f32)] + [((width, hidden), bf16)] * 2 + [((hidden, width), bf16), ((seq_len, width), bf16)]
        + kept + [((seq_len, 256), f32)] * 3 + [((seq_len, 128), f32)] * 2,
        sems=(8, 4),
        limit=VMEM_BYTES,
        flops=2 * seq_len * width * hidden * 5,
        bytes_accessed=16_000_000,
    )
    grad_top = cotangent.astype(f32) * valid
    first = scatter_first(ffn_parts)
    blocks = ((4, width // 8, 3 * hidden), bf16, "a")
    *down_parts, ffn_keep, ffn_give = call(
        ffn_grad_kernel,
        parts + [blocks] * 2,
        (("s", info), ("a", n2, dgu, hid, cotm, w_down)),
        scratch=[kept[0], kept[3], kept[2], kept[1], ((hidden, width), bf16), ((8, width // 8, 3 * hidden), bf16)],
        sems=(5, 2),
        limit=VMEM_BYTES,
        flops=2 * seq_len * width * hidden * 4,
        bytes_accessed=14_000_000,
    )
    first, ffn_keep, ffn_give = hold(first, ffn_keep, ffn_give)
    back = scatter_last(ffn_parts, first)
    if chips:
        ffn_other = swap(ffn_give, 1)
        halves = halve(ffn_keep, ffn_other, info)
        back, halves = hold(back, halves)
        on_x, to_x, on_y, to_y, keep_on_x, keep_x, keep_on_y, keep_y = halves
    grad_middle = grad_top + total(back)
    ga = grad_middle.astype(bf16)
    across, far, pair, own = down_parts
    ga_pair, ga_mid = send(ga, PAIRS), send(ga, MIDDLE)
    if chips:
        got_on_x, got_on_y = swap(on_x, 2), swap(on_y, 4)
        got_x, got_y = swap(to_x, 2), swap(to_y, 4)
        to_y, to_x = pass_on(keep_on_x, got_on_x, keep_on_y, got_on_y, info)
        ga_pair, ga_mid, far, to_y, to_x = hold(ga_pair, ga_mid, far, to_y, to_x)
        from_y, from_x = swap(to_y, 4), swap(to_x, 2)
    ga_end, ga_far = send(pick(end, far, ga_mid), PAIRS), send(ga_pair, MIDDLE)
    if chips:
        left, right = call(
            join_kernel,
            [((width // 8, 3 * hidden // 2), bf16, "v")] * 2,
            (("s", info), ("v", keep_x, got_x, from_y, keep_y, got_y, from_x)),
        )
        ga_end, ga_far, across, left, right = hold(ga_end, ga_far, across, left, right)
        left_y, right_x = swap(left, 4), swap(right, 2)
    ga_last = send(pick(end, across, ga_far), PAIRS)
    got_far = send(add(far, ga_end), MIDDLE)
    if chips:
        ga_last, got_far, left_y, right_x = hold(ga_last, got_far, left_y, right_x)
        lefts, rights = jnp.stack([left, left_y]), jnp.stack([right, right_x])
        lefts_x, rights_y = swap(lefts, 2), swap(rights, 4)
    ga_parts = (ga, ga_pair, ga_mid, ga_end, ga_far, ga_last)
    ffn_terms = (own, send(add(pair, got_far), PAIRS), send(add(across, ga_last), MIDDLE))

    blocks = (4, (width + qw) // 8, width)
    *back_parts, gag, qgg, kgg, keep, give = call(
        attn_backward_kernel,
        parts + [((8, width), f32, "v"), ((8, hd), f32, "v"), ((8, hd), f32, "v"), (blocks, bf16, "a"), (blocks, bf16, "a")],
        (
            ("s", info), ("v", *ga_parts, qg, kg),
            ("a", w_out, qrot, krot, val, mixed, lse, cos, sin, qpre, kpre, n1, w_query, w_key, w_value, r1, gain),
        ),
        scratch=[weights[3], saved[3], saved[4], saved[5], saved[6], saved[7], *tables, saved[1], saved[2], saved[0]]
        + [weights[2], weights[0], weights[1], saved[8], saved[9]]
        + [((seq_len, width), bf16), ((seq_len, qw), bf16), ((seq_len, qw), f32), ((padded, kw), f32), ((padded, kw), f32)]
        + [((seq_len, qw + 2 * kw), bf16), ((seq_len, 128), f32), ((seq_len, shard), f32), ((8, *blocks[1:]), bf16)],
        sems=(16, 2),
        limit=VMEM_BYTES,
        flops=2 * seq_len * width * (4 * qw + 4 * kw) + 10 * seq_len * seq_len * qw,
        bytes_accessed=20_000_000,
    )
    across, far, pair, own = back_parts
    if chips:
        far, ffn_terms, keep, give, lefts_x, rights_y = hold(far, ffn_terms, keep, give, lefts_x, rights_y)
        other = swap(give, 1)
    out_rows, sums = call(
        output_kernel,
        [((seq_len, shard), bf16, "v"), ((8, shard), f32, "v")],
        (("s", info), ("v", middle, attn_local, *ffn_terms)),
        bytes_accessed=2_000_000,
    )
    small = call(small_kernel, [((8, width), f32, "v")], (("s", info), ("v", gag, gfg, qgg, kgg, sums)))[0]
    shapes = [(width, qw), (width, kw), (width, kw), (qw, width)]
    if chips:
        other, small = hold(other, small)
        on_x, to_x, on_y, to_y, keep_on_x, keep_x, keep_on_y, keep_y = halve(keep, other, info)
        got_on_x, got_on_y = swap(on_x, 2), swap(on_y, 4)
        got_x, got_y = swap(to_x, 2), swap(to_y, 4)
        small = small + send(small, PAIRS)
        small = small + send(small, ((0, 2), (2, 0), (1, 3), (3, 1)))
        to_y, to_x = pass_on(keep_on_x, got_on_x, keep_on_y, got_on_y, info)
        to_y, to_x, small, far, across = hold(to_y, to_x, small, far, across)
        from_y, from_x, two = swap(to_y, 4), swap(to_x, 2), send(far, INWARD_TWO)
        late_left, late_right = call(
            block_kernel,
            [((keep_x.shape[0] + TAIL, keep_x.shape[1]), bf16, "v")] * 2,
            (("s", info), ("v", keep_x, got_x, from_y, keep_y, got_y, from_x, small)),
        )
        late_left, late_right, far, across = hold(late_left, late_right, far, across)
        three, one = send(far, MIDDLE), send(across, INWARD)
        left_y, right_x, two, three, one = hold(swap(late_left, 4), swap(late_right, 2), two, three, one)
        late_lefts, late_rights = jnp.stack([late_left, left_y]), jnp.stack([late_right, right_x])
        back_terms = scatter_last((across, far, pair, own), (two, three, one))
        ffn_halves = (lefts, lefts_x, rights, rights_y)
        g_gate, g_up, g_down = call(
            unpack_ffn_kernel,
            [(s, f32, "v") for s in ((width, hidden), (width, hidden), (hidden, width))],
            (("s", info), ("v", *ffn_halves, *[swap(b, 1) for b in ffn_halves])),
            bytes_accessed=14_000_000,
        )
        late = (late_lefts, swap(late_lefts, 2), late_rights, swap(late_rights, 4))
        late, back_terms, g_gate, g_up, g_down = hold(late, back_terms, g_gate, g_up, g_down)
        everyone = [*late, *[swap(b, 1) for b in late]]
        gq, gk, gv, go, ag, fg, qgg, kgg, rms = call(
            unpack_kernel,
            [(s, f32, "v") for s in shapes + [(1, shard), (1, shard), (1, hd), (1, hd), (1, 128)]],
            (("s", info), ("v", *everyone)),
            scratch=[((8, width), f32)],
            bytes_accessed=9_000_000,
        )
    else:
        back_terms = scatter_last(back_parts, scatter_first(back_parts))
        grads, ffn_grads = lax.psum((jnp.concatenate([keep, give]), jnp.concatenate([ffn_keep, ffn_give])), "dp")
        small = lax.psum(small, ("dp", "tensor"))
        ag, fg = [lax.dynamic_slice(small, (i, z * shard), (1, shard)) for i in (0, 1)]
        qgg, kgg = small[2:3, :hd], small[2:3, hd : 2 * hd]
        totals = small[2:3, 2 * hd : 2 * hd + 4]
        rms = jnp.sqrt(totals / totals[:, 3:])
        g_qkv = grads[:, : width // 8].reshape(width, width).astype(f32)
        gq, gk, gv = g_qkv[:, :qw], g_qkv[:, qw : qw + kw], g_qkv[:, qw + kw :]
        go = grads[:, width // 8 :].reshape(qw, width).astype(f32)
        g_gate = ffn_grads[:, :, :hidden].reshape(width, hidden).astype(f32)
        g_up = ffn_grads[:, :, hidden : 2 * hidden].reshape(width, hidden).astype(f32)
        folded = ffn_grads[:, :, 2 * hidden :]
        lower = hidden // 8
        tail = folded[:, lower:].reshape(8, width // 8 - lower, -1, 256).transpose(0, 2, 1, 3).reshape(8, lower, 256)
        g_down = jnp.concatenate([folded[:, :lower], tail], axis=2).reshape(hidden, width).astype(f32)
    input_grad = (grad_middle + total(back_terms)).astype(bf16)
    return (
        out_rows,
        input_grad,
        gq,
        gk,
        gv,
        go,
        ag[0],
        fg[0],
        qgg[0],
        kgg[0],
        g_gate,
        g_up,
        g_down,
        rms[0, :3],
    )


def solution(mesh):
    rows, cols, first = P("dp", "tensor"), P(None, "tensor"), P("tensor", None)
    gain = P("tensor")
    return jax.shard_map(
        per_device,
        mesh=mesh,
        in_specs=(rows, P("dp"), cols, cols, cols, first, gain, gain, P(), P(), cols, cols, first, rows),
        out_specs=(rows, rows, cols, cols, cols, first, gain, gain, P(), P(), cols, cols, first, P()),
        check_vma=False,
    )
```

```python
import functools

import jax
import jax.numpy as jnp
from jax import lax
from jax.experimental import pallas as pl
from jax.experimental.pallas import tpu as pltpu
from jax.sharding import PartitionSpec as P

BLOCK = 256
NORM_EPSILON = 1e-06
ROPE_THETA = 1000000.0
LOG2E = 1.4426950408889634
NEG = -1e30
ROWS = 64
TAIL = 16
FULL_BYTES = 60 * 1024 * 1024
VMEM_BYTES = 40 * 1024 * 1024
SMALL_BYTES = 24 * 1024 * 1024

bf16 = jnp.bfloat16
f32 = jnp.float32


def dot(a, b):
    return jnp.dot(a, b, preferred_element_type=f32)


def dot_t(a, b):
    return lax.dot_general(a, b, (((1,), (1,)), ((), ())), preferred_element_type=f32)


def t_dot(a, b):
    return lax.dot_general(a, b, (((0,), (0,)), ((), ())), preferred_element_type=f32)


def row_loop(count, step, body):
    for start in range(0, count, step):
        body(pl.ds(start, step))


def rolled(count, step, body):
    def run(i, carry):
        body(pl.multiple_of(i * step, step))
        return carry

    lax.fori_loop(0, count // step, run, 0)


def cos_sin(angles):
    turns = jnp.round(angles * (1.0 / 6.283185307179586))
    rest = ((angles - turns * 6.28125) - turns * 0.0019350051879882812) - turns * 3.019916050733e-7
    square = rest * rest
    cos, sin = jnp.ones_like(rest), jnp.ones_like(rest)
    for n in range(8, 0, -1):
        cos = 1.0 - cos * (square * (1.0 / ((2 * n - 1) * (2 * n))))
        sin = 1.0 - sin * (square * (1.0 / ((2 * n) * (2 * n + 1))))
    return cos, rest * sin


def rope_tables(length, width):
    half_width = width // 2
    frequency = ROPE_THETA ** (-(jnp.arange(half_width, dtype=f32) * (2.0 / width)))
    cos, sin = cos_sin(jnp.arange(length, dtype=f32)[:, None] * frequency[None, :])
    return jnp.concatenate([cos, cos], axis=1), jnp.concatenate([-sin, sin], axis=1)


def query_units(seq_len):
    units = []
    start = 0
    while start < seq_len:
        rows = min(128, seq_len - start)
        keys = (start // BLOCK + 1) * BLOCK
        units.append((start, rows, keys))
        start += rows
    return units


def roles(z):
    low = z < 2
    return jnp.where(low, 2, 1), jnp.where(low, 3, 0), z + 1 - 2 * lax.rem(z, 2), z


def shard_slices(z, width):
    return [pl.ds(pl.multiple_of(shard * width, width), width) for shard in roles(z)]


def assemble(z, pieces, body):
    own, pair_mid, pair_end, across_mid, across_end, far_mid, far_end = pieces
    end = (z == 0) | (z == 3)

    @pl.when(end)
    def _():
        body((across_end, far_end, pair_end, own))

    @pl.when(jnp.logical_not(end))
    def _():
        body((across_mid, far_mid, pair_mid, own))


def key_bias(length, keys):
    slot = lax.broadcasted_iota(jnp.int32, (1, keys), 1)
    return jnp.where(slot < length, 0.0, NEG).astype(f32)


def row_scale(squares, width):
    return lax.rsqrt(jnp.sum(squares, axis=1, keepdims=True) * (1.0 / width) + NORM_EPSILON)


def pack_kernel(info_ref, x_ref, ag_ref, fg_ref, out_ref):
    seq_len, shard = x_ref.shape
    out_ref[0:seq_len, :] = x_ref[...]
    gains = jnp.concatenate([ag_ref[...], fg_ref[...], jnp.zeros((6, shard), f32)], axis=0)
    high = gains.astype(bf16)
    out_ref[seq_len : seq_len + TAIL, :] = jnp.concatenate([high, (gains - high.astype(f32)).astype(bf16)], axis=0)


def copies(sources, targets, sems):
    pending = [pltpu.make_async_copy(a, b, sems.at[i]) for i, (a, b) in enumerate(zip(sources, targets))]
    for copy in pending:
        copy.start()
    return pending


def attn_forward_kernel(
    info_ref, x0, x1, x2, x3, x4, x5, qg_ref, kg_ref, wk_hbm, cos_hbm, sin_hbm, wv_hbm, wq_hbm, wo_hbm,
    p_across, p_far, p_pair, p_own, n1_hbm, qpre_hbm, kpre_hbm, qrot_hbm, krot_hbm, val_hbm, mixed_hbm, lse_hbm,
    r1_hbm, gain_hbm,
    wk_ref, cos_ref, sin_ref, wv_ref, wq_ref, wo_ref, n1_ref, qpre_ref, kpre_ref, qrot_ref, krot_ref, val_ref,
    mixed_ref, lse_ref, r1_ref, gain_ref, in_sems, out_sems,
):
    seq_len, width = n1_ref.shape
    hd = qg_ref.shape[1]
    heads = wq_ref.shape[1] // hd
    kvs = wk_ref.shape[1] // hd
    group = heads // kvs
    padded = krot_ref.shape[0]
    length, z = info_ref[0], info_ref[1]
    scale = hd ** (-0.5) * LOG2E
    slices = shard_slices(z, width // 4)
    pending = copies(
        (wk_hbm, cos_hbm, sin_hbm, wv_hbm, wq_hbm, wo_hbm), (wk_ref, cos_ref, sin_ref, wv_ref, wq_ref, wo_ref), in_sems
    )
    sent = []

    def put(source, target):
        copy = pltpu.make_async_copy(source, target, out_sems.at[len(sent)])
        copy.start()
        sent.append(copy)

    def normalise(refs):
        for ref, cols in zip(refs, slices):
            tail = ref[seq_len : seq_len + TAIL, :].astype(f32)
            gain_ref[:, cols] = tail[0:8] + tail[8:16]

        def norm(rows):
            xs = [ref[rows, :].astype(f32) for ref in refs]
            r1 = row_scale(sum(x * x for x in xs), width)
            r1_ref[rows, :] = jnp.broadcast_to(r1, (ROWS, 128))
            for x, cols in zip(xs, slices):
                n1_ref[rows, cols] = (x * r1 * gain_ref[0:1, cols]).astype(bf16)

        row_loop(seq_len, ROWS, norm)

    assemble(z, (x0, x1, x1, x2, x3, x4, x5), normalise)
    put(n1_ref, n1_hbm)
    put(r1_ref, r1_hbm)
    put(gain_ref, gain_hbm)

    def project(w_ref, pre_ref, rot_ref, g_ref):
        count = w_ref.shape[1]
        for c in range(0, count, 2 * hd):
            pre_ref[:, c : c + 2 * hd] = dot(n1_ref[...], w_ref[:, c : c + 2 * hd])

        def rotate(rows):
            cos, sin = cos_ref[rows, :], sin_ref[rows, :]
            for c in range(0, count, hd):
                v = pre_ref[rows, c : c + hd]
                v = v * row_scale(v * v, hd) * g_ref[...]
                rot_ref[rows, c : c + hd] = (v * cos + pltpu.roll(v, hd // 2, 1) * sin).astype(bf16)

        row_loop(seq_len, ROWS, rotate)

    for copy in pending:
        copy.wait()
    project(wk_ref, kpre_ref, krot_ref, kg_ref)
    val_ref[0:seq_len, :] = dot(n1_ref[...], wv_ref[...]).astype(bf16)
    if padded > seq_len:
        krot_ref[seq_len:padded, :] = jnp.zeros((padded - seq_len, kvs * hd), bf16)
        val_ref[seq_len:padded, :] = jnp.zeros((padded - seq_len, kvs * hd), bf16)
    put(kpre_ref, kpre_hbm)
    put(krot_ref, krot_hbm)
    put(val_ref, val_hbm)
    project(wq_ref, qpre_ref, qrot_ref, qg_ref)
    put(qpre_ref, qpre_hbm)
    put(qrot_ref, qrot_hbm)

    for start, rows, keys in query_units(seq_len):
        bias = key_bias(length, keys)
        for g in range(kvs):
            key = krot_ref[0:keys, g * hd : (g + 1) * hd]
            val = val_ref[0:keys, g * hd : (g + 1) * hd]
            first = g * group
            q = jnp.concatenate(
                [qrot_ref[start : start + rows, h * hd : (h + 1) * hd] for h in range(first, first + group)], axis=0
            )
            e = jnp.exp2(dot_t(q, key) * scale + bias)
            total = jnp.sum(e, axis=1, keepdims=True)
            mixed = dot(e.astype(bf16), val) * (1.0 / total)
            lse = jnp.log2(total)
            for r in range(group):
                h = first + r
                mixed_ref[start : start + rows, h * hd : (h + 1) * hd] = mixed[r * rows : (r + 1) * rows].astype(bf16)
                lse_ref[start : start + rows, h : h + 1] = lse[r * rows : (r + 1) * rows]

    put(mixed_ref, mixed_hbm)
    put(lse_ref, lse_hbm)
    for part_ref, cols in zip((p_across, p_far, p_pair, p_own), slices):
        part_ref[...] = dot(mixed_ref[...], wo_ref[:, cols]).astype(part_ref.dtype)
    for copy in sent:
        copy.wait()


def wide(column, width):
    return jnp.concatenate([column] * (width // column.shape[1]), axis=1)


def norm_back(grad_s, normed_ref, scale_ref, inner_s, gain, part_ref, cols, width, gain_grad_ref=None):
    seq_len, step = grad_s.shape
    inverse = 1.0 / gain
    total = jnp.zeros((8, step), f32)
    for start in range(0, seq_len, ROWS):
        rows = pl.ds(start, ROWS)
        grad = grad_s[rows, :]
        unit = normed_ref[rows, cols].astype(f32) * inverse
        coef = wide(inner_s[rows, :] * (1.0 / width), step)
        part_ref[rows, :] = (wide(scale_ref[rows, :], step) * (grad * gain - unit * coef)).astype(part_ref.dtype)
        if gain_grad_ref is not None:
            total = total + jnp.sum((grad * unit).reshape(ROWS // 8, 8, step), axis=0)
    if gain_grad_ref is not None:
        gain_grad_ref[:, cols] = total


def ffn_kernel(
    info_ref, m0, m1, m2, m3, m4, m5, gain_hbm, wg_hbm, wu_hbm, wd_hbm, c0, c1, c2, c3, c4, c5, c6,
    p_across, p_far, p_pair, p_own, gfg_ref, n2_hbm, cotm_hbm, hid_hbm, dgu_hbm,
    gain_ref, wg_ref, wu_ref, wd_ref, cot_s, n2_ref, cotm_ref, hid_ref, dgu_ref,
    gate_s, up_s, gh_s, inner_s, r2_s, in_sems, out_sems,
):
    seq_len, width = n2_ref.shape
    hidden = wg_ref.shape[1]
    length, z = info_ref[0], info_ref[1]
    step = gate_s.shape[1]
    shard = width // 4
    slices = shard_slices(z, shard)
    got_gain, got_wg, got_wu, got_wd = copies(
        (gain_hbm, wg_hbm, wu_hbm, wd_hbm), (gain_ref, wg_ref, wu_ref, wd_ref), in_sems
    )

    def fetch(refs):
        return [
            pltpu.make_async_copy(
                ref.at[pl.ds(0, seq_len), :], cot_s.at[:, pl.ds(k * shard, shard)], in_sems.at[4 + k]
            )
            for k, ref in enumerate(refs)
        ]

    def start_cot(refs):
        for copy in fetch(refs):
            copy.start()

    assemble(z, (c0, c1, c2, c3, c4, c5, c6), start_cot)
    got_gain.wait()

    def normalise(refs):
        def norm(rows):
            ms = [ref[rows, :].astype(f32) for ref in refs]
            r2 = row_scale(sum(m * m for m in ms), width)
            r2_s[rows, :] = jnp.broadcast_to(r2, (ROWS, 128))
            inner_s[rows, :] = jnp.zeros((ROWS, 128), f32)
            for m, cols in zip(ms, slices):
                n2_ref[rows, cols] = (m * r2 * gain_ref[1:2, cols]).astype(bf16)

        row_loop(seq_len, ROWS, norm)

    assemble(z, (m0, m1, m1, m2, m3, m4, m5), normalise)
    for copy in fetch((c0, c1, c2, c3)) + [got_wg, got_wu, got_wd]:
        copy.wait()

    def mask(rows):
        slot = rows.start + lax.broadcasted_iota(jnp.int32, (ROWS, 1), 0)
        for k, cols in enumerate(slices):
            cot = cot_s[rows, k * shard : (k + 1) * shard].astype(f32)
            cotm_ref[rows, cols] = jnp.where(slot < length, cot, 0.0).astype(bf16)

    row_loop(seq_len, ROWS, mask)

    for j in range(0, hidden, step):
        gate_s[...] = dot(n2_ref[...], wg_ref[:, j : j + step])
        up_s[...] = dot(n2_ref[...], wu_ref[:, j : j + step])
        gh_s[...] = dot_t(cotm_ref[...], wd_ref[j : j + step, :])

        def elementwise(rows):
            gate, up, gh = gate_s[rows, :], up_s[rows, :], gh_s[rows, :]
            sig = jax.nn.sigmoid(gate)
            silu = gate * sig
            hid_ref[rows, j : j + step] = (silu * up).astype(bf16)
            dg = (gh * up * (sig * (1.0 + gate * (1.0 - sig)))).astype(bf16)
            du = (gh * silu).astype(bf16)
            dgu_ref[rows, j : j + step] = dg
            dgu_ref[rows, hidden + j : hidden + j + step] = du
            inner = jnp.sum(dg.astype(f32) * gate + du.astype(f32) * up, axis=1, keepdims=True)
            inner_s[rows, :] += jnp.broadcast_to(inner, (ROWS, 128))

        row_loop(seq_len, ROWS, elementwise)

    sent = copies(
        (n2_ref, cotm_ref, hid_ref, dgu_ref), (n2_hbm, cotm_hbm, hid_hbm, dgu_hbm), out_sems
    )
    for part_ref, cols in zip((p_across, p_far, p_pair, p_own), slices):
        gate_s[...] = dot_t(dgu_ref[:, 0:hidden], wg_ref[cols, :]) + dot_t(
            dgu_ref[:, hidden : 2 * hidden], wu_ref[cols, :]
        )
        norm_back(gate_s, n2_ref, r2_s, inner_s, gain_ref[1:2, cols], part_ref, cols, width, gfg_ref)
    for copy in sent:
        copy.wait()


def share(grads_s, core, keep_hbm, give_hbm, sems):
    return copies(
        (grads_s.at[pl.ds(core * 4, 4)], grads_s.at[pl.ds((1 - core) * 4, 4)]), (keep_hbm, give_hbm), sems
    )


def ffn_grad_kernel(
    info_ref, n2_hbm, dgu_hbm, hid_hbm, cotm_hbm, wd_hbm,
    p_across, p_far, p_pair, p_own, keep_hbm, give_hbm,
    n2_ref, dgu_ref, hid_ref, cotm_ref, wd_ref, grads_ref, in_sems, out_sems,
):
    pending = copies(
        (n2_hbm, dgu_hbm, hid_hbm, cotm_hbm, wd_hbm), (n2_ref, dgu_ref, hid_ref, cotm_ref, wd_ref), in_sems
    )
    width, hidden = n2_ref.shape[1], hid_ref.shape[1]
    upper, lower = width // 8, hidden // 8
    rest = upper - lower
    pending[0].wait()
    pending[1].wait()
    def gate_up(c):
        cols = pl.ds(c, 256)
        grad = t_dot(n2_ref[...], dgu_ref[:, cols])
        for d in range(8):
            grads_ref[d, :, cols] = grad[d * upper : (d + 1) * upper].astype(bf16)

    rolled(2 * hidden, 256, gate_up)
    for copy in pending[2:]:
        copy.wait()

    def down(c):
        grad = t_dot(hid_ref[...], cotm_ref[:, pl.ds(c, 256)])
        cols = pl.ds(pl.multiple_of(2 * hidden + c, 256), 256)
        for d in range(8):
            grads_ref[d, 0:lower, cols] = grad[d * lower : (d + 1) * lower].astype(bf16)

    rolled(hidden, 256, down)
    grad = t_dot(hid_ref[...], cotm_ref[:, hidden:width])
    for d in range(8):
        for k in range(lower // rest):
            block = grad[d * lower + k * rest : d * lower + (k + 1) * rest].astype(bf16)
            col = 2 * hidden + k * 256
            grads_ref[d, lower:upper, col : col + 256] = block
    sent = share(grads_ref, info_ref[3], keep_hbm, give_hbm, out_sems)
    for part_ref, cols in zip((p_across, p_far, p_pair, p_own), shard_slices(info_ref[1], p_own.shape[1])):
        part_ref[...] = dot(hid_ref[...], wd_ref[:, cols]).astype(bf16)
    for copy in sent:
        copy.wait()


def halves_kernel(
    info_ref, keep_hbm, other_hbm, on_x, to_x, on_y, to_y, keep_on_x, keep_x, keep_on_y, keep_y, keep_ref, other_ref, sems
):
    for copy in copies((keep_hbm, other_hbm), (keep_ref, other_ref), sems):
        copy.wait()
    cols = to_x.shape[1]
    for out_ref, first, flip in (
        (on_x, 0, 3), (to_x, 0, 1), (keep_on_x, 0, 2), (keep_x, 0, 0),
        (on_y, cols, 3), (to_y, cols, 2), (keep_on_y, cols, 1), (keep_y, cols, 0),
    ):
        block = jnp.bitwise_xor(info_ref[2], flip)
        out_ref[...] = (
            keep_ref[block, :, first : first + cols].astype(f32) + other_ref[block, :, first : first + cols].astype(f32)
        ).astype(bf16)


def pass_kernel(info_ref, keep_on_x, got_on_x, keep_on_y, got_on_y, to_y, to_x):
    to_y[...] = (keep_on_x[...].astype(f32) + got_on_x[...].astype(f32)).astype(bf16)
    to_x[...] = (keep_on_y[...].astype(f32) + got_on_y[...].astype(f32)).astype(bf16)


def join_kernel(info_ref, keep_x, got_x, from_y, keep_y, got_y, from_x, left_ref, right_ref):
    left_ref[...] = (keep_x[...].astype(f32) + (got_x[...].astype(f32) + from_y[...].astype(f32))).astype(bf16)
    right_ref[...] = (keep_y[...].astype(f32) + (got_y[...].astype(f32) + from_x[...].astype(f32))).astype(bf16)


def unpack_ffn_kernel(info_ref, *refs):
    q, core = info_ref[2], info_ref[3]
    gate_ref, up_ref, down_ref = refs[8:]
    width, hidden = gate_ref.shape
    upper, lower = width // 8, hidden // 8
    rest = upper - lower
    cols = 3 * hidden // 2
    first = 2 * hidden - cols
    step = 32
    for half, (lefts, lefts_x, rights, rights_y) in ((core, refs[0:4]), (1 - core, refs[4:8])):
        for k in range(4):
            block = half * 4 + jnp.bitwise_xor(q, k)
            left, i = (lefts if k in (0, 2) else lefts_x), (0 if k in (0, 1) else 1)
            right, j = (rights if k in (0, 1) else rights_y), (0 if k in (0, 2) else 1)

            def gate_up(start):
                here = pl.ds(start, step)
                rows = pl.ds(pl.multiple_of(block * upper + start, step), step)
                gate_ref[rows, :] = left[i, here, 0:hidden].astype(f32)
                up_ref[rows, 0 : cols - hidden] = left[i, here, hidden:cols].astype(f32)
                up_ref[rows, cols - hidden : hidden] = right[j, here, 0:first].astype(f32)

            def down(start):
                rows = pl.ds(pl.multiple_of(block * lower + start, step), step)
                down_ref[rows, 0:hidden] = right[j, pl.ds(start, step), first : first + hidden].astype(f32)

            rolled(upper, step, gate_up)
            rolled(lower, step, down)
            for n in range(lower // rest):
                rows = pl.ds(pl.multiple_of(block * lower + n * rest, rest), rest)
                col = first + n * 256
                down_ref[rows, hidden:width] = right[j, lower:upper, col : col + 256].astype(f32)


def attn_backward_kernel(
    info_ref, g0, g1, g2, g3, g4, g5, qg_ref, kg_ref, wo_hbm, qrot_hbm, krot_hbm, val_hbm, mixed_hbm, lse_hbm,
    cos_hbm, sin_hbm, qpre_hbm, kpre_hbm, n1_hbm, wq_hbm, wk_hbm, wv_hbm, r1_hbm, gain_hbm,
    p_across, p_far, p_pair, p_own, gag_ref, qgg_ref, kgg_ref, keep_hbm, give_hbm,
    wo_ref, qrot_ref, krot_ref, val_ref, mixed_ref, lse_ref, cos_ref, sin_ref, qpre_ref, kpre_ref, n1_ref,
    wq_ref, wk_ref, wv_ref, r1_ref, gain_ref,
    ga_ref, gm_s, dq_s, dk_s, dv_s, dqkv_ref, inner_ref, acc_s, grads_ref, sems, out_sems,
):
    seq_len, width = ga_ref.shape
    hd = qg_ref.shape[1]
    qw, kw = qpre_ref.shape[1], kpre_ref.shape[1]
    heads, kvs = qw // hd, kw // hd
    group = heads // kvs
    length, z = info_ref[0], info_ref[1]
    scale = hd ** (-0.5)
    slices = shard_slices(z, width // 4)
    pending = copies(
        (
            wo_hbm, qrot_hbm, krot_hbm, val_hbm, mixed_hbm, lse_hbm, cos_hbm, sin_hbm, qpre_hbm, kpre_hbm, n1_hbm,
            wq_hbm, wk_hbm, wv_hbm, r1_hbm, gain_hbm,
        ),
        (
            wo_ref, qrot_ref, krot_ref, val_ref, mixed_ref, lse_ref, cos_ref, sin_ref, qpre_ref, kpre_ref, n1_ref,
            wq_ref, wk_ref, wv_ref, r1_ref, gain_ref,
        ),
        sems,
    )

    def collect(refs):
        for ref, cols in zip(refs, slices):
            ga_ref[:, cols] = ref[...]

    assemble(z, (g0, g1, g1, g2, g3, g4, g5), collect)

    pending[0].wait()
    for c in range(0, qw, 256):
        gm_s[:, c : c + 256] = dot_t(ga_ref[...], wo_ref[c : c + 256, :]).astype(bf16)
    dk_s[...] = jnp.zeros_like(dk_s)
    dv_s[...] = jnp.zeros_like(dv_s)
    for copy in pending[1:6]:
        copy.wait()

    def head_group(offset):
        cols = pl.ds(offset, hd)
        heads_here = [pl.ds(pl.multiple_of(offset * group + r * hd, hd), hd) for r in range(group)]
        for start, rows, keys in query_units(seq_len):
            bias = key_bias(length, keys)
            key, val = krot_ref[0:keys, cols], val_ref[0:keys, cols]

            def stacked(ref):
                return jnp.concatenate([ref[start : start + rows, h] for h in heads_here], axis=0)

            def lse_of(r):
                columns = [lse_ref[start : start + rows, g * group + r : g * group + r + 1] for g in range(kvs)]
                column = columns[0]
                for g in range(1, kvs):
                    column = jnp.where(offset == g * hd, columns[g], column)
                return column

            q, gm, mixed = stacked(qrot_ref), stacked(gm_s), stacked(mixed_ref)
            lse = jnp.concatenate([lse_of(r) for r in range(group)], axis=0)
            p = jnp.exp2(dot_t(q, key) * (scale * LOG2E) + bias - lse)
            delta = jnp.sum(gm.astype(f32) * mixed.astype(f32), axis=1, keepdims=True)
            ds = (p * (dot_t(gm, val) - delta)).astype(bf16)
            dv_s[0:keys, cols] += t_dot(p.astype(bf16), gm)
            dk_s[0:keys, cols] += t_dot(ds, q)
            dq = dot(ds, key)
            for r in range(group):
                dq_s[start : start + rows, heads_here[r]] = dq[r * rows : (r + 1) * rows]

    rolled(kw, hd, head_group)
    for copy in pending[6:]:
        copy.wait()
    ones = jnp.full((hd, hd), 1.0 / hd, bf16)

    def unrotate(rows, rot_s, pre_ref, g_ref, count, base, gain_sum):
        cos, sin = cos_ref[rows, :], sin_ref[rows, :]
        inner = jnp.zeros((ROWS, hd), f32)
        for c in range(0, count, hd):
            g = rot_s[rows, c : c + hd] * scale
            u = g * cos + pltpu.roll(g * sin, hd // 2, 1)
            v = pre_ref[rows, c : c + hd]
            r = lax.rsqrt(dot((v * v).astype(bf16), ones) + NORM_EPSILON)
            unit = v * r
            t = u * unit
            gain_sum = gain_sum + jnp.sum(t.reshape(ROWS // 8, 8, hd), axis=0)
            mean = dot((t * g_ref[...]).astype(bf16), ones)
            dqkv_ref[rows, base + c : base + c + hd] = (r * (u * g_ref[...] - unit * mean)).astype(bf16)
            inner = inner + (hd * NORM_EPSILON) * (r * r * mean)
        return inner, gain_sum

    qgs = kgs = jnp.zeros((8, hd), f32)
    for start in range(0, seq_len, ROWS):
        rows = pl.ds(start, ROWS)
        qi, qgs = unrotate(rows, dq_s, qpre_ref, qg_ref, qw, 0, qgs)
        ki, kgs = unrotate(rows, dk_s, kpre_ref, kg_ref, kw, qw, kgs)
        dv = dv_s[rows, :].astype(bf16)
        dqkv_ref[rows, qw + kw : qw + 2 * kw] = dv
        vi = jnp.sum(dv.astype(f32) * val_ref[rows, :].astype(f32), axis=1, keepdims=True)
        inner_ref[rows, :] = qi + ki + vi
    qgg_ref[...] = qgs
    kgg_ref[...] = kgs

    upper, lower = width // 8, qw // 8

    def weight_grads(c):
        cols = pl.ds(c, 256)
        grad = t_dot(n1_ref[...], dqkv_ref[:, cols])
        out = t_dot(mixed_ref[...], ga_ref[:, cols])
        for d in range(8):
            grads_ref[d, 0:upper, cols] = grad[d * upper : (d + 1) * upper].astype(bf16)
            grads_ref[d, upper : upper + lower, cols] = out[d * lower : (d + 1) * lower].astype(bf16)

    rolled(width, 256, weight_grads)
    sent = share(grads_ref, info_ref[3], keep_hbm, give_hbm, out_sems)
    for part_ref, cols in zip((p_across, p_far, p_pair, p_own), slices):
        acc_s[...] = (
            dot_t(dqkv_ref[:, 0:qw], wq_ref[cols, :])
            + dot_t(dqkv_ref[:, qw : qw + kw], wk_ref[cols, :])
            + dot_t(dqkv_ref[:, qw + kw : qw + 2 * kw], wv_ref[cols, :])
        )
        norm_back(acc_s, n1_ref, r1_ref, inner_ref, gain_ref[0:1, cols], part_ref, cols, width, gag_ref)
    for copy in sent:
        copy.wait()


def output_kernel(info_ref, middle_ref, attn_ref, own_ref, pair_ref, across_ref, out_ref, sums_ref):
    seq_len, shard = middle_ref.shape
    length = info_ref[0]
    sums = [jnp.zeros((8, shard), f32)] * 3
    for start in range(0, seq_len, ROWS):
        rows = pl.ds(start, ROWS)
        ffn = own_ref[rows, :].astype(f32) + (pair_ref[rows, :].astype(f32) + across_ref[rows, :].astype(f32))
        out = middle_ref[rows, :] + ffn
        out_ref[rows, :] = out.astype(bf16)
        slot = start + lax.broadcasted_iota(jnp.int32, (ROWS, 1), 0)
        for i, v in enumerate((out, attn_ref[rows, :], ffn)):
            v = jnp.where(slot < length, v, 0.0)
            sums[i] = sums[i] + jnp.sum((v * v).reshape(ROWS // 8, 8, shard), axis=0)
    for i in range(3):
        sums_ref[i : i + 1, :] = jnp.sum(sums[i], axis=0, keepdims=True)


def small_kernel(info_ref, gag_ref, gfg_ref, qgg_ref, kgg_ref, sums_ref, small_ref):
    hd, shard = qgg_ref.shape[1], sums_ref.shape[1]
    small_ref[...] = jnp.zeros(small_ref.shape, f32)
    small_ref[0:1, :] = jnp.sum(gag_ref[...], axis=0, keepdims=True)
    small_ref[1:2, :] = jnp.sum(gfg_ref[...], axis=0, keepdims=True)
    small_ref[2:3, 0:hd] = jnp.sum(qgg_ref[...], axis=0, keepdims=True)
    small_ref[2:3, hd : 2 * hd] = jnp.sum(kgg_ref[...], axis=0, keepdims=True)
    lane = lax.broadcasted_iota(jnp.int32, (1, 128), 1)
    totals = (info_ref[0] * shard).astype(f32) * (lane == 3).astype(f32)
    for i in range(3):
        totals = totals + jnp.sum(sums_ref[i : i + 1, :], axis=1, keepdims=True) * (lane == i).astype(f32)
    small_ref[2:3, 2 * hd : 2 * hd + 128] = totals


def block_kernel(info_ref, keep_x, got_x, from_y, keep_y, got_y, from_x, small_ref, left_ref, right_ref):
    rows, cols = keep_x.shape
    small = small_ref[...]
    high = small.astype(bf16)
    tail = jnp.concatenate([high, (small - high.astype(f32)).astype(bf16)], axis=0)
    for a, b, c, out_ref, first in ((keep_x, got_x, from_y, left_ref, 0), (keep_y, got_y, from_x, right_ref, cols)):
        out_ref[0:rows, :] = (a[...].astype(f32) + (b[...].astype(f32) + c[...].astype(f32))).astype(bf16)
        out_ref[rows : rows + TAIL, :] = tail[:, first : first + cols]


def unpack_kernel(info_ref, *refs):
    q, core = info_ref[2], info_ref[3]
    gq_ref, gk_ref, gv_ref, go_ref, ag_ref, fg_ref, qg_ref, kg_ref, rms_ref, small_ref = refs[8:]
    cols, kw = gq_ref.shape[1], gk_ref.shape[1]
    upper, lower = gq_ref.shape[0] // 8, go_ref.shape[0] // 8
    step = 32
    for half, (lefts, lefts_x, rights, rights_y) in ((core, refs[0:4]), (1 - core, refs[4:8])):
        for k in range(4):
            block = half * 4 + jnp.bitwise_xor(q, k)
            left, i = (lefts if k in (0, 2) else lefts_x), (0 if k in (0, 1) else 1)
            right, j = (rights if k in (0, 1) else rights_y), (0 if k in (0, 2) else 1)

            def qkv(start):
                here = pl.ds(start, step)
                rows = pl.ds(pl.multiple_of(block * upper + start, step), step)
                gq_ref[rows, :] = left[i, here, :].astype(f32)
                gk_ref[rows, :] = right[j, here, 0:kw].astype(f32)
                gv_ref[rows, :] = right[j, here, kw : 2 * kw].astype(f32)

            def out(start):
                here = pl.ds(pl.multiple_of(upper + start, step), step)
                rows = pl.ds(pl.multiple_of(block * lower + start, step), step)
                go_ref[rows, 0:cols] = left[i, here, :].astype(f32)
                go_ref[rows, cols : 2 * cols] = right[j, here, :].astype(f32)

            rolled(upper, step, qkv)
            rolled(lower, step, out)
    for first, group in ((0, (0, 1, 4, 5)), (cols, (2, 3, 6, 7))):
        total = jnp.zeros((8, cols), f32)
        for n in group:
            for i in range(2):
                tail = refs[n][i, upper + lower : upper + lower + TAIL, :].astype(f32)
                total = total + (tail[0:8] + tail[8:16])
        small_ref[:, first : first + cols] = total
    shard, hd = ag_ref.shape[1], qg_ref.shape[1]
    mine = pl.ds(pl.multiple_of(info_ref[1] * shard, shard), shard)
    ag_ref[...] = small_ref[0:1, mine]
    fg_ref[...] = small_ref[1:2, mine]
    qg_ref[...] = small_ref[2:3, 0:hd]
    kg_ref[...] = small_ref[2:3, hd : 2 * hd]
    totals = small_ref[2:3, 2 * hd : 2 * hd + 128]
    lane = lax.broadcasted_iota(jnp.int32, (1, 128), 1)
    count = jnp.sum(jnp.where(lane == 3, totals, 0.0), axis=1, keepdims=True)
    rms_ref[...] = jnp.sqrt(totals / count)


SPECS = {
    "s": pl.BlockSpec(memory_space=pltpu.SMEM),
    "v": pl.BlockSpec(memory_space=pltpu.VMEM),
    "a": pl.BlockSpec(memory_space=pl.ANY),
}


def call(body, outs, args, scratch=(), sems=(), flops=0, bytes_accessed=0, limit=SMALL_BYTES):
    places, arrays = [], []
    for place, *group in args:
        places += [place] * len(group)
        arrays += group
    return pl.pallas_call(
        body,
        out_shape=[jax.ShapeDtypeStruct(s, d) for s, d, _ in outs],
        in_specs=[SPECS[p] for p in places],
        out_specs=[SPECS[p] for _, _, p in outs],
        scratch_shapes=[pltpu.VMEM(s, d) for s, d in scratch] + [pltpu.SemaphoreType.DMA((n,)) for n in sems],
        compiler_params=pltpu.CompilerParams(vmem_limit_bytes=limit),
        cost_estimate=pl.CostEstimate(flops=flops, bytes_accessed=bytes_accessed, transcendentals=0),
    )(*arrays)


PAIRS = ((0, 1), (1, 0), (2, 3), (3, 2))
MIDDLE = ((1, 2), (2, 1))
OUTWARD = ((1, 0), (2, 3))
INWARD = ((0, 1), (3, 2))
OUTWARD_TWO = ((2, 0), (1, 3))
INWARD_TWO = ((0, 2), (3, 1))


def send(rows, pairs):
    return lax.ppermute(rows, "tensor", pairs)


def hold(*values):
    return lax.optimization_barrier(values)


def gather_line(own):
    pair = send(own, PAIRS)
    across_mid = send(own, MIDDLE)
    far_end = send(pair, OUTWARD_TWO)
    far_mid = send(pair, MIDDLE)
    across_end = send(across_mid, OUTWARD)
    return own, pair, across_mid, across_end, far_mid, far_end


def pick(end, from_end, from_middle):
    return jnp.where(end, from_end, from_middle)


def scatter_first(parts):
    across, far, _, _ = parts
    return send(far, INWARD_TWO), send(far, MIDDLE), send(across, INWARD)


def scatter_last(parts, first):
    across, _, pair, own = parts
    two, three, one = first
    to_pair = (pair.astype(f32) + (two.astype(f32) + three.astype(f32))).astype(bf16)
    to_across = (across.astype(f32) + one.astype(f32)).astype(bf16)
    return own, send(to_pair, PAIRS), send(to_across, MIDDLE)


def add(a, b):
    return (a.astype(f32) + b.astype(f32)).astype(bf16)


def total(terms):
    own, pair, across = terms
    return own.astype(f32) + (pair.astype(f32) + across.astype(f32))


def swap(values, bit):
    return lax.ppermute(values, "dp", [(i, i ^ bit) for i in range(8)])


def halve(keep, other, info):
    _, rows, width = keep.shape
    return call(
        halves_kernel,
        [((rows, width // 2), bf16, "v")] * 8,
        (("s", info), ("a", keep, other)),
        scratch=[((4, rows, width), bf16)] * 2,
        sems=(2,),
    )


def pass_on(keep_on_x, got_on_x, keep_on_y, got_on_y, info):
    return call(
        pass_kernel, [(keep_on_x.shape, bf16, "v")] * 2, (("s", info), ("v", keep_on_x, got_on_x, keep_on_y, got_on_y))
    )


def per_device(
    hidden_in, lengths, w_query, w_key, w_value, w_out, attn_gain, ffn_gain,
    query_gain, key_gain, w_gate, w_up, w_down, cotangent,
):
    seq_len, shard = hidden_in.shape
    width = w_query.shape[0]
    hd = query_gain.shape[0]
    qw, kw = w_query.shape[1], w_key.shape[1]
    hidden = w_gate.shape[1]
    padded = -(-seq_len // BLOCK) * BLOCK
    z = lax.axis_index("tensor").astype(jnp.int32)
    dp = lax.axis_index("dp").astype(jnp.int32)
    chips = lax.axis_size("dp") == 8
    q, core = (dp // 2, dp % 2) if chips else (0 * dp, 0 * dp)
    info = jnp.stack([lengths[0], z, q, core])
    parts = [((seq_len, shard), bf16, "v")] * 4

    end = (z == 0) | (z == 3)
    x = call(
        pack_kernel,
        [((seq_len + TAIL, shard), bf16, "v")],
        (("s", lengths), ("v", hidden_in, attn_gain[None], ffn_gain[None])),
    )[0]
    cot = jnp.concatenate([cotangent, jnp.zeros((TAIL, shard), bf16)], axis=0)
    x_pair, x_mid = send(x, PAIRS), send(x, MIDDLE)
    x_pair, x_mid, cot = hold(x_pair, x_mid, cot)
    x_end, x_far = send(pick(end, cot, x_mid), PAIRS), send(x_pair, MIDDLE)
    x_end, x_far, cot = hold(x_end, x_far, cot)
    x_last, cot_far = send(x_far, OUTWARD), send(x_end, MIDDLE)
    x_last, cot_far, x_end, cot = hold(x_last, cot_far, x_end, cot)
    cot_mid, cot_pair, cot_last = send(cot, MIDDLE), send(cot, OUTWARD), send(cot_far, OUTWARD)
    cos, sin = rope_tables(seq_len, hd)
    qg, kg = query_gain[None], key_gain[None]
    resid = hidden_in.astype(f32)
    valid = (jnp.arange(seq_len, dtype=jnp.int32) < lengths[0]).astype(f32)[:, None]

    saved = [
        ((seq_len, width), bf16), ((seq_len, qw), f32), ((seq_len, kw), f32), ((seq_len, qw), bf16),
        ((padded, kw), bf16), ((padded, kw), bf16), ((seq_len, qw), bf16), ((seq_len, 128), f32),
        ((seq_len, 128), f32), ((8, width), f32),
    ]
    weights = [((width, kw), bf16), ((width, kw), bf16), ((width, qw), bf16), ((qw, width), bf16)]
    tables = [((seq_len, hd), f32)] * 2
    *attn_parts, n1, qpre, kpre, qrot, krot, val, mixed, lse, r1, gain = call(
        attn_forward_kernel,
        parts + [(s, d, "a") for s, d in saved],
        (
            ("s", info), ("v", x, x_pair, x_mid, x_end, x_far, x_last, qg, kg),
            ("a", w_key, cos, sin, w_value, w_query, w_out),
        ),
        scratch=weights[:1] + tables + weights[1:] + saved,
        sems=(6, 10),
        limit=FULL_BYTES,
        flops=2 * seq_len * width * (2 * qw + 2 * kw) + 4 * seq_len * seq_len * qw,
        bytes_accessed=14_000_000,
    )
    attn_parts, cot_mid, cot_pair, cot_last = hold(attn_parts, cot_mid, cot_pair, cot_last)
    across, far, pair, own = attn_parts
    two = send(far, INWARD_TWO)
    one, three = hold(pick(end, across, cot_mid[:seq_len]), far)
    three, one = send(three, MIDDLE), send(one, PAIRS)
    zero_end = pick(end, jnp.zeros_like(one), one)
    pair = lax.optimization_barrier(pair.astype(f32) + two.astype(f32))
    attn_local = total(scatter_last((across, far, pair, own), (jnp.zeros_like(two), three, zero_end)))
    middle = resid + attn_local
    shard_two, one = hold(middle.astype(bf16), one)
    m_parts = gather_line(shard_two)

    kept = [((seq_len, width), bf16), ((seq_len, width), bf16), ((seq_len, hidden), bf16), ((seq_len, 2 * hidden), bf16)]
    *ffn_parts, gfg, n2, cotm, hid, dgu = call(
        ffn_kernel,
        parts + [((8, width), f32, "v")] + [(s, d, "a") for s, d in kept],
        (
            ("s", info), ("v", *m_parts), ("a", gain, w_gate, w_up, w_down),
            ("a", cot, x_end, cot_pair, cot_mid, one, cot_far, cot_last),
        ),
        scratch=[((8, width), f32)] + [((width, hidden), bf16)] * 2 + [((hidden, width), bf16), ((seq_len, width), bf16)]
        + kept + [((seq_len, 256), f32)] * 3 + [((seq_len, 128), f32)] * 2,
        sems=(8, 4),
        limit=VMEM_BYTES,
        flops=2 * seq_len * width * hidden * 5,
        bytes_accessed=16_000_000,
    )
    grad_top = cotangent.astype(f32) * valid
    first = scatter_first(ffn_parts)
    blocks = ((4, width // 8, 3 * hidden), bf16, "a")
    *down_parts, ffn_keep, ffn_give = call(
        ffn_grad_kernel,
        parts + [blocks] * 2,
        (("s", info), ("a", n2, dgu, hid, cotm, w_down)),
        scratch=[kept[0], kept[3], kept[2], kept[1], ((hidden, width), bf16), ((8, width // 8, 3 * hidden), bf16)],
        sems=(5, 2),
        limit=VMEM_BYTES,
        flops=2 * seq_len * width * hidden * 4,
        bytes_accessed=14_000_000,
    )
    first, ffn_keep, ffn_give = hold(first, ffn_keep, ffn_give)
    back = scatter_last(ffn_parts, first)
    if chips:
        ffn_other = swap(ffn_give, 1)
        halves = halve(ffn_keep, ffn_other, info)
        back, halves = hold(back, halves)
        on_x, to_x, on_y, to_y, keep_on_x, keep_x, keep_on_y, keep_y = halves
    grad_middle = grad_top + total(back)
    ga = grad_middle.astype(bf16)
    across, far, pair, own = down_parts
    ga_pair, ga_mid = send(ga, PAIRS), send(ga, MIDDLE)
    if chips:
        got_on_x, got_on_y = swap(on_x, 2), swap(on_y, 4)
        got_x, got_y = swap(to_x, 2), swap(to_y, 4)
        to_y, to_x = pass_on(keep_on_x, got_on_x, keep_on_y, got_on_y, info)
        ga_pair, ga_mid, far, to_y, to_x = hold(ga_pair, ga_mid, far, to_y, to_x)
        from_y, from_x = swap(to_y, 4), swap(to_x, 2)
    ga_end, ga_far = send(pick(end, far, ga_mid), PAIRS), send(ga_pair, MIDDLE)
    if chips:
        left, right = call(
            join_kernel,
            [((width // 8, 3 * hidden // 2), bf16, "v")] * 2,
            (("s", info), ("v", keep_x, got_x, from_y, keep_y, got_y, from_x)),
        )
        ga_end, ga_far, across, left, right = hold(ga_end, ga_far, across, left, right)
        left_y, right_x = swap(left, 4), swap(right, 2)
    ga_last = send(pick(end, across, ga_far), PAIRS)
    got_far = send(add(far, ga_end), MIDDLE)
    if chips:
        ga_last, got_far, left_y, right_x = hold(ga_last, got_far, left_y, right_x)
        lefts, rights = jnp.stack([left, left_y]), jnp.stack([right, right_x])
        lefts_x, rights_y = swap(lefts, 2), swap(rights, 4)
    ga_parts = (ga, ga_pair, ga_mid, ga_end, ga_far, ga_last)
    ffn_terms = (own, send(add(pair, got_far), PAIRS), send(add(across, ga_last), MIDDLE))

    blocks = (4, (width + qw) // 8, width)
    *back_parts, gag, qgg, kgg, keep, give = call(
        attn_backward_kernel,
        parts + [((8, width), f32, "v"), ((8, hd), f32, "v"), ((8, hd), f32, "v"), (blocks, bf16, "a"), (blocks, bf16, "a")],
        (
            ("s", info), ("v", *ga_parts, qg, kg),
            ("a", w_out, qrot, krot, val, mixed, lse, cos, sin, qpre, kpre, n1, w_query, w_key, w_value, r1, gain),
        ),
        scratch=[weights[3], saved[3], saved[4], saved[5], saved[6], saved[7], *tables, saved[1], saved[2], saved[0]]
        + [weights[2], weights[0], weights[1], saved[8], saved[9]]
        + [((seq_len, width), bf16), ((seq_len, qw), bf16), ((seq_len, qw), f32), ((padded, kw), f32), ((padded, kw), f32)]
        + [((seq_len, qw + 2 * kw), bf16), ((seq_len, 128), f32), ((seq_len, shard), f32), ((8, *blocks[1:]), bf16)],
        sems=(16, 2),
        limit=VMEM_BYTES,
        flops=2 * seq_len * width * (4 * qw + 4 * kw) + 10 * seq_len * seq_len * qw,
        bytes_accessed=20_000_000,
    )
    across, far, pair, own = back_parts
    if chips:
        far, ffn_terms, keep, give, lefts_x, rights_y = hold(far, ffn_terms, keep, give, lefts_x, rights_y)
        other = swap(give, 1)
    out_rows, sums = call(
        output_kernel,
        [((seq_len, shard), bf16, "v"), ((8, shard), f32, "v")],
        (("s", info), ("v", middle, attn_local, *ffn_terms)),
        bytes_accessed=2_000_000,
    )
    small = call(small_kernel, [((8, width), f32, "v")], (("s", info), ("v", gag, gfg, qgg, kgg, sums)))[0]
    shapes = [(width, qw), (width, kw), (width, kw), (qw, width)]
    if chips:
        other, small = hold(other, small)
        on_x, to_x, on_y, to_y, keep_on_x, keep_x, keep_on_y, keep_y = halve(keep, other, info)
        got_on_x, got_on_y = swap(on_x, 2), swap(on_y, 4)
        got_x, got_y = swap(to_x, 2), swap(to_y, 4)
        small = small + send(small, PAIRS)
        small = small + send(small, ((0, 2), (2, 0), (1, 3), (3, 1)))
        to_y, to_x = pass_on(keep_on_x, got_on_x, keep_on_y, got_on_y, info)
        to_y, to_x, small, far, across = hold(to_y, to_x, small, far, across)
        from_y, from_x, two = swap(to_y, 4), swap(to_x, 2), send(far, INWARD_TWO)
        late_left, late_right = call(
            block_kernel,
            [((keep_x.shape[0] + TAIL, keep_x.shape[1]), bf16, "v")] * 2,
            (("s", info), ("v", keep_x, got_x, from_y, keep_y, got_y, from_x, small)),
        )
        late_left, late_right, far, across = hold(late_left, late_right, far, across)
        three, one = send(far, MIDDLE), send(across, INWARD)
        left_y, right_x, two, three, one = hold(swap(late_left, 4), swap(late_right, 2), two, three, one)
        late_lefts, late_rights = jnp.stack([late_left, left_y]), jnp.stack([late_right, right_x])
        back_terms = scatter_last((across, far, pair, own), (two, three, one))
        ffn_halves = (lefts, lefts_x, rights, rights_y)
        g_gate, g_up, g_down = call(
            unpack_ffn_kernel,
            [(s, f32, "v") for s in ((width, hidden), (width, hidden), (hidden, width))],
            (("s", info), ("v", *ffn_halves, *[swap(b, 1) for b in ffn_halves])),
            bytes_accessed=14_000_000,
        )
        late = (late_lefts, swap(late_lefts, 2), late_rights, swap(late_rights, 4))
        late, back_terms, g_gate, g_up, g_down = hold(late, back_terms, g_gate, g_up, g_down)
        everyone = [*late, *[swap(b, 1) for b in late]]
        gq, gk, gv, go, ag, fg, qgg, kgg, rms = call(
            unpack_kernel,
            [(s, f32, "v") for s in shapes + [(1, shard), (1, shard), (1, hd), (1, hd), (1, 128)]],
            (("s", info), ("v", *everyone)),
            scratch=[((8, width), f32)],
            bytes_accessed=9_000_000,
        )
    else:
        back_terms = scatter_last(back_parts, scatter_first(back_parts))
        grads, ffn_grads = lax.psum((jnp.concatenate([keep, give]), jnp.concatenate([ffn_keep, ffn_give])), "dp")
        small = lax.psum(small, ("dp", "tensor"))
        ag, fg = [lax.dynamic_slice(small, (i, z * shard), (1, shard)) for i in (0, 1)]
        qgg, kgg = small[2:3, :hd], small[2:3, hd : 2 * hd]
        totals = small[2:3, 2 * hd : 2 * hd + 4]
        rms = jnp.sqrt(totals / totals[:, 3:])
        g_qkv = grads[:, : width // 8].reshape(width, width).astype(f32)
        gq, gk, gv = g_qkv[:, :qw], g_qkv[:, qw : qw + kw], g_qkv[:, qw + kw :]
        go = grads[:, width // 8 :].reshape(qw, width).astype(f32)
        g_gate = ffn_grads[:, :, :hidden].reshape(width, hidden).astype(f32)
        g_up = ffn_grads[:, :, hidden : 2 * hidden].reshape(width, hidden).astype(f32)
        folded = ffn_grads[:, :, 2 * hidden :]
        lower = hidden // 8
        tail = folded[:, lower:].reshape(8, width // 8 - lower, -1, 256).transpose(0, 2, 1, 3).reshape(8, lower, 256)
        g_down = jnp.concatenate([folded[:, :lower], tail], axis=2).reshape(hidden, width).astype(f32)
    input_grad = (grad_middle + total(back_terms)).astype(bf16)
    return (
        out_rows,
        input_grad,
        gq,
        gk,
        gv,
        go,
        ag[0],
        fg[0],
        qgg[0],
        kgg[0],
        g_gate,
        g_up,
        g_down,
        rms[0, :3],
    )


def solution(mesh):
    rows, cols, first = P("dp", "tensor"), P(None, "tensor"), P("tensor", None)
    gain = P("tensor")
    return jax.shard_map(
        per_device,
        mesh=mesh,
        in_specs=(rows, P("dp"), cols, cols, cols, first, gain, gain, P(), P(), cols, cols, first, rows),
        out_specs=(rows, rows, cols, cols, cols, first, gain, gain, P(), P(), cols, cols, first, P()),
        check_vma=False,
    )
```

```python
import functools

import jax
import jax.numpy as jnp
from jax import lax
from jax.experimental import pallas as pl
from jax.experimental.pallas import tpu as pltpu
from jax.sharding import PartitionSpec as P

BLOCK = 256
NORM_EPSILON = 1e-06
ROPE_THETA = 1000000.0
LOG2E = 1.4426950408889634
NEG = -1e30
ROWS = 64
TAIL = 16
FULL_BYTES = 60 * 1024 * 1024
VMEM_BYTES = 44 * 1024 * 1024
SMALL_BYTES = 24 * 1024 * 1024

bf16 = jnp.bfloat16
f32 = jnp.float32


def dot(a, b):
    return jnp.dot(a, b, preferred_element_type=f32)


def dot_t(a, b):
    return lax.dot_general(a, b, (((1,), (1,)), ((), ())), preferred_element_type=f32)


def t_dot(a, b):
    return lax.dot_general(a, b, (((0,), (0,)), ((), ())), preferred_element_type=f32)


def row_loop(count, step, body):
    for start in range(0, count, step):
        body(pl.ds(start, step))


def rope_tables(length, width):
    half_width = width // 2
    frequency = ROPE_THETA ** (-(jnp.arange(half_width, dtype=f32) * (2.0 / width)))
    angles = jnp.arange(length, dtype=f32)[:, None] * frequency[None, :]
    cos, sin = jnp.cos(angles), jnp.sin(angles)
    return jnp.concatenate([cos, cos], axis=1), jnp.concatenate([-sin, sin], axis=1)


def query_units(seq_len):
    units = []
    start = 0
    while start < seq_len:
        rows = min(128, seq_len - start)
        keys = (start // BLOCK + 1) * BLOCK
        units.append((start, rows, keys))
        start += rows
    return units


def roles(z):
    low = z < 2
    return jnp.where(low, 2, 1), jnp.where(low, 3, 0), z + 1 - 2 * lax.rem(z, 2), z


def shard_slices(z, width):
    return [pl.ds(pl.multiple_of(shard * width, width), width) for shard in roles(z)]


def assemble(z, pieces, body):
    own, pair_mid, pair_end, across_mid, across_end, far_mid, far_end = pieces
    end = (z == 0) | (z == 3)

    @pl.when(end)
    def _():
        body((across_end, far_end, pair_end, own))

    @pl.when(jnp.logical_not(end))
    def _():
        body((across_mid, far_mid, pair_mid, own))


def key_bias(length, keys):
    slot = lax.broadcasted_iota(jnp.int32, (1, keys), 1)
    return jnp.where(slot < length, 0.0, NEG).astype(f32)


def row_scale(squares, width):
    return lax.rsqrt(jnp.sum(squares, axis=1, keepdims=True) * (1.0 / width) + NORM_EPSILON)


def pack_kernel(info_ref, x_ref, ag_ref, fg_ref, out_ref):
    seq_len, shard = x_ref.shape
    out_ref[0:seq_len, :] = x_ref[...]
    gains = jnp.concatenate([ag_ref[...], fg_ref[...], jnp.zeros((6, shard), f32)], axis=0)
    high = gains.astype(bf16)
    out_ref[seq_len : seq_len + TAIL, :] = jnp.concatenate([high, (gains - high.astype(f32)).astype(bf16)], axis=0)


def copies(sources, targets, sems):
    pending = [pltpu.make_async_copy(a, b, sems.at[i]) for i, (a, b) in enumerate(zip(sources, targets))]
    for copy in pending:
        copy.start()
    return pending


def attn_forward_kernel(
    info_ref, x0, x1, x2, x3, x4, x5, qg_ref, kg_ref, wk_hbm, cos_hbm, sin_hbm, wv_hbm, wq_hbm, wo_hbm,
    p_across, p_far, p_pair, p_own, n1_hbm, qpre_hbm, kpre_hbm, qrot_hbm, krot_hbm, val_hbm, mixed_hbm, lse_hbm,
    r1_hbm, gain_hbm,
    wk_ref, cos_ref, sin_ref, wv_ref, wq_ref, wo_ref, n1_ref, qpre_ref, kpre_ref, qrot_ref, krot_ref, val_ref,
    mixed_ref, lse_ref, r1_ref, gain_ref, in_sems, out_sems,
):
    seq_len, width = n1_ref.shape
    hd = qg_ref.shape[1]
    heads = wq_ref.shape[1] // hd
    kvs = wk_ref.shape[1] // hd
    group = heads // kvs
    padded = krot_ref.shape[0]
    length, z = info_ref[0], info_ref[1]
    scale = hd ** (-0.5) * LOG2E
    slices = shard_slices(z, width // 4)
    pending = copies(
        (wk_hbm, cos_hbm, sin_hbm, wv_hbm, wq_hbm, wo_hbm), (wk_ref, cos_ref, sin_ref, wv_ref, wq_ref, wo_ref), in_sems
    )
    sent = []

    def put(source, target):
        copy = pltpu.make_async_copy(source, target, out_sems.at[len(sent)])
        copy.start()
        sent.append(copy)

    def normalise(refs):
        for ref, cols in zip(refs, slices):
            tail = ref[seq_len : seq_len + TAIL, :].astype(f32)
            gain_ref[:, cols] = tail[0:8] + tail[8:16]

        def norm(rows):
            xs = [ref[rows, :].astype(f32) for ref in refs]
            r1 = row_scale(sum(x * x for x in xs), width)
            r1_ref[rows, :] = jnp.broadcast_to(r1, (ROWS, 128))
            for x, cols in zip(xs, slices):
                n1_ref[rows, cols] = (x * r1 * gain_ref[0:1, cols]).astype(bf16)

        row_loop(seq_len, ROWS, norm)

    assemble(z, (x0, x1, x1, x2, x3, x4, x5), normalise)
    put(n1_ref, n1_hbm)
    put(r1_ref, r1_hbm)
    put(gain_ref, gain_hbm)

    def project(w_ref, pre_ref, rot_ref, g_ref):
        count = w_ref.shape[1]
        for c in range(0, count, 2 * hd):
            pre_ref[:, c : c + 2 * hd] = dot(n1_ref[...], w_ref[:, c : c + 2 * hd])

        def rotate(rows):
            cos, sin = cos_ref[rows, :], sin_ref[rows, :]
            for c in range(0, count, hd):
                v = pre_ref[rows, c : c + hd]
                v = v * row_scale(v * v, hd) * g_ref[...]
                rot_ref[rows, c : c + hd] = (v * cos + pltpu.roll(v, hd // 2, 1) * sin).astype(bf16)

        row_loop(seq_len, ROWS, rotate)

    for copy in pending:
        copy.wait()
    project(wk_ref, kpre_ref, krot_ref, kg_ref)
    val_ref[0:seq_len, :] = dot(n1_ref[...], wv_ref[...]).astype(bf16)
    if padded > seq_len:
        krot_ref[seq_len:padded, :] = jnp.zeros((padded - seq_len, kvs * hd), bf16)
        val_ref[seq_len:padded, :] = jnp.zeros((padded - seq_len, kvs * hd), bf16)
    put(kpre_ref, kpre_hbm)
    put(krot_ref, krot_hbm)
    put(val_ref, val_hbm)
    project(wq_ref, qpre_ref, qrot_ref, qg_ref)
    put(qpre_ref, qpre_hbm)
    put(qrot_ref, qrot_hbm)

    for start, rows, keys in query_units(seq_len):
        bias = key_bias(length, keys)
        for g in range(kvs):
            key = krot_ref[0:keys, g * hd : (g + 1) * hd]
            val = val_ref[0:keys, g * hd : (g + 1) * hd]
            first = g * group
            q = jnp.concatenate(
                [qrot_ref[start : start + rows, h * hd : (h + 1) * hd] for h in range(first, first + group)], axis=0
            )
            e = jnp.exp2(dot_t(q, key) * scale + bias)
            total = jnp.sum(e, axis=1, keepdims=True)
            mixed = dot(e.astype(bf16), val) * (1.0 / total)
            lse = jnp.log2(total)
            for r in range(group):
                h = first + r
                mixed_ref[start : start + rows, h * hd : (h + 1) * hd] = mixed[r * rows : (r + 1) * rows].astype(bf16)
                lse_ref[start : start + rows, h : h + 1] = lse[r * rows : (r + 1) * rows]

    put(mixed_ref, mixed_hbm)
    put(lse_ref, lse_hbm)
    for part_ref, cols in zip((p_across, p_far, p_pair, p_own), slices):
        part_ref[...] = dot(mixed_ref[...], wo_ref[:, cols]).astype(part_ref.dtype)
    for copy in sent:
        copy.wait()


def wide(column, width):
    return jnp.concatenate([column] * (width // column.shape[1]), axis=1)


def norm_back(grad_s, normed_ref, scale_ref, inner_s, gain, part_ref, cols, width, gain_grad_ref=None):
    seq_len, step = grad_s.shape
    inverse = 1.0 / gain
    total = jnp.zeros((8, step), f32)
    for start in range(0, seq_len, ROWS):
        rows = pl.ds(start, ROWS)
        grad = grad_s[rows, :]
        unit = normed_ref[rows, cols].astype(f32) * inverse
        coef = wide(inner_s[rows, :] * (1.0 / width), step)
        part_ref[rows, :] = (wide(scale_ref[rows, :], step) * (grad * gain - unit * coef)).astype(part_ref.dtype)
        if gain_grad_ref is not None:
            total = total + jnp.sum((grad * unit).reshape(ROWS // 8, 8, step), axis=0)
    if gain_grad_ref is not None:
        gain_grad_ref[:, cols] = total


def ffn_kernel(
    info_ref, m0, m1, m2, m3, m4, m5, gain_hbm, wg_hbm, wu_hbm, wd_hbm, c0, c1, c2, c3, c4, c5, c6,
    p_across, p_far, p_pair, p_own, gfg_ref, n2_hbm, cotm_hbm, hid_hbm, dgu_hbm,
    gain_ref, wg_ref, wu_ref, wd_ref, cot_s, n2_ref, cotm_ref, hid_ref, dgu_ref,
    gate_s, up_s, gh_s, inner_s, r2_s, in_sems, out_sems,
):
    seq_len, width = n2_ref.shape
    hidden = wg_ref.shape[1]
    length, z = info_ref[0], info_ref[1]
    step = gate_s.shape[1]
    shard = width // 4
    slices = shard_slices(z, shard)
    got_gain, got_wg, got_wu, got_wd = copies(
        (gain_hbm, wg_hbm, wu_hbm, wd_hbm), (gain_ref, wg_ref, wu_ref, wd_ref), in_sems
    )

    def fetch(refs):
        return [
            pltpu.make_async_copy(
                ref.at[pl.ds(0, seq_len), :], cot_s.at[:, pl.ds(k * shard, shard)], in_sems.at[4 + k]
            )
            for k, ref in enumerate(refs)
        ]

    def start_cot(refs):
        for copy in fetch(refs):
            copy.start()

    assemble(z, (c0, c1, c2, c3, c4, c5, c6), start_cot)
    got_gain.wait()

    def normalise(refs):
        def norm(rows):
            ms = [ref[rows, :].astype(f32) for ref in refs]
            r2 = row_scale(sum(m * m for m in ms), width)
            r2_s[rows, :] = jnp.broadcast_to(r2, (ROWS, 128))
            inner_s[rows, :] = jnp.zeros((ROWS, 128), f32)
            for m, cols in zip(ms, slices):
                n2_ref[rows, cols] = (m * r2 * gain_ref[1:2, cols]).astype(bf16)

        row_loop(seq_len, ROWS, norm)

    assemble(z, (m0, m1, m1, m2, m3, m4, m5), normalise)
    for copy in fetch((c0, c1, c2, c3)) + [got_wg, got_wu, got_wd]:
        copy.wait()

    def mask(rows):
        slot = rows.start + lax.broadcasted_iota(jnp.int32, (ROWS, 1), 0)
        for k, cols in enumerate(slices):
            cot = cot_s[rows, k * shard : (k + 1) * shard].astype(f32)
            cotm_ref[rows, cols] = jnp.where(slot < length, cot, 0.0).astype(bf16)

    row_loop(seq_len, ROWS, mask)

    for j in range(0, hidden, step):
        gate_s[...] = dot(n2_ref[...], wg_ref[:, j : j + step])
        up_s[...] = dot(n2_ref[...], wu_ref[:, j : j + step])
        gh_s[...] = dot_t(cotm_ref[...], wd_ref[j : j + step, :])

        def elementwise(rows):
            gate, up, gh = gate_s[rows, :], up_s[rows, :], gh_s[rows, :]
            sig = jax.nn.sigmoid(gate)
            silu = gate * sig
            hid_ref[rows, j : j + step] = (silu * up).astype(bf16)
            dg = (gh * up * (sig * (1.0 + gate * (1.0 - sig)))).astype(bf16)
            du = (gh * silu).astype(bf16)
            dgu_ref[rows, j : j + step] = dg
            dgu_ref[rows, hidden + j : hidden + j + step] = du
            inner = jnp.sum(dg.astype(f32) * gate + du.astype(f32) * up, axis=1, keepdims=True)
            inner_s[rows, :] += jnp.broadcast_to(inner, (ROWS, 128))

        row_loop(seq_len, ROWS, elementwise)

    sent = copies(
        (n2_ref, cotm_ref, hid_ref, dgu_ref), (n2_hbm, cotm_hbm, hid_hbm, dgu_hbm), out_sems
    )
    for part_ref, cols in zip((p_across, p_far, p_pair, p_own), slices):
        gate_s[...] = dot_t(dgu_ref[:, 0:hidden], wg_ref[cols, :]) + dot_t(
            dgu_ref[:, hidden : 2 * hidden], wu_ref[cols, :]
        )
        norm_back(gate_s, n2_ref, r2_s, inner_s, gain_ref[1:2, cols], part_ref, cols, width, gfg_ref)
    for copy in sent:
        copy.wait()


def share(grads_s, core, keep_hbm, give_hbm, sems):
    return copies(
        (grads_s.at[pl.ds(core * 4, 4)], grads_s.at[pl.ds((1 - core) * 4, 4)]), (keep_hbm, give_hbm), sems
    )


def ffn_grad_kernel(
    info_ref, n2_hbm, dgu_hbm, hid_hbm, cotm_hbm, wd_hbm,
    p_across, p_far, p_pair, p_own, keep_hbm, give_hbm,
    n2_ref, dgu_ref, hid_ref, cotm_ref, wd_ref, grads_ref, in_sems, out_sems,
):
    pending = copies(
        (n2_hbm, dgu_hbm, hid_hbm, cotm_hbm, wd_hbm), (n2_ref, dgu_ref, hid_ref, cotm_ref, wd_ref), in_sems
    )
    width, hidden = n2_ref.shape[1], hid_ref.shape[1]
    upper, lower = width // 8, hidden // 8
    rest = upper - lower
    pending[0].wait()
    pending[1].wait()
    for c in range(0, 2 * hidden, 256):
        grad = t_dot(n2_ref[...], dgu_ref[:, c : c + 256])
        for d in range(8):
            grads_ref[d, :, c : c + 256] = grad[d * upper : (d + 1) * upper].astype(bf16)
    for copy in pending[2:]:
        copy.wait()
    for c in range(0, width, 256):
        grad = t_dot(hid_ref[...], cotm_ref[:, c : c + 256])
        for d in range(8):
            block = grad[d * lower : (d + 1) * lower].astype(bf16)
            if c < hidden:
                grads_ref[d, 0:lower, 2 * hidden + c : 2 * hidden + c + 256] = block
            else:
                for k in range(lower // rest):
                    col = 2 * hidden + k * 256
                    grads_ref[d, lower:upper, col : col + 256] = block[k * rest : (k + 1) * rest]
    sent = share(grads_ref, info_ref[3], keep_hbm, give_hbm, out_sems)
    for part_ref, cols in zip((p_across, p_far, p_pair, p_own), shard_slices(info_ref[1], p_own.shape[1])):
        part_ref[...] = dot(hid_ref[...], wd_ref[:, cols]).astype(bf16)
    for copy in sent:
        copy.wait()


def halves_kernel(
    info_ref, keep_hbm, other_hbm, on_x, to_x, on_y, to_y, keep_on_x, keep_x, keep_on_y, keep_y, keep_ref, other_ref, sems
):
    for copy in copies((keep_hbm, other_hbm), (keep_ref, other_ref), sems):
        copy.wait()
    cols = to_x.shape[1]
    for out_ref, first, flip in (
        (on_x, 0, 3), (to_x, 0, 1), (keep_on_x, 0, 2), (keep_x, 0, 0),
        (on_y, cols, 3), (to_y, cols, 2), (keep_on_y, cols, 1), (keep_y, cols, 0),
    ):
        block = jnp.bitwise_xor(info_ref[2], flip)
        out_ref[...] = (
            keep_ref[block, :, first : first + cols].astype(f32) + other_ref[block, :, first : first + cols].astype(f32)
        ).astype(bf16)


def pass_kernel(info_ref, keep_on_x, got_on_x, keep_on_y, got_on_y, to_y, to_x):
    to_y[...] = (keep_on_x[...].astype(f32) + got_on_x[...].astype(f32)).astype(bf16)
    to_x[...] = (keep_on_y[...].astype(f32) + got_on_y[...].astype(f32)).astype(bf16)


def join_kernel(info_ref, keep_x, got_x, from_y, keep_y, got_y, from_x, left_ref, right_ref):
    left_ref[...] = (keep_x[...].astype(f32) + (got_x[...].astype(f32) + from_y[...].astype(f32))).astype(bf16)
    right_ref[...] = (keep_y[...].astype(f32) + (got_y[...].astype(f32) + from_x[...].astype(f32))).astype(bf16)


def unpack_ffn_kernel(info_ref, *refs):
    q, core = info_ref[2], info_ref[3]
    gate_ref, up_ref, down_ref = refs[8:]
    width, hidden = gate_ref.shape
    upper, lower = width // 8, hidden // 8
    rest = upper - lower
    cols = 3 * hidden // 2
    first = 2 * hidden - cols
    for half, (lefts, lefts_x, rights, rights_y) in ((core, refs[0:4]), (1 - core, refs[4:8])):
        for k in range(4):
            block = half * 4 + jnp.bitwise_xor(q, k)
            left, i = (lefts if k in (0, 2) else lefts_x), (0 if k in (0, 1) else 1)
            right, j = (rights if k in (0, 1) else rights_y), (0 if k in (0, 2) else 1)
            rows = pl.ds(pl.multiple_of(block * upper, upper), upper)
            gate_ref[rows, :] = left[i, :, 0:hidden].astype(f32)
            up_ref[rows, 0 : cols - hidden] = left[i, :, hidden:cols].astype(f32)
            up_ref[rows, cols - hidden : hidden] = right[j, :, 0:first].astype(f32)
            rows = pl.ds(pl.multiple_of(block * lower, lower), lower)
            down_ref[rows, 0:hidden] = right[j, 0:lower, first : first + hidden].astype(f32)
            for n in range(lower // rest):
                rows = pl.ds(pl.multiple_of(block * lower + n * rest, rest), rest)
                col = first + n * 256
                down_ref[rows, hidden:width] = right[j, lower:upper, col : col + 256].astype(f32)


def attn_backward_kernel(
    info_ref, g0, g1, g2, g3, g4, g5, qg_ref, kg_ref, wo_hbm, qrot_hbm, krot_hbm, val_hbm, mixed_hbm, lse_hbm,
    cos_hbm, sin_hbm, qpre_hbm, kpre_hbm, n1_hbm, wq_hbm, wk_hbm, wv_hbm, r1_hbm, gain_hbm,
    p_across, p_far, p_pair, p_own, gag_ref, qgg_ref, kgg_ref, keep_hbm, give_hbm,
    wo_ref, qrot_ref, krot_ref, val_ref, mixed_ref, lse_ref, cos_ref, sin_ref, qpre_ref, kpre_ref, n1_ref,
    wq_ref, wk_ref, wv_ref, r1_ref, gain_ref,
    ga_ref, gm_s, dq_s, dk_s, dv_s, dqkv_ref, inner_ref, acc_s, grads_ref, sems, out_sems,
):
    seq_len, width = ga_ref.shape
    hd = qg_ref.shape[1]
    qw, kw = qpre_ref.shape[1], kpre_ref.shape[1]
    heads, kvs = qw // hd, kw // hd
    group = heads // kvs
    length, z = info_ref[0], info_ref[1]
    scale = hd ** (-0.5)
    slices = shard_slices(z, width // 4)
    pending = copies(
        (
            wo_hbm, qrot_hbm, krot_hbm, val_hbm, mixed_hbm, lse_hbm, cos_hbm, sin_hbm, qpre_hbm, kpre_hbm, n1_hbm,
            wq_hbm, wk_hbm, wv_hbm, r1_hbm, gain_hbm,
        ),
        (
            wo_ref, qrot_ref, krot_ref, val_ref, mixed_ref, lse_ref, cos_ref, sin_ref, qpre_ref, kpre_ref, n1_ref,
            wq_ref, wk_ref, wv_ref, r1_ref, gain_ref,
        ),
        sems,
    )

    def collect(refs):
        for ref, cols in zip(refs, slices):
            ga_ref[:, cols] = ref[...]

    assemble(z, (g0, g1, g1, g2, g3, g4, g5), collect)

    pending[0].wait()
    for c in range(0, qw, 256):
        gm_s[:, c : c + 256] = dot_t(ga_ref[...], wo_ref[c : c + 256, :]).astype(bf16)
    dk_s[...] = jnp.zeros_like(dk_s)
    dv_s[...] = jnp.zeros_like(dv_s)
    for copy in pending[1:6]:
        copy.wait()

    for start, rows, keys in query_units(seq_len):
        bias = key_bias(length, keys)
        for g in range(kvs):
            first = g * group
            cols = slice(g * hd, (g + 1) * hd)
            key, val = krot_ref[0:keys, cols], val_ref[0:keys, cols]

            def stacked(ref):
                return jnp.concatenate(
                    [ref[start : start + rows, h * hd : (h + 1) * hd] for h in range(first, first + group)], axis=0
                )

            q, gm, mixed = stacked(qrot_ref), stacked(gm_s), stacked(mixed_ref)
            lse = jnp.concatenate(
                [lse_ref[start : start + rows, h : h + 1] for h in range(first, first + group)], axis=0
            )
            p = jnp.exp2(dot_t(q, key) * (scale * LOG2E) + bias - lse)
            delta = jnp.sum(gm.astype(f32) * mixed.astype(f32), axis=1, keepdims=True)
            ds = (p * (dot_t(gm, val) - delta)).astype(bf16)
            dv_s[0:keys, cols] += t_dot(p.astype(bf16), gm)
            dk_s[0:keys, cols] += t_dot(ds, q)
            dq = dot(ds, key)
            for r in range(group):
                h = first + r
                dq_s[start : start + rows, h * hd : (h + 1) * hd] = dq[r * rows : (r + 1) * rows]

    for copy in pending[6:]:
        copy.wait()
    ones = jnp.full((hd, hd), 1.0 / hd, bf16)

    def unrotate(rows, rot_s, pre_ref, g_ref, count, base, gain_sum):
        cos, sin = cos_ref[rows, :], sin_ref[rows, :]
        inner = jnp.zeros((ROWS, hd), f32)
        for c in range(0, count, hd):
            g = rot_s[rows, c : c + hd] * scale
            u = g * cos + pltpu.roll(g * sin, hd // 2, 1)
            v = pre_ref[rows, c : c + hd]
            r = lax.rsqrt(dot((v * v).astype(bf16), ones) + NORM_EPSILON)
            unit = v * r
            t = u * unit
            gain_sum = gain_sum + jnp.sum(t.reshape(ROWS // 8, 8, hd), axis=0)
            mean = dot((t * g_ref[...]).astype(bf16), ones)
            dqkv_ref[rows, base + c : base + c + hd] = (r * (u * g_ref[...] - unit * mean)).astype(bf16)
            inner = inner + (hd * NORM_EPSILON) * (r * r * mean)
        return inner, gain_sum

    qgs = kgs = jnp.zeros((8, hd), f32)
    for start in range(0, seq_len, ROWS):
        rows = pl.ds(start, ROWS)
        qi, qgs = unrotate(rows, dq_s, qpre_ref, qg_ref, qw, 0, qgs)
        ki, kgs = unrotate(rows, dk_s, kpre_ref, kg_ref, kw, qw, kgs)
        dv = dv_s[rows, :].astype(bf16)
        dqkv_ref[rows, qw + kw : qw + 2 * kw] = dv
        vi = jnp.sum(dv.astype(f32) * val_ref[rows, :].astype(f32), axis=1, keepdims=True)
        inner_ref[rows, :] = qi + ki + vi
    qgg_ref[...] = qgs
    kgg_ref[...] = kgs

    upper, lower = width // 8, qw // 8
    for c in range(0, width, 256):
        grad = t_dot(n1_ref[...], dqkv_ref[:, c : c + 256])
        out = t_dot(mixed_ref[...], ga_ref[:, c : c + 256])
        for d in range(8):
            grads_ref[d, 0:upper, c : c + 256] = grad[d * upper : (d + 1) * upper].astype(bf16)
            grads_ref[d, upper : upper + lower, c : c + 256] = out[d * lower : (d + 1) * lower].astype(bf16)
    sent = share(grads_ref, info_ref[3], keep_hbm, give_hbm, out_sems)
    for part_ref, cols in zip((p_across, p_far, p_pair, p_own), slices):
        acc_s[...] = (
            dot_t(dqkv_ref[:, 0:qw], wq_ref[cols, :])
            + dot_t(dqkv_ref[:, qw : qw + kw], wk_ref[cols, :])
            + dot_t(dqkv_ref[:, qw + kw : qw + 2 * kw], wv_ref[cols, :])
        )
        norm_back(acc_s, n1_ref, r1_ref, inner_ref, gain_ref[0:1, cols], part_ref, cols, width, gag_ref)
    for copy in sent:
        copy.wait()


def output_kernel(info_ref, middle_ref, attn_ref, own_ref, pair_ref, across_ref, out_ref, sums_ref):
    seq_len, shard = middle_ref.shape
    length = info_ref[0]
    sums = [jnp.zeros((8, shard), f32)] * 3
    for start in range(0, seq_len, ROWS):
        rows = pl.ds(start, ROWS)
        ffn = own_ref[rows, :].astype(f32) + (pair_ref[rows, :].astype(f32) + across_ref[rows, :].astype(f32))
        out = middle_ref[rows, :] + ffn
        out_ref[rows, :] = out.astype(bf16)
        slot = start + lax.broadcasted_iota(jnp.int32, (ROWS, 1), 0)
        for i, v in enumerate((out, attn_ref[rows, :], ffn)):
            v = jnp.where(slot < length, v, 0.0)
            sums[i] = sums[i] + jnp.sum((v * v).reshape(ROWS // 8, 8, shard), axis=0)
    for i in range(3):
        sums_ref[i : i + 1, :] = jnp.sum(sums[i], axis=0, keepdims=True)


def small_kernel(info_ref, gag_ref, gfg_ref, qgg_ref, kgg_ref, sums_ref, small_ref):
    hd, shard = qgg_ref.shape[1], sums_ref.shape[1]
    small_ref[...] = jnp.zeros(small_ref.shape, f32)
    small_ref[0:1, :] = jnp.sum(gag_ref[...], axis=0, keepdims=True)
    small_ref[1:2, :] = jnp.sum(gfg_ref[...], axis=0, keepdims=True)
    small_ref[2:3, 0:hd] = jnp.sum(qgg_ref[...], axis=0, keepdims=True)
    small_ref[2:3, hd : 2 * hd] = jnp.sum(kgg_ref[...], axis=0, keepdims=True)
    lane = lax.broadcasted_iota(jnp.int32, (1, 128), 1)
    totals = (info_ref[0] * shard).astype(f32) * (lane == 3).astype(f32)
    for i in range(3):
        totals = totals + jnp.sum(sums_ref[i : i + 1, :], axis=1, keepdims=True) * (lane == i).astype(f32)
    small_ref[2:3, 2 * hd : 2 * hd + 128] = totals


def block_kernel(info_ref, keep_x, got_x, from_y, keep_y, got_y, from_x, small_ref, left_ref, right_ref):
    rows, cols = keep_x.shape
    small = small_ref[...]
    high = small.astype(bf16)
    tail = jnp.concatenate([high, (small - high.astype(f32)).astype(bf16)], axis=0)
    for a, b, c, out_ref, first in ((keep_x, got_x, from_y, left_ref, 0), (keep_y, got_y, from_x, right_ref, cols)):
        out_ref[0:rows, :] = (a[...].astype(f32) + (b[...].astype(f32) + c[...].astype(f32))).astype(bf16)
        out_ref[rows : rows + TAIL, :] = tail[:, first : first + cols]


def unpack_kernel(info_ref, *refs):
    q, core = info_ref[2], info_ref[3]
    gq_ref, gk_ref, gv_ref, go_ref, ag_ref, fg_ref, qg_ref, kg_ref, rms_ref, small_ref = refs[8:]
    cols, kw = gq_ref.shape[1], gk_ref.shape[1]
    upper, lower = gq_ref.shape[0] // 8, go_ref.shape[0] // 8
    for half, (lefts, lefts_x, rights, rights_y) in ((core, refs[0:4]), (1 - core, refs[4:8])):
        for k in range(4):
            block = half * 4 + jnp.bitwise_xor(q, k)
            left, i = (lefts if k in (0, 2) else lefts_x), (0 if k in (0, 1) else 1)
            right, j = (rights if k in (0, 1) else rights_y), (0 if k in (0, 2) else 1)
            rows = pl.ds(pl.multiple_of(block * upper, upper), upper)
            gq_ref[rows, :] = left[i, 0:upper, :].astype(f32)
            gk_ref[rows, :] = right[j, 0:upper, 0:kw].astype(f32)
            gv_ref[rows, :] = right[j, 0:upper, kw : 2 * kw].astype(f32)
            rows = pl.ds(pl.multiple_of(block * lower, lower), lower)
            go_ref[rows, 0:cols] = left[i, upper : upper + lower, :].astype(f32)
            go_ref[rows, cols : 2 * cols] = right[j, upper : upper + lower, :].astype(f32)
    for first, group in ((0, (0, 1, 4, 5)), (cols, (2, 3, 6, 7))):
        total = jnp.zeros((8, cols), f32)
        for n in group:
            for i in range(2):
                tail = refs[n][i, upper + lower : upper + lower + TAIL, :].astype(f32)
                total = total + (tail[0:8] + tail[8:16])
        small_ref[:, first : first + cols] = total
    shard, hd = ag_ref.shape[1], qg_ref.shape[1]
    mine = pl.ds(pl.multiple_of(info_ref[1] * shard, shard), shard)
    ag_ref[...] = small_ref[0:1, mine]
    fg_ref[...] = small_ref[1:2, mine]
    qg_ref[...] = small_ref[2:3, 0:hd]
    kg_ref[...] = small_ref[2:3, hd : 2 * hd]
    totals = small_ref[2:3, 2 * hd : 2 * hd + 128]
    lane = lax.broadcasted_iota(jnp.int32, (1, 128), 1)
    count = jnp.sum(jnp.where(lane == 3, totals, 0.0), axis=1, keepdims=True)
    rms_ref[...] = jnp.sqrt(totals / count)


SPECS = {
    "s": pl.BlockSpec(memory_space=pltpu.SMEM),
    "v": pl.BlockSpec(memory_space=pltpu.VMEM),
    "a": pl.BlockSpec(memory_space=pl.ANY),
}


def call(body, outs, args, scratch=(), sems=(), flops=0, bytes_accessed=0, limit=SMALL_BYTES):
    places, arrays = [], []
    for place, *group in args:
        places += [place] * len(group)
        arrays += group
    return pl.pallas_call(
        body,
        out_shape=[jax.ShapeDtypeStruct(s, d) for s, d, _ in outs],
        in_specs=[SPECS[p] for p in places],
        out_specs=[SPECS[p] for _, _, p in outs],
        scratch_shapes=[pltpu.VMEM(s, d) for s, d in scratch] + [pltpu.SemaphoreType.DMA((n,)) for n in sems],
        compiler_params=pltpu.CompilerParams(vmem_limit_bytes=limit),
        cost_estimate=pl.CostEstimate(flops=flops, bytes_accessed=bytes_accessed, transcendentals=0),
    )(*arrays)


PAIRS = ((0, 1), (1, 0), (2, 3), (3, 2))
MIDDLE = ((1, 2), (2, 1))
OUTWARD = ((1, 0), (2, 3))
INWARD = ((0, 1), (3, 2))
OUTWARD_TWO = ((2, 0), (1, 3))
INWARD_TWO = ((0, 2), (3, 1))


def send(rows, pairs):
    return lax.ppermute(rows, "tensor", pairs)


def hold(*values):
    return lax.optimization_barrier(values)


def gather_line(own):
    pair = send(own, PAIRS)
    across_mid = send(own, MIDDLE)
    far_end = send(pair, OUTWARD_TWO)
    far_mid = send(pair, MIDDLE)
    across_end = send(across_mid, OUTWARD)
    return own, pair, across_mid, across_end, far_mid, far_end


def pick(end, from_end, from_middle):
    return jnp.where(end, from_end, from_middle)


def scatter_first(parts):
    across, far, _, _ = parts
    return send(far, INWARD_TWO), send(far, MIDDLE), send(across, INWARD)


def scatter_last(parts, first):
    across, _, pair, own = parts
    two, three, one = first
    to_pair = (pair.astype(f32) + (two.astype(f32) + three.astype(f32))).astype(bf16)
    to_across = (across.astype(f32) + one.astype(f32)).astype(bf16)
    return own, send(to_pair, PAIRS), send(to_across, MIDDLE)


def add(a, b):
    return (a.astype(f32) + b.astype(f32)).astype(bf16)


def total(terms):
    own, pair, across = terms
    return own.astype(f32) + (pair.astype(f32) + across.astype(f32))


def swap(values, bit):
    return lax.ppermute(values, "dp", [(i, i ^ bit) for i in range(8)])


def halve(keep, other, info):
    _, rows, width = keep.shape
    return call(
        halves_kernel,
        [((rows, width // 2), bf16, "v")] * 8,
        (("s", info), ("a", keep, other)),
        scratch=[((4, rows, width), bf16)] * 2,
        sems=(2,),
    )


def pass_on(keep_on_x, got_on_x, keep_on_y, got_on_y, info):
    return call(
        pass_kernel, [(keep_on_x.shape, bf16, "v")] * 2, (("s", info), ("v", keep_on_x, got_on_x, keep_on_y, got_on_y))
    )


def per_device(
    hidden_in, lengths, w_query, w_key, w_value, w_out, attn_gain, ffn_gain,
    query_gain, key_gain, w_gate, w_up, w_down, cotangent,
):
    seq_len, shard = hidden_in.shape
    width = w_query.shape[0]
    hd = query_gain.shape[0]
    qw, kw = w_query.shape[1], w_key.shape[1]
    hidden = w_gate.shape[1]
    padded = -(-seq_len // BLOCK) * BLOCK
    z = lax.axis_index("tensor").astype(jnp.int32)
    dp = lax.axis_index("dp").astype(jnp.int32)
    chips = lax.axis_size("dp") == 8
    q, core = (dp // 2, dp % 2) if chips else (0 * dp, 0 * dp)
    info = jnp.stack([lengths[0], z, q, core])
    parts = [((seq_len, shard), bf16, "v")] * 4

    end = (z == 0) | (z == 3)
    x = call(
        pack_kernel,
        [((seq_len + TAIL, shard), bf16, "v")],
        (("s", lengths), ("v", hidden_in, attn_gain[None], ffn_gain[None])),
    )[0]
    cot = jnp.concatenate([cotangent, jnp.zeros((TAIL, shard), bf16)], axis=0)
    x_pair, x_mid = send(x, PAIRS), send(x, MIDDLE)
    x_pair, x_mid, cot = hold(x_pair, x_mid, cot)
    x_end, x_far = send(pick(end, cot, x_mid), PAIRS), send(x_pair, MIDDLE)
    x_end, x_far, cot = hold(x_end, x_far, cot)
    x_last, cot_far = send(x_far, OUTWARD), send(x_end, MIDDLE)
    x_last, cot_far, x_end, cot = hold(x_last, cot_far, x_end, cot)
    cot_mid, cot_pair, cot_last = send(cot, MIDDLE), send(cot, OUTWARD), send(cot_far, OUTWARD)
    cos, sin = rope_tables(seq_len, hd)
    qg, kg = query_gain[None], key_gain[None]
    resid = hidden_in.astype(f32)
    valid = (jnp.arange(seq_len, dtype=jnp.int32) < lengths[0]).astype(f32)[:, None]

    saved = [
        ((seq_len, width), bf16), ((seq_len, qw), f32), ((seq_len, kw), f32), ((seq_len, qw), bf16),
        ((padded, kw), bf16), ((padded, kw), bf16), ((seq_len, qw), bf16), ((seq_len, 128), f32),
        ((seq_len, 128), f32), ((8, width), f32),
    ]
    weights = [((width, kw), bf16), ((width, kw), bf16), ((width, qw), bf16), ((qw, width), bf16)]
    tables = [((seq_len, hd), f32)] * 2
    *attn_parts, n1, qpre, kpre, qrot, krot, val, mixed, lse, r1, gain = call(
        attn_forward_kernel,
        parts + [(s, d, "a") for s, d in saved],
        (
            ("s", info), ("v", x, x_pair, x_mid, x_end, x_far, x_last, qg, kg),
            ("a", w_key, cos, sin, w_value, w_query, w_out),
        ),
        scratch=weights[:1] + tables + weights[1:] + saved,
        sems=(6, 10),
        limit=FULL_BYTES,
        flops=2 * seq_len * width * (2 * qw + 2 * kw) + 4 * seq_len * seq_len * qw,
        bytes_accessed=14_000_000,
    )
    attn_parts, cot_mid, cot_pair, cot_last = hold(attn_parts, cot_mid, cot_pair, cot_last)
    across, far, pair, own = attn_parts
    two = send(far, INWARD_TWO)
    one, three = hold(pick(end, across, cot_mid[:seq_len]), far)
    three, one = send(three, MIDDLE), send(one, PAIRS)
    zero_end = pick(end, jnp.zeros_like(one), one)
    pair = lax.optimization_barrier(pair.astype(f32) + two.astype(f32))
    attn_local = total(scatter_last((across, far, pair, own), (jnp.zeros_like(two), three, zero_end)))
    middle = resid + attn_local
    shard_two, one = hold(middle.astype(bf16), one)
    m_parts = gather_line(shard_two)

    kept = [((seq_len, width), bf16), ((seq_len, width), bf16), ((seq_len, hidden), bf16), ((seq_len, 2 * hidden), bf16)]
    *ffn_parts, gfg, n2, cotm, hid, dgu = call(
        ffn_kernel,
        parts + [((8, width), f32, "v")] + [(s, d, "a") for s, d in kept],
        (
            ("s", info), ("v", *m_parts), ("a", gain, w_gate, w_up, w_down),
            ("a", cot, x_end, cot_pair, cot_mid, one, cot_far, cot_last),
        ),
        scratch=[((8, width), f32)] + [((width, hidden), bf16)] * 2 + [((hidden, width), bf16), ((seq_len, width), bf16)]
        + kept + [((seq_len, 256), f32)] * 3 + [((seq_len, 128), f32)] * 2,
        sems=(8, 4),
        limit=VMEM_BYTES,
        flops=2 * seq_len * width * hidden * 5,
        bytes_accessed=16_000_000,
    )
    grad_top = cotangent.astype(f32) * valid
    first = scatter_first(ffn_parts)
    blocks = ((4, width // 8, 3 * hidden), bf16, "a")
    *down_parts, ffn_keep, ffn_give = call(
        ffn_grad_kernel,
        parts + [blocks] * 2,
        (("s", info), ("a", n2, dgu, hid, cotm, w_down)),
        scratch=[kept[0], kept[3], kept[2], kept[1], ((hidden, width), bf16), ((8, width // 8, 3 * hidden), bf16)],
        sems=(5, 2),
        limit=VMEM_BYTES,
        flops=2 * seq_len * width * hidden * 4,
        bytes_accessed=14_000_000,
    )
    first, ffn_keep, ffn_give = hold(first, ffn_keep, ffn_give)
    back = scatter_last(ffn_parts, first)
    if chips:
        ffn_other = swap(ffn_give, 1)
        halves = halve(ffn_keep, ffn_other, info)
        back, halves = hold(back, halves)
        on_x, to_x, on_y, to_y, keep_on_x, keep_x, keep_on_y, keep_y = halves
    grad_middle = grad_top + total(back)
    ga = grad_middle.astype(bf16)
    across, far, pair, own = down_parts
    ga_pair, ga_mid = send(ga, PAIRS), send(ga, MIDDLE)
    if chips:
        got_on_x, got_on_y = swap(on_x, 2), swap(on_y, 4)
        got_x, got_y = swap(to_x, 2), swap(to_y, 4)
        to_y, to_x = pass_on(keep_on_x, got_on_x, keep_on_y, got_on_y, info)
        ga_pair, ga_mid, far, to_y, to_x = hold(ga_pair, ga_mid, far, to_y, to_x)
        from_y, from_x = swap(to_y, 4), swap(to_x, 2)
    ga_end, ga_far = send(pick(end, far, ga_mid), PAIRS), send(ga_pair, MIDDLE)
    if chips:
        left, right = call(
            join_kernel,
            [((width // 8, 3 * hidden // 2), bf16, "v")] * 2,
            (("s", info), ("v", keep_x, got_x, from_y, keep_y, got_y, from_x)),
        )
        ga_end, ga_far, across, left, right = hold(ga_end, ga_far, across, left, right)
        left_y, right_x = swap(left, 4), swap(right, 2)
    ga_last = send(pick(end, across, ga_far), PAIRS)
    got_far = send(add(far, ga_end), MIDDLE)
    if chips:
        ga_last, got_far, left_y, right_x = hold(ga_last, got_far, left_y, right_x)
        lefts, rights = jnp.stack([left, left_y]), jnp.stack([right, right_x])
        lefts_x, rights_y = swap(lefts, 2), swap(rights, 4)
    ga_parts = (ga, ga_pair, ga_mid, ga_end, ga_far, ga_last)
    ffn_terms = (own, send(add(pair, got_far), PAIRS), send(add(across, ga_last), MIDDLE))

    blocks = (4, (width + qw) // 8, width)
    *back_parts, gag, qgg, kgg, keep, give = call(
        attn_backward_kernel,
        parts + [((8, width), f32, "v"), ((8, hd), f32, "v"), ((8, hd), f32, "v"), (blocks, bf16, "a"), (blocks, bf16, "a")],
        (
            ("s", info), ("v", *ga_parts, qg, kg),
            ("a", w_out, qrot, krot, val, mixed, lse, cos, sin, qpre, kpre, n1, w_query, w_key, w_value, r1, gain),
        ),
        scratch=[weights[3], saved[3], saved[4], saved[5], saved[6], saved[7], *tables, saved[1], saved[2], saved[0]]
        + [weights[2], weights[0], weights[1], saved[8], saved[9]]
        + [((seq_len, width), bf16), ((seq_len, qw), bf16), ((seq_len, qw), f32), ((padded, kw), f32), ((padded, kw), f32)]
        + [((seq_len, qw + 2 * kw), bf16), ((seq_len, 128), f32), ((seq_len, shard), f32), ((8, *blocks[1:]), bf16)],
        sems=(16, 2),
        limit=VMEM_BYTES,
        flops=2 * seq_len * width * (4 * qw + 4 * kw) + 10 * seq_len * seq_len * qw,
        bytes_accessed=20_000_000,
    )
    across, far, pair, own = back_parts
    if chips:
        far, ffn_terms, keep, give, lefts_x, rights_y = hold(far, ffn_terms, keep, give, lefts_x, rights_y)
        other = swap(give, 1)
    out_rows, sums = call(
        output_kernel,
        [((seq_len, shard), bf16, "v"), ((8, shard), f32, "v")],
        (("s", info), ("v", middle, attn_local, *ffn_terms)),
        bytes_accessed=2_000_000,
    )
    small = call(small_kernel, [((8, width), f32, "v")], (("s", info), ("v", gag, gfg, qgg, kgg, sums)))[0]
    shapes = [(width, qw), (width, kw), (width, kw), (qw, width)]
    if chips:
        other, small = hold(other, small)
        on_x, to_x, on_y, to_y, keep_on_x, keep_x, keep_on_y, keep_y = halve(keep, other, info)
        got_on_x, got_on_y = swap(on_x, 2), swap(on_y, 4)
        got_x, got_y = swap(to_x, 2), swap(to_y, 4)
        small = small + send(small, PAIRS)
        small = small + send(small, ((0, 2), (2, 0), (1, 3), (3, 1)))
        to_y, to_x = pass_on(keep_on_x, got_on_x, keep_on_y, got_on_y, info)
        to_y, to_x, small, far, across = hold(to_y, to_x, small, far, across)
        from_y, from_x, two = swap(to_y, 4), swap(to_x, 2), send(far, INWARD_TWO)
        late_left, late_right = call(
            block_kernel,
            [((keep_x.shape[0] + TAIL, keep_x.shape[1]), bf16, "v")] * 2,
            (("s", info), ("v", keep_x, got_x, from_y, keep_y, got_y, from_x, small)),
        )
        late_left, late_right, far, across = hold(late_left, late_right, far, across)
        three, one = send(far, MIDDLE), send(across, INWARD)
        left_y, right_x, two, three, one = hold(swap(late_left, 4), swap(late_right, 2), two, three, one)
        late_lefts, late_rights = jnp.stack([late_left, left_y]), jnp.stack([late_right, right_x])
        back_terms = scatter_last((across, far, pair, own), (two, three, one))
        ffn_halves = (lefts, lefts_x, rights, rights_y)
        g_gate, g_up, g_down = call(
            unpack_ffn_kernel,
            [(s, f32, "v") for s in ((width, hidden), (width, hidden), (hidden, width))],
            (("s", info), ("v", *ffn_halves, *[swap(b, 1) for b in ffn_halves])),
            bytes_accessed=14_000_000,
        )
        late = (late_lefts, swap(late_lefts, 2), late_rights, swap(late_rights, 4))
        late, back_terms, g_gate, g_up, g_down = hold(late, back_terms, g_gate, g_up, g_down)
        everyone = [*late, *[swap(b, 1) for b in late]]
        gq, gk, gv, go, ag, fg, qgg, kgg, rms = call(
            unpack_kernel,
            [(s, f32, "v") for s in shapes + [(1, shard), (1, shard), (1, hd), (1, hd), (1, 128)]],
            (("s", info), ("v", *everyone)),
            scratch=[((8, width), f32)],
            bytes_accessed=9_000_000,
        )
    else:
        back_terms = scatter_last(back_parts, scatter_first(back_parts))
        grads, ffn_grads = lax.psum((jnp.concatenate([keep, give]), jnp.concatenate([ffn_keep, ffn_give])), "dp")
        small = lax.psum(small, ("dp", "tensor"))
        ag, fg = [lax.dynamic_slice(small, (i, z * shard), (1, shard)) for i in (0, 1)]
        qgg, kgg = small[2:3, :hd], small[2:3, hd : 2 * hd]
        totals = small[2:3, 2 * hd : 2 * hd + 4]
        rms = jnp.sqrt(totals / totals[:, 3:])
        g_qkv = grads[:, : width // 8].reshape(width, width).astype(f32)
        gq, gk, gv = g_qkv[:, :qw], g_qkv[:, qw : qw + kw], g_qkv[:, qw + kw :]
        go = grads[:, width // 8 :].reshape(qw, width).astype(f32)
        g_gate = ffn_grads[:, :, :hidden].reshape(width, hidden).astype(f32)
        g_up = ffn_grads[:, :, hidden : 2 * hidden].reshape(width, hidden).astype(f32)
        folded = ffn_grads[:, :, 2 * hidden :]
        lower = hidden // 8
        tail = folded[:, lower:].reshape(8, width // 8 - lower, -1, 256).transpose(0, 2, 1, 3).reshape(8, lower, 256)
        g_down = jnp.concatenate([folded[:, :lower], tail], axis=2).reshape(hidden, width).astype(f32)
    input_grad = (grad_middle + total(back_terms)).astype(bf16)
    return (
        out_rows,
        input_grad,
        gq,
        gk,
        gv,
        go,
        ag[0],
        fg[0],
        qgg[0],
        kgg[0],
        g_gate,
        g_up,
        g_down,
        rms[0, :3],
    )


def solution(mesh):
    rows, cols, first = P("dp", "tensor"), P(None, "tensor"), P("tensor", None)
    gain = P("tensor")
    return jax.shard_map(
        per_device,
        mesh=mesh,
        in_specs=(rows, P("dp"), cols, cols, cols, first, gain, gain, P(), P(), cols, cols, first, rows),
        out_specs=(rows, rows, cols, cols, cols, first, gain, gain, P(), P(), cols, cols, first, P()),
        check_vma=False,
    )
```
